128 devices in a mesh: var: 4 (over z), patch: 32 (over x, y, core).
Axes of the slice: x: 4, y: 4, z: 4, core: 2. Of those that a mesh axis runs over, the one named last changes fastest.
Arguments:
- tokens: bfloat16 [48, 16384, 1024], P('var', 'patch'), may hold values from -8.25 to 8.25
- key_query: bfloat16 [1024, 16], replicated, may hold values from -0.2 to 0.2
- value_weight: bfloat16 [1024, 1024], replicated, may hold values from -0.1875 to 0.1875
- proj_weight: bfloat16 [1024, 2048], replicated, may hold values from -0.1875 to 0.1875
- norm_gain: float32 [2048], replicated, may hold values from 0.1 to 1.9
- qkv_weight: bfloat16 [2048, 3, 16, 128], P(None, None, 'var'), may hold values from -0.3 to 0.3
- out_weight: bfloat16 [16, 128, 2048], P('var'), may hold values from -0.125 to 0.125
Outputs:
- block_out: bfloat16 [16384, 2048], P('patch', 'var')
The draws below stay inside these ranges and needn't reach their ends.
All inputs are finite; a program needn't handle non-finite values.
Results may differ from the reference program's by a relative error of at most 0.006.
Values may be sent and summed in bfloat16 or wider, within the bound.
A program may use at most 192 MiB of HBM per device.

```python
import math
import jax
import jax.numpy as jnp
from jax import lax

D = 1024
HEADS = 16
WIDTH = 2048
AGG_HEAD = 64
VIT_HEAD = 128
VARS = 48
NP = 16384
N_VAR = 4


def draw_key_query(key, part):
    key = jax.random.fold_in(key, 11)
    table = jnp.clip(jax.random.normal(key, (D, HEADS), jnp.float32), -4.0, 4.0) * (1.5 / 32.0)
    return table.astype(jnp.bfloat16)


def draw_tokens(key, part):
    key = jax.random.fold_in(key, 12)
    tokens = jnp.clip(jax.random.normal(key, (VARS, NP, D), jnp.float32), -6.0, 6.0)
    return tokens.astype(jnp.bfloat16)


def draw_qkv_weight(key, part):
    key = jax.random.fold_in(key, 13)
    key_base = jax.random.fold_in(key, 0)
    norm_scale = WIDTH ** (-0.5)
    base = jnp.clip(jax.random.normal(key_base, (WIDTH, 3, HEADS, VIT_HEAD), jnp.float32), -4.0, 4.0) * norm_scale
    table = base
    table = jnp.clip(table, -0.296875, 0.296875)
    return table.astype(jnp.bfloat16)


def block_levels(own_key, dims, cuts, smallest, largest):
    def one(position, shards_of):
        draws = jax.random.uniform(jax.random.fold_in(jax.random.fold_in(own_key, 6), position), (shards_of,), jnp.float32, smallest / len(cuts), largest / len(cuts))
        return jnp.repeat(jnp.exp(draws), dims[position] // shards_of).reshape((-1,) + (1,) * (len(dims) - position - 1))

    factor_of = one(*cuts[0])
    for cut in cuts[1:]:
        factor_of = factor_of * one(*cut)
    return factor_of


def bell_draw(key, extent, width, reach, shards=(), held_as=jnp.bfloat16):
    array = jax.random.normal(key, extent, jnp.float32) * width
    if len(shards) > 0:
        array = block_levels(key, extent, shards, -0.22, 0.18) * array
    return jnp.clip(array, min=-reach, max=reach).astype(held_as)


def setup_inputs(seed: int = 0) -> dict:
    key_list = jax.random.split(jax.random.key(seed), 8)
    return {
        "tokens": draw_tokens(jax.random.fold_in(key_list[7], 71), 0),
        "key_query": draw_key_query(jax.random.fold_in(key_list[7], 71), 0),
        "value_weight": bell_draw(key_list[2], (D, D), D ** -0.5, 0.1875),
        "proj_weight": bell_draw(key_list[3], (D, WIDTH), D ** -0.5, 0.1875),
        "norm_gain": jnp.clip(1.0 + 0.18 * jax.random.normal(key_list[4], (WIDTH,), jnp.float32), 0.1, 1.9),
        "qkv_weight": draw_qkv_weight(jax.random.fold_in(key_list[7], 71), 0),
        "out_weight": bell_draw(key_list[6], (HEADS, VIT_HEAD, WIDTH), WIDTH ** -0.5, 0.125, ((0, 4),)),
    }


def pool_block(tokens, key_query, value_weight, start, width_block):
    tok_block = lax.dynamic_slice_in_dim(tokens, start, width_block, 1)
    group_count = N_VAR
    per_group = VARS // N_VAR
    scores = jnp.einsum('vpd,dh->vph', tok_block.astype(jnp.float32), key_query.astype(jnp.float32))
    grouped = scores.reshape(group_count, per_group, width_block, HEADS)
    peak = lax.optimization_barrier(jnp.max(grouped, axis=1))
    weights = jnp.exp(grouped - peak[:, None])
    totals = lax.optimization_barrier(jnp.sum(weights, axis=1))
    rounded = weights.astype(jnp.bfloat16)
    tok_grouped = tok_block.reshape(group_count, per_group, width_block, D)
    mixture = jnp.einsum('gvph,gvpd->gphd', rounded.astype(jnp.float32), tok_grouped.astype(jnp.float32)).astype(jnp.bfloat16)
    heads_weight = value_weight.reshape(D, HEADS, AGG_HEAD).astype(jnp.float32)
    partial_sums = jnp.einsum('gphd,dhj->gphj', mixture.astype(jnp.float32), heads_weight)
    top_all = lax.optimization_barrier(jnp.max(peak, axis=0))
    factor = jnp.exp(peak - top_all[None])
    numer = lax.optimization_barrier(jnp.sum(factor[..., None] * partial_sums, axis=0))
    denom = lax.optimization_barrier(jnp.sum(factor * totals, axis=0))
    return (numer / denom[..., None]).reshape(width_block, D).astype(jnp.bfloat16)

def reference(tokens, key_query, value_weight, proj_weight, norm_gain, qkv_weight, out_weight):
    block_rows = math.gcd(NP, 512)
    starts = jnp.arange(NP // block_rows, dtype=jnp.int32) * block_rows
    pooled = lax.map(lambda start: pool_block(tokens, key_query, value_weight, start, block_rows), starts).reshape(NP, D)
    embedded = jnp.dot(pooled, proj_weight, preferred_element_type=jnp.float32)
    center = embedded - lax.optimization_barrier(jnp.mean(embedded, axis=1, keepdims=True))
    variance = lax.optimization_barrier(jnp.mean(center * center, axis=1, keepdims=True))
    normed = (center / jnp.sqrt(variance + 1e-05) * norm_gain).astype(jnp.bfloat16)
    projected = jnp.dot(normed, qkv_weight.reshape(WIDTH, 3 * HEADS * VIT_HEAD), preferred_element_type=jnp.float32)
    projected = projected.reshape(NP, 3, HEADS, VIT_HEAD)
    queries = (projected[:, 0] * VIT_HEAD ** (-0.5)).astype(jnp.bfloat16)
    keys = projected[:, 1].astype(jnp.bfloat16)
    values = projected[:, 2].astype(jnp.bfloat16)

    def attend(start):
        query_block = lax.dynamic_slice_in_dim(queries, start, block_rows, 0)
        logits = jnp.einsum('qhd,khd->hqk', query_block.astype(jnp.float32), keys.astype(jnp.float32))
        rowmax = lax.optimization_barrier(jnp.max(logits, axis=2, keepdims=True))
        expw = jnp.exp(logits - rowmax)
        denom = lax.optimization_barrier(jnp.sum(expw, axis=2))
        summed = jnp.einsum('hqk,khd->hqd', expw.astype(jnp.bfloat16).astype(jnp.float32), values.astype(jnp.float32))
        result = summed / denom[..., None]
        return jnp.transpose(result, (1, 0, 2)).reshape(block_rows, WIDTH).astype(jnp.bfloat16)
    attended = lax.map(attend, starts).reshape(NP, WIDTH)
    branch = jnp.dot(attended, out_weight.reshape(WIDTH, WIDTH), preferred_element_type=jnp.float32)
    return (embedded + branch).astype(jnp.bfloat16)
```

```python
import functools

import jax
import jax.numpy as jnp
from jax import lax
from jax.experimental import pallas as pl
from jax.experimental.pallas import tpu as pltpu
from jax.sharding import PartitionSpec as P

MESH = pl.DeviceIdType.MESH
NT = (((1,), (1,)), ((), ()))
BF = jnp.bfloat16
F32 = jnp.float32

ROWS, NV, CH = 512, 12, 128
Q_SCALE = 128 ** (-0.5) * 1.4426950408889634


def order(e):
    if isinstance(e, int):
        return (0, 1, 3, 2)[e]
    return e + lax.div(e, 2) * (5 - 2 * e)


def dot(a, b):
    return jnp.dot(a, b, preferred_element_type=F32)


def kernel(
    tok_hbm, kq_ref, vw_hbm, proj_hbm, gain_ref, w2_hbm, ow_hbm,
    out_ref,
    tok, kqp, expand, vw, proj, wstage, wf, wq,
    wn, part_send, part_recv, stat_send, stat_recv, pooled,
    emb, normed, q4, kv4, q_buf, kv, s0, s1, acc, mref,
    ow, stage, att,
    sem_tok, sem_w, sem_w2, sem_ow_own,
    ps_send, ps_recv, st_send, st_recv, pool_send, pool_recv,
    q_send, q_recv, kvx_send, own_send, fwd_send, kv_recv,
    ow_send, ow_recv, ax_send, ax_recv, az_send, az_recv,
):
    z = lax.axis_index("var")
    place = lax.axis_index("patch")
    x = lax.div(place, 8)
    y = lax.rem(lax.div(place, 2), 4)
    c = lax.rem(place, 2)

    def at(dx=0, dy=0, dz=0, dc=0):
        px = lax.rem(x + dx, 4)
        py = lax.rem(y + dy, 4)
        pc = lax.rem(c + dc, 2)
        return (lax.rem(z + dz, 4), (px * 4 + py) * 2 + pc)

    def remote(src, dst, send, recv, device):
        return pltpu.make_async_remote_copy(
            src_ref=src, dst_ref=dst, send_sem=send, recv_sem=recv,
            device_id=device, device_id_type=MESH,
        )

    def tok_copy(j, slot):
        base = pl.multiple_of(lax.rem(z + order(3 - j), 4) * CH, CH)
        return pltpu.make_async_copy(
            tok_hbm.at[:, pl.ds(base, CH), :], tok.at[slot], sem_tok.at[slot]
        )

    vw_copy = pltpu.make_async_copy(vw_hbm, vw, sem_w.at[0])
    proj_copy = pltpu.make_async_copy(proj_hbm, proj, sem_w.at[1])
    tok_copy(0, 0).start()
    vw_copy.start()
    tok_copy(1, 1).start()
    proj_copy.start()

    def w2_copy(i, slot):
        base = pl.multiple_of(i * 1536, 1536)
        return pltpu.make_async_copy(
            w2_hbm.at[pl.ds(base, 1536), :], wstage.at[slot], sem_w2.at[slot]
        )

    w2_copy(0, 0).start()
    w2_copy(1, 1).start()

    barrier = pltpu.get_barrier_semaphore()
    partners = [at(dx=d) for d in (1, 2, 3)] + [at(dy=d) for d in (1, 2, 3)]
    partners += [at(dz=d) for d in (1, 2, 3)] + [at(dc=1)]
    for device in partners:
        pl.semaphore_signal(barrier, inc=1, device_id=device, device_id_type=MESH)
    pl.semaphore_wait(barrier, len(partners))

    kqp[...] = jnp.zeros_like(kqp)
    kqp[0:16, :] = kq_ref[...]
    head_of = lax.broadcasted_iota(jnp.int32, (128, 1024), 0)
    lane = lax.broadcasted_iota(jnp.int32, (128, 1024), 1)
    expand[...] = jnp.where(lax.div(lane, 64) == head_of, 1.0, 0.0).astype(BF)

    vw_copy.wait()

    def part_copy(j):
        dz = order(3 - j)
        return remote(
            part_send.at[j], part_recv.at[3 - dz], ps_send.at[j], ps_recv.at[3 - dz], at(dz=dz)
        )

    def stat_copy(j):
        dz = order(3 - j)
        return remote(
            stat_send.at[j], stat_recv.at[3 - dz], st_send.at[j], st_recv.at[3 - dz], at(dz=dz)
        )

    def pool_chunk(j, _):
        slot = lax.rem(j, 2)
        tok_copy(j, slot).wait()
        scores = lax.dot_general(
            tok[slot].reshape(NV * CH, 1024), kqp[...], NT, preferred_element_type=F32
        ).reshape(NV, CH, 128)
        peak = jnp.max(scores, axis=0)
        weights = jnp.exp(scores - peak[None])
        totals = jnp.sum(weights, axis=0)
        first_lanes = lax.broadcasted_iota(jnp.int32, (CH, 128), 1) < 16
        stat_send[j] = jnp.where(first_lanes, peak, pltpu.roll(totals, 16, 1))
        wn[...] = weights.astype(BF).reshape(NV * CH, 128)

        def columns(i, _):
            cs = pl.ds(pl.multiple_of(i * 256, 256), 256)
            values = dot(tok[slot].reshape(NV * CH, 1024), vw[:, cs])
            wide = dot(wn[...], expand[:, cs])
            summed = jnp.sum((values * wide).reshape(NV, CH, 256), axis=0)
            part_send[j, :, cs] = summed.astype(BF)
            return 0

        lax.fori_loop(0, 4, columns, 0)

        @pl.when(j < 2)
        def _():
            tok_copy(j + 2, slot).start()

        @pl.when(j < 3)
        def _():
            part_copy(j).start()
            stat_copy(j).start()

        return 0

    lax.fori_loop(0, 4, pool_chunk, 0)

    for i in range(3):
        part_copy(i).wait_send()
        stat_copy(i).wait_send()
        remote(part_send.at[0], part_recv.at[i], ps_send.at[0], ps_recv.at[i], at(dz=1)).wait_recv()
        remote(stat_send.at[0], stat_recv.at[i], st_send.at[0], st_recv.at[i], at(dz=1)).wait_recv()
    peaks = [stat_send[3]] + [stat_recv[i] for i in range(3)]
    top = functools.reduce(jnp.maximum, peaks)
    factors = [jnp.exp(l - top) for l in peaks]
    inverse = 1.0 / sum(f * pltpu.roll(l, 112, 1) for f, l in zip(factors, peaks))
    real = lax.broadcasted_iota(jnp.int32, (CH, 128), 1) < 16
    total = jnp.zeros((CH, 1024), F32)
    for g in range(4):
        share = jnp.where(real, factors[g] * inverse, 0.0)
        high = share.astype(BF)
        low = (share - high.astype(F32)).astype(BF)
        wide = dot(high, expand[...]) + dot(low, expand[...])
        part = part_send[3] if g == 0 else part_recv[g - 1]
        total = total + wide * part.astype(F32)
    own_rows = pl.ds(pl.multiple_of(z * CH, CH), CH)
    pooled[own_rows, :] = total.astype(BF)

    def pool_copy(d):
        return remote(
            pooled.at[own_rows, :], pooled.at[own_rows, :],
            pool_send.at[d - 1], pool_recv.at[3 - d], at(dz=d),
        )

    for d in (1, 3, 2):
        pool_copy(d).start()

    def relayout(i, _):
        slot = lax.rem(i, 2)
        w2_copy(i, slot).wait()
        wf[...] = wstage[slot].astype(F32)
        rows = pl.ds(pl.multiple_of(i * 128, 128), 128)
        for n in range(12):
            wq[rows, n * 128 : (n + 1) * 128] = wf[pl.ds(n, 128, stride=12), :].astype(BF)

        @pl.when(i < 14)
        def _():
            w2_copy(i + 2, slot).start()

        return 0

    lax.fori_loop(0, 16, relayout, 0)
    proj_copy.wait()

    for d in (1, 2, 3):
        src_rows = pl.ds(pl.multiple_of(lax.rem(z + d, 4) * CH, CH), CH)
        remote(
            pooled.at[src_rows, :], pooled.at[src_rows, :],
            pool_send.at[0], pool_recv.at[d - 1], at(dz=d),
        ).wait_recv()

    def project(i, _):
        cs = pl.ds(pl.multiple_of(i * 512, 512), 512)
        emb[:, cs] = dot(pooled[...], proj[:, cs])
        return 0

    lax.fori_loop(0, 4, project, 0)

    def norm(i, _):
        rows = pl.ds(pl.multiple_of(i * 128, 128), 128)
        block = emb[rows, :]
        center = block - jnp.mean(block, axis=1, keepdims=True)
        variance = jnp.mean(center * center, axis=1, keepdims=True)
        normed[rows, :] = (center / jnp.sqrt(variance + 1e-05) * gain_ref[...]).astype(BF)
        return 0

    lax.fori_loop(0, 4, norm, 0)

    queries = dot(normed[...], wq[:, 0:512]) * Q_SCALE
    for h in range(4):
        q4[h] = queries[:, h * 128 : (h + 1) * 128].astype(BF)
    keys = dot(normed[...], wq[:, 512:1024])
    for h in range(4):
        kv4[h, 0:512, :] = keys[:, h * 128 : (h + 1) * 128].astype(BF)
    values = dot(normed[...], wq[:, 1024:1536])
    for h in range(4):
        for j in range(4):
            tile = values[j * 128 : (j + 1) * 128, h * 128 : (h + 1) * 128]
            kv4[h, 512 + j * 128 : 512 + (j + 1) * 128, :] = tile.T.astype(BF)

    def q_copy(d):
        dst = order((4 - d) % 4)
        head = lax.rem(x + d, 4)
        return remote(q4.at[head], q_buf.at[dst], q_send.at[d - 1], q_recv.at[dst - 1], at(dx=d))

    def kvx_copy(d):
        dst = order((4 - d) % 4)
        head = lax.rem(x + d, 4)
        return remote(kv4.at[head], kv.at[dst], kvx_send.at[d - 1], kv_recv.at[dst], at(dx=d))

    def own_copy(n, k):
        device = (at(dc=1), at(dy=1), at(dy=3), at(dy=2))[k]
        slot = n + (4, 16, 8, 24)[k]
        return remote(kv.at[n], kv.at[slot], own_send.at[n * 4 + k], kv_recv.at[slot], device)

    def fwd_copy(n):
        index = lax.div(n - 8, 8) * 4 + lax.rem(n, 4)
        return remote(
            kv.at[n], kv.at[n + 4], fwd_send.at[index], kv_recv.at[n + 4], at(dc=1)
        )

    for d in (1, 3, 2):
        q_copy(d).start()
    for d in (1, 3, 2):
        kvx_copy(d).start()
    q_buf[0] = q4[x]
    kv[0] = kv4[x]
    for k in range(3):
        own_copy(0, k).start()

    my_cols = pl.ds(pl.multiple_of(z * 512, 512), 512)
    ow_own = pltpu.make_async_copy(ow_hbm.at[:, my_cols], ow.at[z], sem_ow_own)
    ow_own.start()

    def ow_copy(d):
        cols = pl.ds(pl.multiple_of(lax.rem(z + d, 4) * 512, 512), 512)
        return remote(
            ow_hbm.at[:, cols], ow.at[z], ow_send.at[d - 1], ow_recv.at[3 - d], at(dz=d)
        )

    for d in (1, 3, 2):
        ow_copy(d).start()

    def arrive(n):
        remote(kv.at[n], kv.at[n], own_send.at[0], kv_recv.at[n], at(dc=1)).wait_recv()
        section = lax.div(n, 4)

        @pl.when(section == 0)
        def _():
            for k in range(3):
                own_copy(n, k).start()

        @pl.when(section == 1)
        def _():
            own_copy(n - 4, 3).start()

        @pl.when(jnp.logical_and(section >= 2, lax.rem(section, 2) == 0))
        def _():
            fwd_copy(n).start()

    for r in range(3):
        remote(q_buf.at[0], q_buf.at[r + 1], q_send.at[0], q_recv.at[r], at(dx=1)).wait_recv()
    acc[...] = jnp.zeros_like(acc)
    mref[...] = jnp.full_like(mref, -1e30)
    tiles = (s0, s1)
    ones = jnp.ones((16, 512), BF)

    def logits(n, t, slot):
        s = lax.dot_general(kv[n, 0:512, :], q_buf[t], NT, preferred_element_type=F32)
        tiles[slot][...] = s
        return jnp.max(s, axis=0, keepdims=True)

    def fold(n, t, slot, block_max):
        old = mref[t, 0:1, :]
        new = jnp.maximum(old, block_max)
        mref[t, 0:1, :] = new
        p = jnp.exp2(tiles[slot][...] - new).astype(BF)
        vt = jnp.concatenate([kv[n, 512 + j * 128 : 640 + j * 128, :] for j in range(4)], axis=1)
        vt = jnp.concatenate([vt, ones], axis=0)
        acc[t] = acc[t] * jnp.exp2(old - new) + dot(vt, p)

    first = logits(0, 0, 0)

    def block_step(n, block_max):
        @pl.when(n < 31)
        def _():
            arrive(n + 1)

        for u in range(4):
            ahead = n if u < 3 else jnp.minimum(n + 1, 31)
            following = logits(ahead, (u + 1) % 4, (u + 1) % 2)
            fold(n, u, u % 2, block_max)
            block_max = following
        return block_max

    lax.fori_loop(0, 32, block_step, first)

    mine = z * 4 + x

    def ax_copy(r):
        dx = order(r)
        back = order((4 - dx) % 4)
        return remote(
            stage.at[r - 1], att.at[mine], ax_send.at[r - 1], ax_recv.at[back - 1], at(dx=dx)
        )

    for r in (3, 2, 1, 0):
        a = acc[r]
        block = (a[0:128] / a[128:129]).T.astype(BF)
        if r == 0:
            att[mine] = block
        else:
            stage[r - 1] = block
            ax_copy(r).start()

    def az_copy(r, d):
        head = z * 4 + lax.rem(x + order(r), 4)
        return remote(
            att.at[head], att.at[head], az_send.at[r * 3 + d - 1], az_recv.at[r * 3 + 3 - d],
            at(dz=d),
        )

    for r in (0, 3, 1, 2):
        if r > 0:
            head = z * 4 + lax.rem(x + order(r), 4)
            remote(
                stage.at[0], att.at[head], ax_send.at[0], ax_recv.at[r - 1], at(dx=1)
            ).wait_recv()
        for d in (1, 3, 2):
            az_copy(r, d).start()

    ow_own.wait()
    for d in (1, 2, 3):
        src = lax.rem(z + d, 4)
        remote(
            ow.at[src], ow.at[src], ow_send.at[0], ow_recv.at[d - 1], at(dz=1)
        ).wait_recv()
    for r in range(4):
        for d in (1, 2, 3):
            head = lax.rem(z + d, 4) * 4 + lax.rem(x + order(r), 4)
            remote(
                att.at[head], att.at[head], az_send.at[0], az_recv.at[r * 3 + d - 1], at(dz=1)
            ).wait_recv()

    result = emb[:, my_cols]
    for g in range(4):
        heads = jnp.concatenate([att[g * 4 + h] for h in range(4)], axis=1)
        result = result + dot(heads, ow[g])
    out_ref[...] = result.astype(BF)

    for d in (1, 2, 3):
        pool_copy(d).wait_send()
        q_copy(d).wait_send()
        kvx_copy(d).wait_send()
        ow_copy(d).wait_send()
        ax_copy(d).wait_send()
        for r in range(4):
            az_copy(r, d).wait_send()

    def drain(n, _):
        for k in range(4):
            own_copy(n, k).wait_send()
        return 0

    lax.fori_loop(0, 4, drain, 0)

    def drain_fwd(i, _):
        fwd_copy(8 + lax.div(i, 4) * 8 + lax.rem(i, 4)).wait_send()
        return 0

    lax.fori_loop(0, 12, drain_fwd, 0)


def on_device(tokens, key_query, value_weight, proj_weight, norm_gain, qkv_weight, out_weight):
    dma = pltpu.SemaphoreType.DMA
    vm = pltpu.VMEM
    scratch = [
        vm((2, NV, CH, 1024), BF),
        vm((128, 1024), BF),
        vm((128, 1024), BF),
        vm((1024, 1024), BF),
        vm((1024, 2048), BF),
        vm((2, 1536, 128), BF),
        vm((1536, 128), F32),
        vm((2048, 1536), BF),
        vm((NV * CH, 128), BF),
        vm((4, CH, 1024), BF),
        vm((3, CH, 1024), BF),
        vm((4, CH, 128), F32),
        vm((3, CH, 128), F32),
        vm((ROWS, 1024), BF),
        vm((ROWS, 2048), F32),
        vm((ROWS, 2048), BF),
        vm((4, ROWS, 128), BF),
        vm((4, 2 * ROWS, 128), BF),
        vm((4, ROWS, 128), BF),
        vm((32, 2 * ROWS, 128), BF),
        vm((512, 512), F32),
        vm((512, 512), F32),
        vm((4, 144, 512), F32),
        vm((4, 8, 512), F32),
        vm((4, 512, 512), BF),
        vm((3, ROWS, 128), BF),
        vm((16, ROWS, 128), BF),
        dma((2,)), dma((2,)), dma((2,)), dma,
        dma((3,)), dma((3,)), dma((3,)), dma((3,)), dma((3,)), dma((3,)),
        dma((3,)), dma((3,)), dma((3,)), dma((16,)), dma((12,)), dma((32,)),
        dma((3,)), dma((3,)), dma((3,)), dma((3,)), dma((12,)), dma((12,)),
    ]
    anywhere = pl.BlockSpec(memory_space=pl.ANY)
    vmem = pl.BlockSpec(memory_space=pltpu.VMEM)
    return pl.pallas_call(
        kernel,
        out_shape=jax.ShapeDtypeStruct((ROWS, 512), BF),
        in_specs=[anywhere, vmem, anywhere, anywhere, vmem, anywhere, anywhere],
        out_specs=vmem,
        scratch_shapes=scratch,
        compiler_params=pltpu.CompilerParams(
            collective_id=1, has_side_effects=True, vmem_limit_bytes=62 * 1024 * 1024
        ),
        name="block",
    )(
        tokens,
        key_query.T,
        value_weight,
        proj_weight,
        norm_gain.reshape(1, 2048),
        qkv_weight.reshape(2048 * 12, 128),
        out_weight.reshape(512, 2048),
    )


def solution(mesh):
    return jax.shard_map(
        on_device,
        mesh=mesh,
        in_specs=(
            P("var", "patch", None),
            P(),
            P(),
            P(),
            P(),
            P(None, None, "var", None),
            P("var", None, None),
        ),
        out_specs=P("patch", "var"),
        check_vma=False,
    )
```

```python
import functools

import jax
import jax.numpy as jnp
from jax import lax
from jax.experimental import pallas as pl
from jax.experimental.pallas import tpu as pltpu
from jax.sharding import PartitionSpec as P

MESH = pl.DeviceIdType.MESH
NT = (((1,), (1,)), ((), ()))
BF = jnp.bfloat16
F32 = jnp.float32

ROWS, NV, CH = 512, 12, 128
EARLY = 24
Q_SCALE = 128 ** (-0.5) * 1.4426950408889634


def order(e):
    if isinstance(e, int):
        return (0, 1, 3, 2)[e]
    return e + lax.div(e, 2) * (5 - 2 * e)


def dot(a, b):
    return jnp.dot(a, b, preferred_element_type=F32)


def kernel(
    tok_hbm, kq_ref, vw_hbm, proj_hbm, gain_ref, w2_hbm, ow_hbm,
    out_ref,
    tok, kqp, expand, vw, proj, wstage, wf, wq,
    wn, part_send, part_recv, stat_send, stat_recv, pooled,
    emb, normed, q4, kv4, q_buf, kv, s0, s1, acc, mref,
    ow, stage, att,
    sem_tok, sem_w, sem_w2, sem_ow_own,
    ps_send, ps_recv, st_send, st_recv, pool_send, pool_recv,
    q_send, q_recv, kvx_send, own_send, fwd_send, kv_recv,
    ow_send, ow_recv, ax_send, ax_recv, az_send, az_recv,
):
    z = lax.axis_index("var")
    place = lax.axis_index("patch")
    x = lax.div(place, 8)
    y = lax.rem(lax.div(place, 2), 4)
    c = lax.rem(place, 2)

    def at(dx=0, dy=0, dz=0, dc=0):
        px = lax.rem(x + dx, 4)
        py = lax.rem(y + dy, 4)
        pc = lax.rem(c + dc, 2)
        return (lax.rem(z + dz, 4), (px * 4 + py) * 2 + pc)

    def remote(src, dst, send, recv, device):
        return pltpu.make_async_remote_copy(
            src_ref=src, dst_ref=dst, send_sem=send, recv_sem=recv,
            device_id=device, device_id_type=MESH,
        )

    def tok_copy(j, slot):
        base = pl.multiple_of(lax.rem(z + order(3 - j), 4) * CH, CH)
        return pltpu.make_async_copy(
            tok_hbm.at[:, pl.ds(base, CH), :], tok.at[slot], sem_tok.at[slot]
        )

    vw_copy = pltpu.make_async_copy(vw_hbm, vw, sem_w.at[0])
    proj_copy = pltpu.make_async_copy(proj_hbm, proj, sem_w.at[1])
    tok_copy(0, 0).start()
    vw_copy.start()
    tok_copy(1, 1).start()
    proj_copy.start()

    def w2_copy(i, slot):
        base = pl.multiple_of(i * 1536, 1536)
        return pltpu.make_async_copy(
            w2_hbm.at[pl.ds(base, 1536), :], wstage.at[slot], sem_w2.at[slot]
        )

    w2_copy(0, 0).start()
    w2_copy(1, 1).start()

    barrier = pltpu.get_barrier_semaphore()
    partners = [at(dx=d) for d in (1, 2, 3)] + [at(dy=d) for d in (1, 2, 3)]
    partners += [at(dz=d) for d in (1, 2, 3)] + [at(dc=1)]
    for device in partners:
        pl.semaphore_signal(barrier, inc=1, device_id=device, device_id_type=MESH)

    kqp[...] = jnp.zeros_like(kqp)
    kqp[0:16, :] = kq_ref[...]
    head_of = lax.broadcasted_iota(jnp.int32, (128, 1024), 0)
    lane = lax.broadcasted_iota(jnp.int32, (128, 1024), 1)
    expand[...] = jnp.where(lax.div(lane, 64) == head_of, 1.0, 0.0).astype(BF)

    vw_copy.wait()

    def part_copy(j):
        dz = order(3 - j)
        return remote(
            part_send.at[j], part_recv.at[3 - dz], ps_send.at[j], ps_recv.at[3 - dz], at(dz=dz)
        )

    def stat_copy(j):
        dz = order(3 - j)
        return remote(
            stat_send.at[j], stat_recv.at[3 - dz], st_send.at[j], st_recv.at[3 - dz], at(dz=dz)
        )

    def pool_chunk(j, _):
        slot = lax.rem(j, 2)
        tok_copy(j, slot).wait()
        scores = lax.dot_general(
            tok[slot].reshape(NV * CH, 1024), kqp[...], NT, preferred_element_type=F32
        ).reshape(NV, CH, 128)
        peak = jnp.max(scores, axis=0)
        weights = jnp.exp(scores - peak[None])
        totals = jnp.sum(weights, axis=0)
        first_lanes = lax.broadcasted_iota(jnp.int32, (CH, 128), 1) < 16
        stat_send[j] = jnp.where(first_lanes, peak, pltpu.roll(totals, 16, 1))
        wn[...] = weights.astype(BF).reshape(NV * CH, 128)

        def columns(i, _):
            cs = pl.ds(pl.multiple_of(i * 256, 256), 256)
            values = dot(tok[slot].reshape(NV * CH, 1024), vw[:, cs])
            wide = dot(wn[...], expand[:, cs])
            summed = jnp.sum((values * wide).reshape(NV, CH, 256), axis=0)
            part_send[j, :, cs] = summed.astype(BF)
            return 0

        lax.fori_loop(0, 4, columns, 0)

        @pl.when(j < 2)
        def _():
            tok_copy(j + 2, slot).start()

        @pl.when(j == 0)
        def _():
            pl.semaphore_wait(barrier, len(partners))

        @pl.when(j < 3)
        def _():
            part_copy(j).start()
            stat_copy(j).start()

        return 0

    lax.fori_loop(0, 4, pool_chunk, 0)

    for i in range(3):
        part_copy(i).wait_send()
        stat_copy(i).wait_send()
        remote(part_send.at[0], part_recv.at[i], ps_send.at[0], ps_recv.at[i], at(dz=1)).wait_recv()
        remote(stat_send.at[0], stat_recv.at[i], st_send.at[0], st_recv.at[i], at(dz=1)).wait_recv()
    peaks = [stat_send[3]] + [stat_recv[i] for i in range(3)]
    top = functools.reduce(jnp.maximum, peaks)
    factors = [jnp.exp(l - top) for l in peaks]
    inverse = 1.0 / sum(f * pltpu.roll(l, 112, 1) for f, l in zip(factors, peaks))
    real = lax.broadcasted_iota(jnp.int32, (CH, 128), 1) < 16
    total = jnp.zeros((CH, 1024), F32)
    for g in range(4):
        share = jnp.where(real, factors[g] * inverse, 0.0)
        high = share.astype(BF)
        low = (share - high.astype(F32)).astype(BF)
        wide = dot(high, expand[...]) + dot(low, expand[...])
        part = part_send[3] if g == 0 else part_recv[g - 1]
        total = total + wide * part.astype(F32)
    own_rows = pl.ds(pl.multiple_of(z * CH, CH), CH)
    pooled[own_rows, :] = total.astype(BF)

    def pool_copy(d):
        return remote(
            pooled.at[own_rows, :], pooled.at[own_rows, :],
            pool_send.at[d - 1], pool_recv.at[3 - d], at(dz=d),
        )

    for d in (1, 3, 2):
        pool_copy(d).start()

    def relayout(i, _):
        slot = lax.rem(i, 2)
        w2_copy(i, slot).wait()
        wf[...] = wstage[slot].astype(F32)
        rows = pl.ds(pl.multiple_of(i * 128, 128), 128)
        for n in range(12):
            to = n if n < 4 else 4 + 2 * (n % 4) + n // 8
            wq[rows, to * 128 : (to + 1) * 128] = wf[pl.ds(n, 128, stride=12), :].astype(BF)

        @pl.when(i < 14)
        def _():
            w2_copy(i + 2, slot).start()

        return 0

    lax.fori_loop(0, 16, relayout, 0)
    proj_copy.wait()

    for d in (1, 2, 3):
        src_rows = pl.ds(pl.multiple_of(lax.rem(z + d, 4) * CH, CH), CH)
        remote(
            pooled.at[src_rows, :], pooled.at[src_rows, :],
            pool_send.at[0], pool_recv.at[d - 1], at(dz=d),
        ).wait_recv()

    def project(i, _):
        cs = pl.ds(pl.multiple_of(i * 512, 512), 512)
        emb[:, cs] = dot(pooled[...], proj[:, cs])
        return 0

    lax.fori_loop(0, 4, project, 0)

    def norm(i, _):
        rows = pl.ds(pl.multiple_of(i * 128, 128), 128)
        block = emb[rows, :]
        center = block - jnp.mean(block, axis=1, keepdims=True)
        variance = jnp.mean(center * center, axis=1, keepdims=True)
        normed[rows, :] = (center / jnp.sqrt(variance + 1e-05) * gain_ref[...]).astype(BF)
        return 0

    lax.fori_loop(0, 4, norm, 0)

    def q_copy(d):
        dst = order((4 - d) % 4)
        head = lax.rem(x + d, 4)
        return remote(
            q4.at[head], q_buf.at[3 - dst], q_send.at[d - 1], q_recv.at[dst - 1], at(dx=d)
        )

    def kvx_copy(d):
        dst = order((4 - d) % 4)
        head = lax.rem(x + d, 4)
        return remote(kv4.at[head], kv.at[dst], kvx_send.at[d - 1], kv_recv.at[dst], at(dx=d))

    def own_copy(n, k):
        device = (at(dc=1), at(dy=1), at(dy=3), at(dy=2))[k]
        slot = n + (4, 16, 8, 24)[k]
        return remote(kv.at[n], kv.at[slot], own_send.at[n * 4 + k], kv_recv.at[slot], device)

    def fwd_copy(n):
        index = lax.div(n - 8, 8) * 4 + lax.rem(n, 4)
        return remote(
            kv.at[n], kv.at[n + 4], fwd_send.at[index], kv_recv.at[n + 4], at(dc=1)
        )

    queries = dot(normed[...], wq[:, 0:512]) * Q_SCALE
    for h in range(4):
        q4[h] = queries[:, h * 128 : (h + 1) * 128].astype(BF)
    for d in (2, 1, 3):
        q_copy(d).start()
    q_buf[3] = q4[x]

    def keys_values(head, write):
        cs = pl.ds(pl.multiple_of(512 + head * 256, 256), 256)
        both = dot(normed[...], wq[:, cs])
        write(slice(0, 512), both[:, 0:128].astype(BF))
        for j in range(4):
            tile = both[j * 128 : (j + 1) * 128, 128:256]
            write(slice(512 + j * 128, 640 + j * 128), tile.T.astype(BF))

    def write_own(rows, value):
        kv[0, rows, :] = value

    keys_values(x, write_own)
    for k in range(3):
        own_copy(0, k).start()
    for d in (1, 3, 2):
        head = lax.rem(x + d, 4)

        def write_other(rows, value, head=head):
            kv4[head, rows, :] = value

        keys_values(head, write_other)
        kvx_copy(d).start()

    my_cols = pl.ds(pl.multiple_of(z * 512, 512), 512)
    ow_own = pltpu.make_async_copy(ow_hbm.at[:, my_cols], ow.at[z], sem_ow_own)
    ow_own.start()

    def ow_copy(d):
        cols = pl.ds(pl.multiple_of(lax.rem(z + d, 4) * 512, 512), 512)
        return remote(
            ow_hbm.at[:, cols], ow.at[z], ow_send.at[d - 1], ow_recv.at[3 - d], at(dz=d)
        )

    for d in (1, 3, 2):
        ow_copy(d).start()

    def arrive(n):
        remote(kv.at[n], kv.at[n], own_send.at[0], kv_recv.at[n], at(dc=1)).wait_recv()
        section = lax.div(n, 4)

        @pl.when(section == 0)
        def _():
            for k in range(3):
                own_copy(n, k).start()

        @pl.when(section == 1)
        def _():
            own_copy(n - 4, 3).start()

        @pl.when(jnp.logical_and(section >= 2, lax.rem(section, 2) == 0))
        def _():
            fwd_copy(n).start()

    for r in range(3):
        remote(q_buf.at[3], q_buf.at[2 - r], q_send.at[0], q_recv.at[r], at(dx=1)).wait_recv()
    acc[...] = jnp.zeros_like(acc)
    mref[...] = jnp.full_like(mref, -1e30)
    tiles = (s0, s1)
    ones = jnp.ones((16, 512), BF)

    def logits(n, t, slot):
        s = lax.dot_general(kv[n, 0:512, :], q_buf[t], NT, preferred_element_type=F32)
        tiles[slot][...] = s
        return jnp.max(s, axis=0, keepdims=True)

    def fold(n, t, slot, block_max):
        old = mref[t, 0:1, :]
        new = jnp.maximum(old, block_max)
        mref[t, 0:1, :] = new
        p = jnp.exp2(tiles[slot][...] - new).astype(BF)
        vt = jnp.concatenate([kv[n, 512 + j * 128 : 640 + j * 128, :] for j in range(4)], axis=1)
        vt = jnp.concatenate([vt, ones], axis=0)
        acc[t] = acc[t] * jnp.exp2(old - new) + dot(vt, p)

    first = logits(0, 0, 0)

    def block_step(n, block_max):
        arrive(n + 1)
        for u in range(4):
            ahead = n if u < 3 else n + 1
            following = logits(ahead, (u + 1) % 4, (u + 1) % 2)
            fold(n, u, u % 2, block_max)
            block_max = following
        return block_max

    carry = lax.fori_loop(0, EARLY, block_step, first)
    for n in range(EARLY + 1, 32):
        arrive(n)

    mine = z * 4 + x

    def ax_copy(t):
        dx = order(3 - t)
        back = order((4 - dx) % 4) if isinstance(dx, int) else order(lax.rem(4 - dx, 4))
        return remote(
            stage.at[t], att.at[mine], ax_send.at[t], ax_recv.at[3 - back], at(dx=dx)
        )

    def az_copy(t, d):
        head = z * 4 + lax.rem(x + order(3 - t), 4)
        return remote(
            att.at[head], att.at[head], az_send.at[t * 3 + d - 1], az_recv.at[t * 3 + 3 - d],
            at(dz=d),
        )

    def share(t):
        for d in (2, 1, 3):
            az_copy(t, d).start()

    def ax_arrive(t):
        head = z * 4 + lax.rem(x + order(3 - t), 4)
        remote(stage.at[0], att.at[head], ax_send.at[0], ax_recv.at[t], at(dx=1)).wait_recv()

    def tile_step(t, block_max):
        def group(i, block_max):
            base = EARLY + i * 4
            last = i == (32 - EARLY) // 4 - 1
            for u in range(4):
                if u < 3:
                    following = logits(base + u + 1, t, (u + 1) % 2)
                else:
                    following = logits(
                        jnp.where(last, EARLY, base + 4),
                        jnp.where(last, jnp.minimum(t + 1, 3), t),
                        0,
                    )
                fold(base + u, t, u % 2, block_max)
                block_max = following
            return block_max

        block_max = lax.fori_loop(0, (32 - EARLY) // 4, group, block_max)
        a = acc[t]
        block = (a[0:128] / a[128:129]).T.astype(BF)

        @pl.when(t < 3)
        def _():
            stage[t] = block
            ax_copy(t).start()

        @pl.when(t == 3)
        def _():
            att[mine] = block
            share(3)

        @pl.when(t > 0)
        def _():
            ax_arrive(t - 1)
            share(t - 1)

        return block_max

    lax.fori_loop(0, 4, tile_step, carry)

    ow_own.wait()
    for d in (1, 2, 3):
        src = lax.rem(z + d, 4)
        remote(
            ow.at[src], ow.at[src], ow_send.at[0], ow_recv.at[d - 1], at(dz=1)
        ).wait_recv()
    for t in range(4):
        for d in (1, 2, 3):
            head = lax.rem(z + d, 4) * 4 + lax.rem(x + order(3 - t), 4)
            remote(
                att.at[head], att.at[head], az_send.at[0], az_recv.at[t * 3 + d - 1], at(dz=1)
            ).wait_recv()

    result = emb[:, my_cols]
    for g in range(4):
        heads = jnp.concatenate([att[g * 4 + h] for h in range(4)], axis=1)
        result = result + dot(heads, ow[g])
    out_ref[...] = result.astype(BF)

    for d in (1, 2, 3):
        pool_copy(d).wait_send()
        q_copy(d).wait_send()
        kvx_copy(d).wait_send()
        ow_copy(d).wait_send()
        ax_copy(d - 1).wait_send()
        for t in range(4):
            az_copy(t, d).wait_send()

    def drain(n, _):
        for k in range(4):
            own_copy(n, k).wait_send()
        return 0

    lax.fori_loop(0, 4, drain, 0)

    def drain_fwd(i, _):
        fwd_copy(8 + lax.div(i, 4) * 8 + lax.rem(i, 4)).wait_send()
        return 0

    lax.fori_loop(0, 12, drain_fwd, 0)


def on_device(tokens, key_query, value_weight, proj_weight, norm_gain, qkv_weight, out_weight):
    dma = pltpu.SemaphoreType.DMA
    vm = pltpu.VMEM
    scratch = [
        vm((2, NV, CH, 1024), BF),
        vm((128, 1024), BF),
        vm((128, 1024), BF),
        vm((1024, 1024), BF),
        vm((1024, 2048), BF),
        vm((2, 1536, 128), BF),
        vm((1536, 128), F32),
        vm((2048, 1536), BF),
        vm((NV * CH, 128), BF),
        vm((4, CH, 1024), BF),
        vm((3, CH, 1024), BF),
        vm((4, CH, 128), F32),
        vm((3, CH, 128), F32),
        vm((ROWS, 1024), BF),
        vm((ROWS, 2048), F32),
        vm((ROWS, 2048), BF),
        vm((4, ROWS, 128), BF),
        vm((4, 2 * ROWS, 128), BF),
        vm((4, ROWS, 128), BF),
        vm((32, 2 * ROWS, 128), BF),
        vm((512, 512), F32),
        vm((512, 512), F32),
        vm((4, 144, 512), F32),
        vm((4, 8, 512), F32),
        vm((4, 512, 512), BF),
        vm((3, ROWS, 128), BF),
        vm((16, ROWS, 128), BF),
        dma((2,)), dma((2,)), dma((2,)), dma,
        dma((3,)), dma((3,)), dma((3,)), dma((3,)), dma((3,)), dma((3,)),
        dma((3,)), dma((3,)), dma((3,)), dma((16,)), dma((12,)), dma((32,)),
        dma((3,)), dma((3,)), dma((3,)), dma((3,)), dma((12,)), dma((12,)),
    ]
    anywhere = pl.BlockSpec(memory_space=pl.ANY)
    vmem = pl.BlockSpec(memory_space=pltpu.VMEM)
    return pl.pallas_call(
        kernel,
        out_shape=jax.ShapeDtypeStruct((ROWS, 512), BF),
        in_specs=[anywhere, vmem, anywhere, anywhere, vmem, anywhere, anywhere],
        out_specs=vmem,
        scratch_shapes=scratch,
        compiler_params=pltpu.CompilerParams(
            collective_id=1, has_side_effects=True, vmem_limit_bytes=62 * 1024 * 1024
        ),
        name="block",
    )(
        tokens,
        key_query.T,
        value_weight,
        proj_weight,
        norm_gain.reshape(1, 2048),
        qkv_weight.reshape(2048 * 12, 128),
        out_weight.reshape(512, 2048),
    )


def solution(mesh):
    return jax.shard_map(
        on_device,
        mesh=mesh,
        in_specs=(
            P("var", "patch", None),
            P(),
            P(),
            P(),
            P(),
            P(None, None, "var", None),
            P("var", None, None),
        ),
        out_specs=P("patch", "var"),
        check_vma=False,
    )
```

```python
import functools

import jax
import jax.numpy as jnp
from jax import lax
from jax.experimental import pallas as pl
from jax.experimental.pallas import tpu as pltpu
from jax.sharding import PartitionSpec as P

MESH = pl.DeviceIdType.MESH
NT = (((1,), (1,)), ((), ()))
BF = jnp.bfloat16
F32 = jnp.float32

ROWS, NV, CH = 512, 12, 128
EARLY = 20
Q_SCALE = 128 ** (-0.5) * 1.4426950408889634


def order(e):
    if isinstance(e, int):
        return (0, 1, 3, 2)[e]
    return e + lax.div(e, 2) * (5 - 2 * e)


def dot(a, b):
    return jnp.dot(a, b, preferred_element_type=F32)


def kernel(
    tok_hbm, kq_ref, vw_hbm, proj_hbm, gain_ref, w2_hbm, ow_hbm,
    out_ref,
    tok, kqp, expand, vw, proj, wstage, wf, wq,
    wn, part_send, part_recv, stat_send, stat_recv, pooled,
    emb, normed, q4, kv4, q_buf, kv, s0, s1, acc, mref,
    ow, stage, att,
    sem_tok, sem_w, sem_w2, sem_ow_own,
    ps_send, ps_recv, st_send, st_recv, pool_send, pool_recv,
    q_send, q_recv, kvx_send, own_send, fwd_send, hop_send, kv_recv,
    ow_send, ow_recv, ax_send, ax_recv, az_send, az_recv,
):
    z = lax.axis_index("var")
    place = lax.axis_index("patch")
    x = lax.div(place, 8)
    y = lax.rem(lax.div(place, 2), 4)
    c = lax.rem(place, 2)

    def at(dx=0, dy=0, dz=0, dc=0):
        px = lax.rem(x + dx, 4)
        py = lax.rem(y + dy, 4)
        pc = lax.rem(c + dc, 2)
        return (lax.rem(z + dz, 4), (px * 4 + py) * 2 + pc)

    def remote(src, dst, send, recv, device):
        return pltpu.make_async_remote_copy(
            src_ref=src, dst_ref=dst, send_sem=send, recv_sem=recv,
            device_id=device, device_id_type=MESH,
        )

    def tok_copy(j, slot):
        base = pl.multiple_of(lax.rem(z + order(3 - j), 4) * CH, CH)
        return pltpu.make_async_copy(
            tok_hbm.at[:, pl.ds(base, CH), :], tok.at[slot], sem_tok.at[slot]
        )

    vw_copy = pltpu.make_async_copy(vw_hbm, vw, sem_w.at[0])
    proj_copy = pltpu.make_async_copy(proj_hbm, proj, sem_w.at[1])
    tok_copy(0, 0).start()
    vw_copy.start()
    tok_copy(1, 1).start()
    proj_copy.start()

    def w2_copy(i, slot):
        base = pl.multiple_of(i * 1536, 1536)
        return pltpu.make_async_copy(
            w2_hbm.at[pl.ds(base, 1536), :], wstage.at[slot], sem_w2.at[slot]
        )

    w2_copy(0, 0).start()
    w2_copy(1, 1).start()

    barrier = pltpu.get_barrier_semaphore()
    partners = [at(dx=d) for d in (1, 2, 3)] + [at(dy=d) for d in (1, 2, 3)]
    partners += [at(dz=d) for d in (1, 2, 3)] + [at(dc=1)]
    for device in partners:
        pl.semaphore_signal(barrier, inc=1, device_id=device, device_id_type=MESH)

    kqp[...] = jnp.zeros_like(kqp)
    kqp[0:16, :] = kq_ref[...]
    head_of = lax.broadcasted_iota(jnp.int32, (128, 1024), 0)
    lane = lax.broadcasted_iota(jnp.int32, (128, 1024), 1)
    expand[...] = jnp.where(lax.div(lane, 64) == head_of, 1.0, 0.0).astype(BF)

    vw_copy.wait()

    def part_copy(j):
        dz = order(3 - j)
        return remote(
            part_send.at[j], part_recv.at[3 - dz], ps_send.at[j], ps_recv.at[3 - dz], at(dz=dz)
        )

    def stat_copy(j):
        dz = order(3 - j)
        return remote(
            stat_send.at[j], stat_recv.at[3 - dz], st_send.at[j], st_recv.at[3 - dz], at(dz=dz)
        )

    def relayout(i):
        slot = lax.rem(i, 2)
        w2_copy(i, slot).wait()
        wf[...] = wstage[slot].astype(F32)
        rows = pl.ds(pl.multiple_of(i * 128, 128), 128)
        for n in range(12):
            to = n if n < 4 else 4 + 2 * (n % 4) + n // 8
            wq[rows, to * 128 : (to + 1) * 128] = wf[pl.ds(n, 128, stride=12), :].astype(BF)

        @pl.when(i < 14)
        def _():
            w2_copy(i + 2, slot).start()

    def pool_chunk(j, _):
        slot = lax.rem(j, 2)
        tok_copy(j, slot).wait()
        scores = lax.dot_general(
            tok[slot].reshape(NV * CH, 1024), kqp[...], NT, preferred_element_type=F32
        ).reshape(NV, CH, 128)
        peak = jnp.max(scores, axis=0)
        weights = jnp.exp(scores - peak[None])
        totals = jnp.sum(weights, axis=0)
        first_lanes = lax.broadcasted_iota(jnp.int32, (CH, 128), 1) < 16
        stat_send[j] = jnp.where(first_lanes, peak, pltpu.roll(totals, 16, 1))
        wn[...] = weights.astype(BF).reshape(NV * CH, 128)

        def columns(i, _):
            cs = pl.ds(pl.multiple_of(i * 256, 256), 256)
            values = dot(tok[slot].reshape(NV * CH, 1024), vw[:, cs])
            wide = dot(wn[...], expand[:, cs])
            summed = jnp.sum((values * wide).reshape(NV, CH, 256), axis=0)
            part_send[j, :, cs] = summed.astype(BF)
            relayout(j * 4 + i)
            return 0

        lax.fori_loop(0, 4, columns, 0)

        @pl.when(j < 2)
        def _():
            tok_copy(j + 2, slot).start()

        @pl.when(j == 0)
        def _():
            pl.semaphore_wait(barrier, len(partners))

        @pl.when(j < 3)
        def _():
            part_copy(j).start()
            stat_copy(j).start()

        return 0

    lax.fori_loop(0, 4, pool_chunk, 0)

    for i in range(3):
        part_copy(i).wait_send()
        stat_copy(i).wait_send()
        remote(part_send.at[0], part_recv.at[i], ps_send.at[0], ps_recv.at[i], at(dz=1)).wait_recv()
        remote(stat_send.at[0], stat_recv.at[i], st_send.at[0], st_recv.at[i], at(dz=1)).wait_recv()
    peaks = [stat_send[3]] + [stat_recv[i] for i in range(3)]
    top = functools.reduce(jnp.maximum, peaks)
    factors = [jnp.exp(l - top) for l in peaks]
    inverse = 1.0 / sum(f * pltpu.roll(l, 112, 1) for f, l in zip(factors, peaks))
    real = lax.broadcasted_iota(jnp.int32, (CH, 128), 1) < 16
    total = jnp.zeros((CH, 1024), F32)
    for g in range(4):
        share = jnp.where(real, factors[g] * inverse, 0.0)
        high = share.astype(BF)
        low = (share - high.astype(F32)).astype(BF)
        wide = dot(high, expand[...]) + dot(low, expand[...])
        part = part_send[3] if g == 0 else part_recv[g - 1]
        total = total + wide * part.astype(F32)
    own_rows = pl.ds(pl.multiple_of(z * CH, CH), CH)
    pooled[own_rows, :] = total.astype(BF)

    def pool_rows(dz, half=None):
        base = lax.rem(z + dz, 4) * CH
        if half is None:
            return pooled.at[pl.ds(pl.multiple_of(base, CH), CH), :]
        return pooled.at[pl.ds(pl.multiple_of(base + half * (CH // 2), CH // 2), CH // 2), :]

    def pool_copy(i):
        rows = (pool_rows(0), pool_rows(0), pool_rows(3, 0), pool_rows(1, 1))[i]
        return remote(rows, rows, pool_send.at[i], pool_recv.at[i], at(dz=(1, 3, 1, 3)[i]))

    def pool_arrive(i):
        rows = (pool_rows(3), pool_rows(1), pool_rows(2, 0), pool_rows(2, 1))[i]
        remote(rows, rows, pool_send.at[0], pool_recv.at[i], at(dz=1)).wait_recv()

    pool_copy(0).start()
    pool_copy(1).start()
    proj_copy.wait()
    for i in (0, 1):
        pool_arrive(i)
        pool_copy(i + 2).start()
    for i in (2, 3):
        pool_arrive(i)

    def project(i, _):
        cs = pl.ds(pl.multiple_of(i * 512, 512), 512)
        emb[:, cs] = dot(pooled[...], proj[:, cs])
        return 0

    lax.fori_loop(0, 4, project, 0)

    def norm(i, _):
        rows = pl.ds(pl.multiple_of(i * 128, 128), 128)
        block = emb[rows, :]
        center = block - jnp.mean(block, axis=1, keepdims=True)
        variance = jnp.mean(center * center, axis=1, keepdims=True)
        normed[rows, :] = (center / jnp.sqrt(variance + 1e-05) * gain_ref[...]).astype(BF)
        return 0

    lax.fori_loop(0, 4, norm, 0)

    def q_copy(d):
        dst = order((4 - d) % 4)
        head = lax.rem(x + d, 4)
        return remote(
            q4.at[head], q_buf.at[3 - dst], q_send.at[d - 1], q_recv.at[dst - 1], at(dx=d)
        )

    def kvx_copy(d):
        dst = order((4 - d) % 4)
        head = lax.rem(x + d, 4)
        return remote(kv4.at[head], kv.at[dst], kvx_send.at[d - 1], kv_recv.at[dst], at(dx=d))

    def own_copy(n, k):
        device = (at(dc=1), at(dy=1), at(dy=3))[k]
        slot = (n + 4, 9 + 2 * n, 8 + 2 * n)[k]
        return remote(kv.at[n], kv.at[slot], own_send.at[n * 3 + k], kv_recv.at[slot], device)

    def fwd_copy(n):
        late = lax.div(n, 24)
        return remote(
            kv.at[n], kv.at[n + 8 - 4 * late], fwd_send.at[n - 8 - 8 * late],
            kv_recv.at[n + 8 - 4 * late], at(dc=1),
        )

    def hop_copy(n):
        r = lax.div(n - 8, 2)
        up = lax.rem(n, 2)
        return remote(
            kv.at[n], kv.at[24 + r], hop_send.at[r], kv_recv.at[24 + r], at(dy=3 - 2 * up)
        )

    queries = dot(normed[...], wq[:, 0:512]) * Q_SCALE
    for h in range(4):
        q4[h] = queries[:, h * 128 : (h + 1) * 128].astype(BF)
    for d in (2, 1, 3):
        q_copy(d).start()
    q_buf[3] = q4[x]

    def keys_values(head, write):
        cs = pl.ds(pl.multiple_of(512 + head * 256, 256), 256)
        both = dot(normed[...], wq[:, cs])
        write(slice(0, 512), both[:, 0:128].astype(BF))
        for j in range(4):
            tile = both[j * 128 : (j + 1) * 128, 128:256]
            write(slice(512 + j * 128, 640 + j * 128), tile.T.astype(BF))

    def write_own(rows, value):
        kv[0, rows, :] = value

    keys_values(x, write_own)
    for k in range(3):
        own_copy(0, k).start()
    for d in (1, 3, 2):
        head = lax.rem(x + d, 4)

        def write_other(rows, value, head=head):
            kv4[head, rows, :] = value

        keys_values(head, write_other)
        kvx_copy(d).start()

    my_cols = pl.ds(pl.multiple_of(z * 512, 512), 512)
    ow_own = pltpu.make_async_copy(ow_hbm.at[:, my_cols], ow.at[z], sem_ow_own)
    ow_own.start()

    def ow_copy(d):
        cols = pl.ds(pl.multiple_of(lax.rem(z + d, 4) * 512, 512), 512)
        return remote(
            ow_hbm.at[:, cols], ow.at[z], ow_send.at[d - 1], ow_recv.at[3 - d], at(dz=d)
        )

    for d in (1, 3, 2):
        ow_copy(d).start()

    def arrive(n):
        remote(kv.at[n], kv.at[n], own_send.at[0], kv_recv.at[n], at(dc=1)).wait_recv()

        @pl.when(n < 4)
        def _():
            for k in range(3):
                own_copy(n, k).start()

        near = jnp.logical_and(n >= 8, n < 16)

        @pl.when(jnp.logical_and(near, lax.rem(n, 2) == jnp.where(n < 12, 1, 0)))
        def _():
            hop_copy(n).start()

        @pl.when(jnp.logical_or(near, jnp.logical_and(n >= 24, n < 28)))
        def _():
            fwd_copy(n).start()

    for r in range(3):
        remote(q_buf.at[3], q_buf.at[2 - r], q_send.at[0], q_recv.at[r], at(dx=1)).wait_recv()
    acc[...] = jnp.zeros_like(acc)
    mref[...] = jnp.full_like(mref, -1e30)
    tiles = (s0, s1)
    ones = jnp.ones((16, 512), BF)

    def logits(n, t, slot):
        s = lax.dot_general(kv[n, 0:512, :], q_buf[t], NT, preferred_element_type=F32)
        tiles[slot][...] = s
        return jnp.max(s, axis=0, keepdims=True)

    def fold(n, t, slot, block_max):
        old = mref[t, 0:1, :]
        new = jnp.maximum(old, block_max)
        mref[t, 0:1, :] = new
        p = jnp.exp2(tiles[slot][...] - new).astype(BF)
        vt = jnp.concatenate([kv[n, 512 + j * 128 : 640 + j * 128, :] for j in range(4)], axis=1)
        vt = jnp.concatenate([vt, ones], axis=0)
        acc[t] = acc[t] * jnp.exp2(old - new) + dot(vt, p)

    first = logits(0, 0, 0)

    def block_step(n, block_max):
        arrive(n + 1)
        for u in range(4):
            ahead = n if u < 3 else n + 1
            following = logits(ahead, (u + 1) % 4, (u + 1) % 2)
            fold(n, u, u % 2, block_max)
            block_max = following
        return block_max

    carry = lax.fori_loop(0, EARLY, block_step, first)

    def arrive_late(n, _):
        arrive(n)
        return 0

    lax.fori_loop(EARLY + 1, 32, arrive_late, 0)

    mine = z * 4 + x

    def ax_copy(t):
        dx = order(3 - t)
        back = order((4 - dx) % 4) if isinstance(dx, int) else order(lax.rem(4 - dx, 4))
        return remote(
            stage.at[t], att.at[mine], ax_send.at[t], ax_recv.at[3 - back], at(dx=dx)
        )

    def az_rows(t, dz, half=None):
        head = lax.rem(z + dz, 4) * 4 + lax.rem(x + order(3 - t), 4)
        if half is None:
            return att.at[head]
        return att.at[head, pl.ds(half * 256, 256), :]

    def az_copy(t, i):
        rows = (az_rows(t, 0), az_rows(t, 0), az_rows(t, 3, 0), az_rows(t, 1, 1))[i]
        return remote(
            rows, rows, az_send.at[t * 4 + i], az_recv.at[t * 4 + i], at(dz=(1, 3, 1, 3)[i])
        )

    def az_arrive(t, i):
        rows = (az_rows(t, 3), az_rows(t, 1), az_rows(t, 2, 0), az_rows(t, 2, 1))[i]
        remote(rows, rows, az_send.at[0], az_recv.at[t * 4 + i], at(dz=1)).wait_recv()

    def share(t):
        az_copy(t, 0).start()
        az_copy(t, 1).start()

    def relay(t):
        for i in (0, 1):
            az_arrive(t, i)
            az_copy(t, i + 2).start()

    def ax_arrive(t):
        head = z * 4 + lax.rem(x + order(3 - t), 4)
        remote(stage.at[0], att.at[head], ax_send.at[0], ax_recv.at[t], at(dx=1)).wait_recv()

    def tile_step(t, block_max):
        def group(i, block_max):
            base = EARLY + i * 4
            last = i == (32 - EARLY) // 4 - 1
            for u in range(4):
                if u < 3:
                    following = logits(base + u + 1, t, (u + 1) % 2)
                else:
                    following = logits(
                        jnp.where(last, EARLY, base + 4),
                        jnp.where(last, jnp.minimum(t + 1, 3), t),
                        0,
                    )
                fold(base + u, t, u % 2, block_max)
                block_max = following
            return block_max

        block_max = lax.fori_loop(0, (32 - EARLY) // 4, group, block_max)
        a = acc[t]
        block = (a[0:128] / a[128:129]).T.astype(BF)

        @pl.when(t < 3)
        def _():
            stage[t] = block
            ax_copy(t).start()

        @pl.when(t == 3)
        def _():
            att[mine] = block
            share(3)

        @pl.when(t > 0)
        def _():
            ax_arrive(t - 1)
            share(t - 1)

        @pl.when(t > 1)
        def _():
            relay(t - 2)

        return block_max

    lax.fori_loop(0, 4, tile_step, carry)

    def branch(dz):
        zs = lax.rem(z + dz, 4)
        heads = jnp.concatenate([att[zs * 4 + h] for h in range(4)], axis=1)
        return dot(heads, ow[zs])

    def ow_arrive(d):
        src = lax.rem(z + d, 4)
        remote(ow.at[src], ow.at[src], ow_send.at[0], ow_recv.at[d - 1], at(dz=1)).wait_recv()

    ow_own.wait()
    for d in (1, 2, 3):
        ow_arrive(d)
    result = emb[:, my_cols] + branch(0)
    relay(2)
    relay(3)
    result = result + branch(1) + branch(3)
    for t in range(4):
        az_arrive(t, 2)
        az_arrive(t, 3)
    out_ref[...] = (result + branch(2)).astype(BF)

    for i in range(4):
        pool_copy(i).wait_send()
    for d in (1, 2, 3):
        q_copy(d).wait_send()
        kvx_copy(d).wait_send()
        ow_copy(d).wait_send()
        ax_copy(d - 1).wait_send()

    def drain(n, _):
        for k in range(3):
            own_copy(n, k).wait_send()
        for i in range(4):
            az_copy(n, i).wait_send()
        hop_copy(9 + 2 * n - lax.div(n, 2)).wait_send()
        return 0

    lax.fori_loop(0, 4, drain, 0)

    def drain_fwd(i, _):
        fwd_copy(8 + i + 8 * lax.div(i, 8)).wait_send()
        return 0

    lax.fori_loop(0, 12, drain_fwd, 0)


def on_device(tokens, key_query, value_weight, proj_weight, norm_gain, qkv_weight, out_weight):
    dma = pltpu.SemaphoreType.DMA
    vm = pltpu.VMEM
    scratch = [
        vm((2, NV, CH, 1024), BF),
        vm((128, 1024), BF),
        vm((128, 1024), BF),
        vm((1024, 1024), BF),
        vm((1024, 2048), BF),
        vm((2, 1536, 128), BF),
        vm((1536, 128), F32),
        vm((2048, 1536), BF),
        vm((NV * CH, 128), BF),
        vm((4, CH, 1024), BF),
        vm((3, CH, 1024), BF),
        vm((4, CH, 128), F32),
        vm((3, CH, 128), F32),
        vm((ROWS, 1024), BF),
        vm((ROWS, 2048), F32),
        vm((ROWS, 2048), BF),
        vm((4, ROWS, 128), BF),
        vm((4, 2 * ROWS, 128), BF),
        vm((4, ROWS, 128), BF),
        vm((32, 2 * ROWS, 128), BF),
        vm((512, 512), F32),
        vm((512, 512), F32),
        vm((4, 144, 512), F32),
        vm((4, 8, 512), F32),
        vm((4, 512, 512), BF),
        vm((3, ROWS, 128), BF),
        vm((16, ROWS, 128), BF),
        dma((2,)), dma((2,)), dma((2,)), dma,
        dma((3,)), dma((3,)), dma((3,)), dma((3,)), dma((4,)), dma((4,)),
        dma((3,)), dma((3,)), dma((3,)), dma((12,)), dma((12,)), dma((4,)), dma((32,)),
        dma((3,)), dma((3,)), dma((3,)), dma((3,)), dma((16,)), dma((16,)),
    ]
    anywhere = pl.BlockSpec(memory_space=pl.ANY)
    vmem = pl.BlockSpec(memory_space=pltpu.VMEM)
    return pl.pallas_call(
        kernel,
        out_shape=jax.ShapeDtypeStruct((ROWS, 512), BF),
        in_specs=[anywhere, vmem, anywhere, anywhere, vmem, anywhere, anywhere],
        out_specs=vmem,
        scratch_shapes=scratch,
        compiler_params=pltpu.CompilerParams(
            collective_id=1, has_side_effects=True, vmem_limit_bytes=62 * 1024 * 1024
        ),
        name="block",
    )(
        tokens,
        key_query.T,
        value_weight,
        proj_weight,
        norm_gain.reshape(1, 2048),
        qkv_weight.reshape(2048 * 12, 128),
        out_weight.reshape(512, 2048),
    )


def solution(mesh):
    return jax.shard_map(
        on_device,
        mesh=mesh,
        in_specs=(
            P("var", "patch", None),
            P(),
            P(),
            P(),
            P(),
            P(None, None, "var", None),
            P("var", None, None),
        ),
        out_specs=P("patch", "var"),
        check_vma=False,
    )
```

```python
import functools

import jax
import jax.numpy as jnp
from jax import lax
from jax.experimental import pallas as pl
from jax.experimental.pallas import tpu as pltpu
from jax.sharding import PartitionSpec as P

MESH = pl.DeviceIdType.MESH
NT = (((1,), (1,)), ((), ()))
BF = jnp.bfloat16
F32 = jnp.float32

ROWS, NV, CH = 512, 12, 128
EARLY = 12
Q_SCALE = 128 ** (-0.5) * 1.4426950408889634


def order(e):
    if isinstance(e, int):
        return (0, 1, 3, 2)[e]
    return e + lax.div(e, 2) * (5 - 2 * e)


def dot(a, b):
    return jnp.dot(a, b, preferred_element_type=F32)


def kernel(
    tok_hbm, kq_ref, vw_hbm, proj_hbm, gain_ref, w2_hbm, ow_hbm,
    out_ref,
    tok, kqp, expand, vw, proj, wstage, wf, wq,
    wn, part_send, part_recv, stat_send, stat_recv, pooled,
    emb, normed, q4, kv4, q_buf, kv, s0, s1, p0, p1, acc, mref,
    ow, stage, att,
    sem_tok, sem_w, sem_w2, sem_ow_own,
    ps_send, ps_recv, st_send, st_recv, pool_send, pool_recv,
    q_send, q_recv, kvx_send, own_send, fwd_send, hop_send, kv_recv,
    ow_send, ow_recv, ax_send, ax_recv, az_send, az_recv,
):
    z = lax.axis_index("var")
    place = lax.axis_index("patch")
    x = lax.div(place, 8)
    y = lax.rem(lax.div(place, 2), 4)
    c = lax.rem(place, 2)

    def at(dx=0, dy=0, dz=0, dc=0):
        px = lax.rem(x + dx, 4)
        py = lax.rem(y + dy, 4)
        pc = lax.rem(c + dc, 2)
        return (lax.rem(z + dz, 4), (px * 4 + py) * 2 + pc)

    def remote(src, dst, send, recv, device):
        return pltpu.make_async_remote_copy(
            src_ref=src, dst_ref=dst, send_sem=send, recv_sem=recv,
            device_id=device, device_id_type=MESH,
        )

    def tok_copy(j, slot):
        base = pl.multiple_of(lax.rem(z + order(3 - j), 4) * CH, CH)
        return pltpu.make_async_copy(
            tok_hbm.at[:, pl.ds(base, CH), :], tok.at[slot], sem_tok.at[slot]
        )

    vw_copy = pltpu.make_async_copy(vw_hbm, vw, sem_w.at[0])
    proj_copy = pltpu.make_async_copy(proj_hbm, proj, sem_w.at[1])
    tok_copy(0, 0).start()
    vw_copy.start()
    tok_copy(1, 1).start()
    proj_copy.start()

    def w2_copy(i, slot):
        base = pl.multiple_of(i * 1536, 1536)
        return pltpu.make_async_copy(
            w2_hbm.at[pl.ds(base, 1536), :], wstage.at[slot], sem_w2.at[slot]
        )

    w2_copy(0, 0).start()
    w2_copy(1, 1).start()

    barrier = pltpu.get_barrier_semaphore()
    partners = [at(dx=d) for d in (1, 2, 3)] + [at(dy=d) for d in (1, 2, 3)]
    partners += [at(dz=d) for d in (1, 2, 3)] + [at(dc=1)]
    for device in partners:
        pl.semaphore_signal(barrier, inc=1, device_id=device, device_id_type=MESH)

    kqp[...] = jnp.zeros_like(kqp)
    kqp[0:16, :] = kq_ref[...]
    head_of = lax.broadcasted_iota(jnp.int32, (128, 1024), 0)
    lane = lax.broadcasted_iota(jnp.int32, (128, 1024), 1)
    expand[...] = jnp.where(lax.div(lane, 64) == head_of, 1.0, 0.0).astype(BF)

    vw_copy.wait()

    def part_copy(j):
        dz = order(3 - j)
        return remote(
            part_send.at[j], part_recv.at[3 - dz], ps_send.at[j], ps_recv.at[3 - dz], at(dz=dz)
        )

    def stat_copy(j):
        dz = order(3 - j)
        return remote(
            stat_send.at[j], stat_recv.at[3 - dz], st_send.at[j], st_recv.at[3 - dz], at(dz=dz)
        )

    def pool_chunk(j, _):
        slot = lax.rem(j, 2)
        tok_copy(j, slot).wait()
        scores = lax.dot_general(
            tok[slot].reshape(NV * CH, 1024), kqp[...], NT, preferred_element_type=F32
        ).reshape(NV, CH, 128)
        peak = jnp.max(scores, axis=0)
        weights = jnp.exp(scores - peak[None])
        totals = jnp.sum(weights, axis=0)
        first_lanes = lax.broadcasted_iota(jnp.int32, (CH, 128), 1) < 16
        stat_send[j] = jnp.where(first_lanes, peak, pltpu.roll(totals, 16, 1))
        wn[...] = weights.astype(BF).astype(F32).reshape(NV * CH, 128)

        upper = jnp.where(lax.broadcasted_iota(jnp.int32, (NV * CH, 128), 1) >= 64, 1, 0)
        values = dot(tok[slot].reshape(NV * CH, 1024), vw[...])
        wide = jnp.concatenate(
            [jnp.take_along_axis(wn[...], 2 * q + upper, axis=1) for q in range(8)], axis=1
        )
        part_send[j] = jnp.sum((values * wide).reshape(NV, CH, 1024), axis=0).astype(BF)

        @pl.when(j < 2)
        def _():
            tok_copy(j + 2, slot).start()

        @pl.when(j == 0)
        def _():
            pl.semaphore_wait(barrier, len(partners))

        @pl.when(j < 3)
        def _():
            part_copy(j).start()
            stat_copy(j).start()

        return 0

    lax.fori_loop(0, 4, pool_chunk, 0)

    for i in range(3):
        part_copy(i).wait_send()
        stat_copy(i).wait_send()
        remote(part_send.at[0], part_recv.at[i], ps_send.at[0], ps_recv.at[i], at(dz=1)).wait_recv()
        remote(stat_send.at[0], stat_recv.at[i], st_send.at[0], st_recv.at[i], at(dz=1)).wait_recv()
    peaks = [stat_send[3]] + [stat_recv[i] for i in range(3)]
    top = functools.reduce(jnp.maximum, peaks)
    factors = [jnp.exp(l - top) for l in peaks]
    inverse = 1.0 / sum(f * pltpu.roll(l, 112, 1) for f, l in zip(factors, peaks))
    real = lax.broadcasted_iota(jnp.int32, (CH, 128), 1) < 16
    total = jnp.zeros((CH, 1024), F32)
    for g in range(4):
        share = jnp.where(real, factors[g] * inverse, 0.0)
        high = share.astype(BF)
        low = (share - high.astype(F32)).astype(BF)
        wide = dot(high, expand[...]) + dot(low, expand[...])
        part = part_send[3] if g == 0 else part_recv[g - 1]
        total = total + wide * part.astype(F32)
    own_rows = pl.ds(pl.multiple_of(z * CH, CH), CH)
    pooled[own_rows, :] = total.astype(BF)

    def pool_rows(dz, half=None):
        base = lax.rem(z + dz, 4) * CH
        if half is None:
            return pooled.at[pl.ds(pl.multiple_of(base, CH), CH), :]
        return pooled.at[pl.ds(pl.multiple_of(base + half * (CH // 2), CH // 2), CH // 2), :]

    def pool_copy(i):
        rows = (pool_rows(0), pool_rows(0), pool_rows(3, 0), pool_rows(1, 1))[i]
        return remote(rows, rows, pool_send.at[i], pool_recv.at[i], at(dz=(1, 3, 1, 3)[i]))

    def pool_arrive(i):
        rows = (pool_rows(3), pool_rows(1), pool_rows(2, 0), pool_rows(2, 1))[i]
        remote(rows, rows, pool_send.at[0], pool_recv.at[i], at(dz=1)).wait_recv()

    pool_copy(0).start()
    pool_copy(1).start()

    def relayout(i, _):
        slot = lax.rem(i, 2)
        w2_copy(i, slot).wait()
        wf[...] = wstage[slot].astype(F32)
        rows = pl.ds(pl.multiple_of(i * 128, 128), 128)
        for n in range(12):
            to = n if n < 4 else 4 + 2 * (n % 4) + n // 8
            wq[rows, to * 128 : (to + 1) * 128] = wf[pl.ds(n, 128, stride=12), :].astype(BF)

        @pl.when(i < 14)
        def _():
            w2_copy(i + 2, slot).start()

        return 0

    lax.fori_loop(0, 11, relayout, 0)
    for i in (0, 1):
        pool_arrive(i)
        pool_copy(i + 2).start()
    lax.fori_loop(11, 16, relayout, 0)
    proj_copy.wait()
    for i in (2, 3):
        pool_arrive(i)

    def project(i, _):
        cs = pl.ds(pl.multiple_of(i * 512, 512), 512)
        emb[:, cs] = dot(pooled[...], proj[:, cs])
        return 0

    lax.fori_loop(0, 4, project, 0)

    def norm(i, _):
        rows = pl.ds(pl.multiple_of(i * 128, 128), 128)
        block = emb[rows, :]
        center = block - jnp.mean(block, axis=1, keepdims=True)
        variance = jnp.mean(center * center, axis=1, keepdims=True)
        normed[rows, :] = (center / jnp.sqrt(variance + 1e-05) * gain_ref[...]).astype(BF)
        return 0

    lax.fori_loop(0, 4, norm, 0)

    def q_copy(d):
        dst = order((4 - d) % 4)
        head = lax.rem(x + d, 4)
        return remote(
            q4.at[head], q_buf.at[3 - dst], q_send.at[d - 1], q_recv.at[dst - 1], at(dx=d)
        )

    def kvx_copy(d):
        dst = order((4 - d) % 4)
        head = lax.rem(x + d, 4)
        slot = own_slot(dst)
        return remote(kv4.at[head], kv.at[slot], kvx_send.at[d - 1], kv_recv.at[slot], at(dx=d))

    def own_slot(r):
        return (0, 6, 8, 10)[r] if isinstance(r, int) else jnp.where(r == 0, 0, 4 + 2 * r)

    def near_slot(r):
        return (2, 12, 16, 20)[r] if isinstance(r, int) else jnp.where(r == 0, 2, 8 + 4 * r)

    def own_copy(r, k):
        device = (at(dc=1), at(dy=1), at(dy=3))[k]
        slot = (own_slot(r) + 1, near_slot(r) + 1, near_slot(r))[k]
        return remote(
            kv.at[own_slot(r)], kv.at[slot], own_send.at[r * 3 + k], kv_recv.at[slot], device
        )

    def near_copy(r, k):
        slot = near_slot(r) + k
        return remote(
            kv.at[slot], kv.at[slot + 2], fwd_send.at[r * 2 + k], kv_recv.at[slot + 2], at(dc=1)
        )

    def far_copy(r):
        return remote(
            kv.at[24 + r], kv.at[28 + r], fwd_send.at[8 + r], kv_recv.at[28 + r], at(dc=1)
        )

    def hop_copy(r):
        up = 1 - lax.div(r, 2)
        return remote(
            kv.at[near_slot(r) + up], kv.at[24 + r], hop_send.at[r], kv_recv.at[24 + r],
            at(dy=3 - 2 * up),
        )

    queries = dot(normed[...], wq[:, 0:512]) * Q_SCALE
    for h in range(4):
        q4[h] = queries[:, h * 128 : (h + 1) * 128].astype(BF)
    for d in (2, 1, 3):
        q_copy(d).start()
    q_buf[3] = q4[x]

    def keys_values(head, write):
        cs = pl.ds(pl.multiple_of(512 + head * 256, 256), 256)
        both = dot(normed[...], wq[:, cs])
        write(slice(0, 512), both[:, 0:128].astype(BF))
        for j in range(4):
            tile = both[j * 128 : (j + 1) * 128, 128:256]
            write(slice(512 + j * 128, 640 + j * 128), tile.T.astype(BF))

    def write_own(rows, value):
        kv[0, rows, :] = value

    keys_values(x, write_own)
    for k in range(3):
        own_copy(0, k).start()
    for d in (1, 3, 2):
        head = lax.rem(x + d, 4)

        def write_other(rows, value, head=head):
            kv4[head, rows, :] = value

        keys_values(head, write_other)
        kvx_copy(d).start()

    my_cols = pl.ds(pl.multiple_of(z * 512, 512), 512)
    ow_own = pltpu.make_async_copy(ow_hbm.at[:, my_cols], ow.at[z], sem_ow_own)
    ow_own.start()

    def ow_copy(d):
        cols = pl.ds(pl.multiple_of(lax.rem(z + d, 4) * 512, 512), 512)
        return remote(
            ow_hbm.at[:, cols], ow.at[z], ow_send.at[d - 1], ow_recv.at[3 - d], at(dz=d)
        )

    for d in (1, 3, 2):
        ow_copy(d).start()

    def landed(slot):
        remote(
            kv.at[slot], kv.at[slot], own_send.at[0], kv_recv.at[slot], at(dc=1)
        ).wait_recv()

    def arrive(step, _):
        landed(2 * step)

        @pl.when(jnp.logical_and(step >= 3, step < 6))
        def _():
            for k in range(3):
                own_copy(step - 2, k).start()

        landed(2 * step + 1)
        late = jnp.logical_and(jnp.logical_and(step >= 6, step < 12), lax.rem(step, 2) == 0)

        @pl.when(jnp.logical_or(step == 1, late))
        def _():
            r = jnp.where(step == 1, 0, lax.div(step, 2) - 2)
            hop_copy(r).start()
            near_copy(r, 0).start()
            near_copy(r, 1).start()

        @pl.when(jnp.logical_or(step == 12, step == 13))
        def _():
            far_copy(2 * (step - 12)).start()
            far_copy(2 * (step - 12) + 1).start()

        return 0

    for r in range(3):
        remote(q_buf.at[3], q_buf.at[2 - r], q_send.at[0], q_recv.at[r], at(dx=1)).wait_recv()
    acc[...] = jnp.zeros_like(acc)
    mref[...] = jnp.full_like(mref, -1e30)
    ones = jnp.ones((16, 1024), BF)
    landed(1)

    def logits(step, t, slot):
        keys = jnp.concatenate([kv[2 * step, 0:512, :], kv[2 * step + 1, 0:512, :]], axis=0)
        s = lax.dot_general(keys, q_buf[t], NT, preferred_element_type=F32)
        (s0, s1)[slot][...] = s
        return jnp.max(s, axis=0, keepdims=True)

    def weigh(t, slot, block_max):
        old = mref[t, 0:1, :]
        new = jnp.maximum(old, block_max)
        mref[t, 0:1, :] = new
        (p0, p1)[slot][...] = jnp.exp2((s0, s1)[slot][...] - new).astype(BF)
        return jnp.exp2(old - new)

    def add(step, t, slot, rescale):
        pieces = [
            kv[2 * step + i, 512 + j * 128 : 640 + j * 128, :] for i in range(2) for j in range(4)
        ]
        vt = jnp.concatenate([jnp.concatenate(pieces, axis=1), ones], axis=0)
        acc[t] = acc[t] * rescale + dot(vt, (p0, p1)[slot][...])

    def turns(units, state):
        block_max, rescale = state
        for u in range(4):
            following = logits(*units[u + 2], u % 2)
            next_rescale = weigh(units[u + 1][1], (u + 1) % 2, block_max)
            add(*units[u], u % 2, rescale)
            block_max, rescale = following, next_rescale
        return block_max, rescale

    first = weigh(0, 0, logits(0, 0, 0))
    state = (logits(0, 1, 1), first)

    def by_step(step, state):
        last = step == EARLY - 1
        lax.fori_loop(step + 1, jnp.where(last, 16, step + 2), arrive, 0)
        units = [(step, 0), (step, 1), (step, 2), (step, 3), (step + 1, 0)]
        units.append((jnp.where(last, step + 2, step + 1), jnp.where(last, 0, 1)))
        return turns(units, state)

    state = lax.fori_loop(0, EARLY, by_step, state)

    mine = z * 4 + x

    def ax_copy(t):
        dx = order(3 - t)
        back = order((4 - dx) % 4) if isinstance(dx, int) else order(lax.rem(4 - dx, 4))
        return remote(
            stage.at[t], att.at[mine], ax_send.at[t], ax_recv.at[3 - back], at(dx=dx)
        )

    def az_rows(t, dz, half=None):
        head = lax.rem(z + dz, 4) * 4 + lax.rem(x + order(3 - t), 4)
        if half is None:
            return att.at[head]
        return att.at[head, pl.ds(half * 256, 256), :]

    def az_copy(t, i):
        rows = (az_rows(t, 0), az_rows(t, 0), az_rows(t, 3, 0), az_rows(t, 1, 1))[i]
        return remote(
            rows, rows, az_send.at[t * 4 + i], az_recv.at[t * 4 + i], at(dz=(1, 3, 1, 3)[i])
        )

    def az_arrive(t, i):
        rows = (az_rows(t, 3), az_rows(t, 1), az_rows(t, 2, 0), az_rows(t, 2, 1))[i]
        remote(rows, rows, az_send.at[0], az_recv.at[t * 4 + i], at(dz=1)).wait_recv()

    def share(t):
        az_copy(t, 0).start()
        az_copy(t, 1).start()

    def relay(t):
        for i in (0, 1):
            az_arrive(t, i)
            az_copy(t, i + 2).start()

    def ax_arrive(t):
        head = z * 4 + lax.rem(x + order(3 - t), 4)
        remote(stage.at[0], att.at[head], ax_send.at[0], ax_recv.at[t], at(dx=1)).wait_recv()

    def by_tile(t, state):
        after = jnp.minimum(t + 1, 3)
        units = [(EARLY + i, t) for i in range(4)] + [(EARLY, after), (EARLY + 1, after)]
        state = turns(units, state)
        a = acc[t]
        block = (a[0:128] / a[128:129]).T.astype(BF)

        @pl.when(t < 3)
        def _():
            stage[t] = block
            ax_copy(t).start()

        @pl.when(t == 3)
        def _():
            att[mine] = block
            share(3)

        @pl.when(t > 0)
        def _():
            ax_arrive(t - 1)
            share(t - 1)

        @pl.when(t > 1)
        def _():
            relay(t - 2)

        return state

    lax.fori_loop(0, 4, by_tile, state)

    def branch(dz):
        zs = lax.rem(z + dz, 4)
        heads = jnp.concatenate([att[zs * 4 + h] for h in range(4)], axis=1)
        return dot(heads, ow[zs])

    def ow_arrive(d):
        src = lax.rem(z + d, 4)
        remote(ow.at[src], ow.at[src], ow_send.at[0], ow_recv.at[d - 1], at(dz=1)).wait_recv()

    ow_own.wait()
    for d in (1, 2, 3):
        ow_arrive(d)
    result = emb[:, my_cols] + branch(0)
    relay(2)
    relay(3)
    result = result + branch(1) + branch(3)
    for t in range(4):
        az_arrive(t, 2)
        az_arrive(t, 3)
    out_ref[...] = (result + branch(2)).astype(BF)

    for i in range(4):
        pool_copy(i).wait_send()
    for d in (1, 2, 3):
        q_copy(d).wait_send()
        kvx_copy(d).wait_send()
        ow_copy(d).wait_send()
        ax_copy(d - 1).wait_send()

    def drain(n, _):
        for k in range(3):
            own_copy(n, k).wait_send()
        for i in range(4):
            az_copy(n, i).wait_send()
        hop_copy(n).wait_send()
        near_copy(n, 0).wait_send()
        near_copy(n, 1).wait_send()
        far_copy(n).wait_send()
        return 0

    lax.fori_loop(0, 4, drain, 0)


def on_device(tokens, key_query, value_weight, proj_weight, norm_gain, qkv_weight, out_weight):
    dma = pltpu.SemaphoreType.DMA
    vm = pltpu.VMEM
    scratch = [
        vm((2, NV, CH, 1024), BF),
        vm((128, 1024), BF),
        vm((128, 1024), BF),
        vm((1024, 1024), BF),
        vm((1024, 2048), BF),
        vm((2, 1536, 128), BF),
        vm((1536, 128), F32),
        vm((2048, 1536), BF),
        vm((NV * CH, 128), F32),
        vm((4, CH, 1024), BF),
        vm((3, CH, 1024), BF),
        vm((4, CH, 128), F32),
        vm((3, CH, 128), F32),
        vm((ROWS, 1024), BF),
        vm((ROWS, 2048), F32),
        vm((ROWS, 2048), BF),
        vm((4, ROWS, 128), BF),
        vm((4, 2 * ROWS, 128), BF),
        vm((4, ROWS, 128), BF),
        vm((32, 2 * ROWS, 128), BF),
        vm((1024, 512), F32),
        vm((1024, 512), F32),
        vm((1024, 512), BF),
        vm((1024, 512), BF),
        vm((4, 144, 512), F32),
        vm((4, 8, 512), F32),
        vm((4, 512, 512), BF),
        vm((3, ROWS, 128), BF),
        vm((16, ROWS, 128), BF),
        dma((2,)), dma((2,)), dma((2,)), dma,
        dma((3,)), dma((3,)), dma((3,)), dma((3,)), dma((4,)), dma((4,)),
        dma((3,)), dma((3,)), dma((3,)), dma((12,)), dma((12,)), dma((4,)), dma((32,)),
        dma((3,)), dma((3,)), dma((3,)), dma((3,)), dma((16,)), dma((16,)),
    ]
    anywhere = pl.BlockSpec(memory_space=pl.ANY)
    vmem = pl.BlockSpec(memory_space=pltpu.VMEM)
    return pl.pallas_call(
        kernel,
        out_shape=jax.ShapeDtypeStruct((ROWS, 512), BF),
        in_specs=[anywhere, vmem, anywhere, anywhere, vmem, anywhere, anywhere],
        out_specs=vmem,
        scratch_shapes=scratch,
        compiler_params=pltpu.CompilerParams(
            collective_id=1, has_side_effects=True, vmem_limit_bytes=62 * 1024 * 1024
        ),
        name="block",
    )(
        tokens,
        key_query.T,
        value_weight,
        proj_weight,
        norm_gain.reshape(1, 2048),
        qkv_weight.reshape(2048 * 12, 128),
        out_weight.reshape(512, 2048),
    )


def solution(mesh):
    return jax.shard_map(
        on_device,
        mesh=mesh,
        in_specs=(
            P("var", "patch", None),
            P(),
            P(),
            P(),
            P(),
            P(None, None, "var", None),
            P("var", None, None),
        ),
        out_specs=P("patch", "var"),
        check_vma=False,
    )
```

```python
import functools

import jax
import jax.numpy as jnp
from jax import lax
from jax.experimental import pallas as pl
from jax.experimental.pallas import tpu as pltpu
from jax.sharding import PartitionSpec as P

MESH = pl.DeviceIdType.MESH
NT = (((1,), (1,)), ((), ()))
BF = jnp.bfloat16
F32 = jnp.float32

ROWS, NV, CH = 512, 12, 128
Q_SCALE = 128 ** (-0.5) * 1.4426950408889634


def order(e):
    if isinstance(e, int):
        return (0, 1, 3, 2)[e]
    return e + lax.div(e, 2) * (5 - 2 * e)


def dot(a, b):
    return jnp.dot(a, b, preferred_element_type=F32)


def kernel(
    tok_hbm, kq_ref, vw_hbm, proj_hbm, gain_ref, w2_hbm, ow_hbm,
    out_ref,
    tok, kqp, expand, vw, proj, wstage, wf, wq,
    wn, part_send, part_recv, stat_send, stat_recv, pooled,
    emb, normed, q4, kv4, q_buf, kv, s0, s1, p0, p1, acc, mref,
    res_send, res_recv, scale_send, scale_recv,
    ow, stage, att,
    sem_tok, sem_w, sem_w2, sem_ow_own,
    ps_send, ps_recv, st_send, st_recv, pool_send, pool_recv,
    q_send, q_recv, kvx_send, own_send, fwd_send, kv_recv,
    mate_send, mate_recv, rs_send, rs_recv, ss_send, ss_recv,
    ow_send, ow_recv, ax_send, ax_recv, az_send, az_recv,
):
    z = lax.axis_index("var")
    place = lax.axis_index("patch")
    x = lax.div(place, 8)
    y = lax.rem(lax.div(place, 2), 4)
    c = lax.rem(place, 2)

    def at(dx=0, dy=0, dz=0, dc=0):
        px = lax.rem(x + dx, 4)
        py = lax.rem(y + dy, 4)
        pc = lax.rem(c + dc, 2)
        return (lax.rem(z + dz, 4), (px * 4 + py) * 2 + pc)

    def remote(src, dst, send, recv, device):
        return pltpu.make_async_remote_copy(
            src_ref=src, dst_ref=dst, send_sem=send, recv_sem=recv,
            device_id=device, device_id_type=MESH,
        )

    def tok_copy(j, slot):
        base = pl.multiple_of(lax.rem(z + order(3 - j), 4) * CH, CH)
        return pltpu.make_async_copy(
            tok_hbm.at[:, pl.ds(base, CH), :], tok.at[slot], sem_tok.at[slot]
        )

    vw_copy = pltpu.make_async_copy(vw_hbm, vw, sem_w.at[0])
    proj_copy = pltpu.make_async_copy(proj_hbm, proj, sem_w.at[1])
    tok_copy(0, 0).start()
    vw_copy.start()
    tok_copy(1, 1).start()
    proj_copy.start()

    def w2_copy(i, slot):
        base = pl.multiple_of(i * 1536, 1536)
        return pltpu.make_async_copy(
            w2_hbm.at[pl.ds(base, 1536), :], wstage.at[slot], sem_w2.at[slot]
        )

    w2_copy(0, 0).start()
    w2_copy(1, 1).start()

    barrier = pltpu.get_barrier_semaphore()
    partners = [at(dx=d) for d in (1, 2, 3)] + [at(dy=d) for d in (1, 2, 3)]
    partners += [at(dz=d) for d in (1, 2, 3)] + [at(dc=1)]
    for device in partners:
        pl.semaphore_signal(barrier, inc=1, device_id=device, device_id_type=MESH)

    kqp[...] = jnp.zeros_like(kqp)
    kqp[0:16, :] = kq_ref[...]
    head_of = lax.broadcasted_iota(jnp.int32, (128, 1024), 0)
    lane = lax.broadcasted_iota(jnp.int32, (128, 1024), 1)
    expand[...] = jnp.where(lax.div(lane, 64) == head_of, 1.0, 0.0).astype(BF)

    vw_copy.wait()

    def part_copy(j):
        dz = order(3 - j)
        return remote(
            part_send.at[j], part_recv.at[3 - dz], ps_send.at[j], ps_recv.at[3 - dz], at(dz=dz)
        )

    def stat_copy(j):
        dz = order(3 - j)
        return remote(
            stat_send.at[j], stat_recv.at[3 - dz], st_send.at[j], st_recv.at[3 - dz], at(dz=dz)
        )

    def pool_chunk(j, _):
        slot = lax.rem(j, 2)
        tok_copy(j, slot).wait()
        scores = lax.dot_general(
            tok[slot].reshape(NV * CH, 1024), kqp[...], NT, preferred_element_type=F32
        ).reshape(NV, CH, 128)
        peak = jnp.max(scores, axis=0)
        weights = jnp.exp(scores - peak[None])
        totals = jnp.sum(weights, axis=0)
        first_lanes = lax.broadcasted_iota(jnp.int32, (CH, 128), 1) < 16
        stat_send[j] = jnp.where(first_lanes, peak, pltpu.roll(totals, 16, 1))
        wn[...] = weights.astype(BF).astype(F32).reshape(NV * CH, 128)

        upper = jnp.where(lax.broadcasted_iota(jnp.int32, (NV * CH, 128), 1) >= 64, 1, 0)
        values = dot(tok[slot].reshape(NV * CH, 1024), vw[...])
        wide = jnp.concatenate(
            [jnp.take_along_axis(wn[...], 2 * q + upper, axis=1) for q in range(8)], axis=1
        )
        part_send[j] = jnp.sum((values * wide).reshape(NV, CH, 1024), axis=0).astype(BF)

        @pl.when(j < 2)
        def _():
            tok_copy(j + 2, slot).start()

        @pl.when(j == 0)
        def _():
            pl.semaphore_wait(barrier, len(partners))

        @pl.when(j < 3)
        def _():
            part_copy(j).start()
            stat_copy(j).start()

        return 0

    lax.fori_loop(0, 4, pool_chunk, 0)

    for i in range(3):
        part_copy(i).wait_send()
        stat_copy(i).wait_send()
        remote(part_send.at[0], part_recv.at[i], ps_send.at[0], ps_recv.at[i], at(dz=1)).wait_recv()
        remote(stat_send.at[0], stat_recv.at[i], st_send.at[0], st_recv.at[i], at(dz=1)).wait_recv()
    peaks = [stat_send[3]] + [stat_recv[i] for i in range(3)]
    top = functools.reduce(jnp.maximum, peaks)
    factors = [jnp.exp(l - top) for l in peaks]
    inverse = 1.0 / sum(f * pltpu.roll(l, 112, 1) for f, l in zip(factors, peaks))
    real = lax.broadcasted_iota(jnp.int32, (CH, 128), 1) < 16
    total = jnp.zeros((CH, 1024), F32)
    for g in range(4):
        share = jnp.where(real, factors[g] * inverse, 0.0)
        high = share.astype(BF)
        low = (share - high.astype(F32)).astype(BF)
        wide = dot(high, expand[...]) + dot(low, expand[...])
        part = part_send[3] if g == 0 else part_recv[g - 1]
        total = total + wide * part.astype(F32)
    own_rows = pl.ds(pl.multiple_of(z * CH, CH), CH)
    pooled[own_rows, :] = total.astype(BF)

    def pool_rows(dz, half=None):
        base = lax.rem(z + dz, 4) * CH
        if half is None:
            return pooled.at[pl.ds(pl.multiple_of(base, CH), CH), :]
        return pooled.at[pl.ds(pl.multiple_of(base + half * (CH // 2), CH // 2), CH // 2), :]

    def pool_copy(i):
        rows = (pool_rows(0), pool_rows(0), pool_rows(3, 0), pool_rows(1, 1))[i]
        return remote(rows, rows, pool_send.at[i], pool_recv.at[i], at(dz=(1, 3, 1, 3)[i]))

    def pool_arrive(i):
        rows = (pool_rows(3), pool_rows(1), pool_rows(2, 0), pool_rows(2, 1))[i]
        remote(rows, rows, pool_send.at[0], pool_recv.at[i], at(dz=1)).wait_recv()

    pool_copy(0).start()
    pool_copy(1).start()

    def relayout(i, _):
        slot = lax.rem(i, 2)
        w2_copy(i, slot).wait()
        wf[...] = wstage[slot].astype(F32)
        rows = pl.ds(pl.multiple_of(i * 128, 128), 128)
        for n in range(12):
            to = n if n < 4 else 4 + 2 * (n % 4) + n // 8
            wq[rows, to * 128 : (to + 1) * 128] = wf[pl.ds(n, 128, stride=12), :].astype(BF)

        @pl.when(i < 14)
        def _():
            w2_copy(i + 2, slot).start()

        return 0

    lax.fori_loop(0, 11, relayout, 0)
    for i in (0, 1):
        pool_arrive(i)
        pool_copy(i + 2).start()
    lax.fori_loop(11, 16, relayout, 0)
    proj_copy.wait()
    for i in (2, 3):
        pool_arrive(i)

    def project(i, _):
        cs = pl.ds(pl.multiple_of(i * 512, 512), 512)
        emb[:, cs] = dot(pooled[...], proj[:, cs])
        return 0

    lax.fori_loop(0, 4, project, 0)

    def norm(i, _):
        rows = pl.ds(pl.multiple_of(i * 128, 128), 128)
        block = emb[rows, :]
        center = block - jnp.mean(block, axis=1, keepdims=True)
        variance = jnp.mean(center * center, axis=1, keepdims=True)
        normed[rows, :] = (center / jnp.sqrt(variance + 1e-05) * gain_ref[...]).astype(BF)
        return 0

    lax.fori_loop(0, 4, norm, 0)

    def q_copy(d):
        dst = order((4 - d) % 4)
        head = lax.rem(x + d, 4)
        return remote(
            q4.at[head], q_buf.at[3 - dst], q_send.at[d - 1], q_recv.at[dst - 1], at(dx=d)
        )

    def kvx_copy(d):
        dst = order((4 - d) % 4)
        head = lax.rem(x + d, 4)
        slot = own_slot(dst)
        return remote(kv4.at[head], kv.at[slot], kvx_send.at[d - 1], kv_recv.at[slot], at(dx=d))

    odd = lax.rem(y, 2)
    partner = at(dy=1 + 2 * odd)
    mate = at(dy=3 - 2 * odd)

    def own_slot(r):
        return (0, 4, 6, 8)[r] if isinstance(r, int) else jnp.where(r == 0, 0, 2 + 2 * r)

    def pair_slot(r):
        return (2, 10, 12, 14)[r] if isinstance(r, int) else jnp.where(r == 0, 2, 8 + 2 * r)

    def own_copy(r, k):
        slot = (own_slot(r) + 1, pair_slot(r))[k]
        return remote(
            kv.at[own_slot(r)], kv.at[slot], own_send.at[r * 2 + k], kv_recv.at[slot],
            (at(dc=1), partner)[k],
        )

    def pair_copy(r):
        slot = pair_slot(r)
        return remote(
            kv.at[slot], kv.at[slot + 1], fwd_send.at[r], kv_recv.at[slot + 1], at(dc=1)
        )

    def mate_copy(r):
        return remote(
            q_buf.at[3 - r], q_buf.at[4 + r], mate_send.at[r], mate_recv.at[r], mate
        )

    def keys_values(head, write):
        cs = pl.ds(pl.multiple_of(512 + head * 256, 256), 256)
        both = dot(normed[...], wq[:, cs])
        write(slice(0, 512), both[:, 0:128].astype(BF))
        for j in range(4):
            tile = both[j * 128 : (j + 1) * 128, 128:256]
            write(slice(512 + j * 128, 640 + j * 128), tile.T.astype(BF))

    def write_own(rows, value):
        kv[0, rows, :] = value

    keys_values(x, write_own)
    own_copy(0, 0).start()
    own_copy(0, 1).start()
    queries = dot(normed[...], wq[:, 0:512]) * Q_SCALE
    for h in range(4):
        q4[h] = queries[:, h * 128 : (h + 1) * 128].astype(BF)
    for d in (1, 3, 2):
        q_copy(d).start()
    q_buf[3] = q4[x]
    mate_copy(0).start()
    for d in (1, 3, 2):
        head = lax.rem(x + d, 4)

        def write_other(rows, value, head=head):
            kv4[head, rows, :] = value

        keys_values(head, write_other)
        kvx_copy(d).start()

    my_cols = pl.ds(pl.multiple_of(z * 512, 512), 512)
    ow_own = pltpu.make_async_copy(ow_hbm.at[:, my_cols], ow.at[z], sem_ow_own)
    ow_own.start()

    def ow_copy(d):
        cols = pl.ds(pl.multiple_of(lax.rem(z + d, 4) * 512, 512), 512)
        return remote(
            ow_hbm.at[:, cols], ow.at[z], ow_send.at[d - 1], ow_recv.at[3 - d], at(dz=d)
        )

    for d in (1, 3, 2):
        ow_copy(d).start()

    def landed(slot):
        remote(
            kv.at[slot], kv.at[slot], own_send.at[0], kv_recv.at[slot], at(dc=1)
        ).wait_recv()

    def arrive(step):
        landed(2 * step)
        own = jnp.logical_and(step >= 2, step < 5)

        @pl.when(own)
        def _():
            own_copy(step - 1, 0).start()
            own_copy(step - 1, 1).start()

        @pl.when(jnp.logical_not(own))
        def _():
            pair_copy(jnp.where(step == 1, 0, step - 4)).start()

        landed(2 * step + 1)

    for r in (1, 2, 3):
        remote(
            q_buf.at[3], q_buf.at[3 - r], q_send.at[0], q_recv.at[r - 1], at(dx=1)
        ).wait_recv()
        mate_copy(r).start()

    def mate_arrive(r):
        remote(
            q_buf.at[0], q_buf.at[4 + r], mate_send.at[0], mate_recv.at[r], mate
        ).wait_recv()

    acc[...] = jnp.zeros_like(acc)
    mref[...] = jnp.full_like(mref, -1e30)
    ones = jnp.ones((16, 1024), BF)
    landed(1)

    def logits(step, t, slot):
        keys = jnp.concatenate([kv[2 * step, 0:512, :], kv[2 * step + 1, 0:512, :]], axis=0)
        s = lax.dot_general(keys, q_buf[t], NT, preferred_element_type=F32)
        (s0, s1)[slot][...] = s
        return jnp.max(s, axis=0, keepdims=True)

    def weigh(t, slot, block_max):
        old = mref[t, 0:1, :]
        new = jnp.maximum(old, block_max)
        mref[t, 0:1, :] = new
        (p0, p1)[slot][...] = jnp.exp2((s0, s1)[slot][...] - new).astype(BF)
        return jnp.exp2(old - new)

    def add(step, t, slot, rescale):
        pieces = [
            kv[2 * step + i, 512 + j * 128 : 640 + j * 128, :] for i in range(2) for j in range(4)
        ]
        vt = jnp.concatenate([jnp.concatenate(pieces, axis=1), ones], axis=0)
        acc[t] = acc[t] * rescale + dot(vt, (p0, p1)[slot][...])

    def turns(units, state):
        block_max, rescale = state
        for u in range(4):
            following = logits(*units[u + 2], u % 2)
            next_rescale = weigh(units[u + 1][1], (u + 1) % 2, block_max)
            add(*units[u], u % 2, rescale)
            block_max, rescale = following, next_rescale
        return block_max, rescale

    first = weigh(0, 0, logits(0, 0, 0))
    state = (logits(0, 1, 1), first)

    def place_of(k):
        step = jnp.where(k < 4, lax.rem(k, 2), lax.div(k, 2))
        group = jnp.where(k < 4, lax.div(k, 2), lax.rem(k, 2))
        return step, 4 * group

    def by_step(k, state):
        @pl.when(k == 0)
        def _():
            arrive(1)

        @pl.when(jnp.logical_or(k == 1, k == 2))
        def _():
            arrive(k + 1)
            mate_arrive(2 * k - 2)
            mate_arrive(2 * k - 1)

        @pl.when(k >= 4)
        def _():
            arrive(k)

        step, tile = place_of(k)
        next_step, next_tile = place_of(k + 1)
        last = k == 7
        units = [(step, tile + u) for u in range(4)]
        units.append((next_step, jnp.where(last, 7, next_tile)))
        units.append((jnp.where(last, 5, next_step), jnp.where(last, 7, next_tile + 1)))
        return turns(units, state)

    state = lax.fori_loop(0, 8, by_step, state)

    mine = z * 4 + x

    def ax_copy(t):
        dx = order(3 - t)
        back = order((4 - dx) % 4) if isinstance(dx, int) else order(lax.rem(4 - dx, 4))
        return remote(
            stage.at[t], att.at[mine], ax_send.at[t], ax_recv.at[3 - back], at(dx=dx)
        )

    def az_rows(t, dz, half=None):
        head = lax.rem(z + dz, 4) * 4 + lax.rem(x + order(3 - t), 4)
        if half is None:
            return att.at[head]
        return att.at[head, pl.ds(half * 256, 256), :]

    def az_copy(t, i):
        rows = (az_rows(t, 0), az_rows(t, 0), az_rows(t, 3, 0), az_rows(t, 1, 1))[i]
        return remote(
            rows, rows, az_send.at[t * 4 + i], az_recv.at[t * 4 + i], at(dz=(1, 3, 1, 3)[i])
        )

    def az_arrive(t, i):
        rows = (az_rows(t, 3), az_rows(t, 1), az_rows(t, 2, 0), az_rows(t, 2, 1))[i]
        remote(rows, rows, az_send.at[0], az_recv.at[t * 4 + i], at(dz=1)).wait_recv()

    def share(t):
        az_copy(t, 0).start()
        az_copy(t, 1).start()

    def relay(t):
        for i in (0, 1):
            az_arrive(t, i)
            az_copy(t, i + 2).start()

    def ax_arrive(t):
        head = z * 4 + lax.rem(x + order(3 - t), 4)
        remote(stage.at[0], att.at[head], ax_send.at[0], ax_recv.at[t], at(dx=1)).wait_recv()

    def result_copy(r):
        return remote(
            res_send.at[r], res_recv.at[r], rs_send.at[r], rs_recv.at[r], mate
        )

    def scale_copy(r):
        return remote(
            scale_send.at[r], scale_recv.at[r], ss_send.at[r], ss_recv.at[r], mate
        )

    def tile_of(i):
        return jnp.where(i < 4, 7 - i, i - 4)

    def by_tile(i, state):
        tile = tile_of(i)
        after = tile_of(jnp.minimum(i + 1, 7))
        units = [(4 + j, tile) for j in range(4)] + [(4, after), (5, after)]
        state = turns(units, state)

        @pl.when(i < 4)
        def _():
            r = 3 - i
            total = acc[tile, 128:129, :]
            res_send[r] = (acc[tile, 0:128, :] / total).astype(BF)
            scale_send[r, 0:1, :] = mref[tile, 0:1, :]
            scale_send[r, 1:2, :] = total
            result_copy(r).start()
            scale_copy(r).start()

        @pl.when(i >= 4)
        def _():
            t = i - 4
            r = 3 - t
            remote(
                res_send.at[0], res_recv.at[r], rs_send.at[0], rs_recv.at[r], mate
            ).wait_recv()
            remote(
                scale_send.at[0], scale_recv.at[r], ss_send.at[0], ss_recv.at[r], mate
            ).wait_recv()
            here, there = mref[tile, 0:1, :], scale_recv[r, 0:1, :]
            high = jnp.maximum(here, there)
            here = jnp.exp2(here - high)
            there = jnp.exp2(there - high) * scale_recv[r, 1:2, :]
            inverse = 1.0 / (here * acc[tile, 128:129, :] + there)
            both = acc[tile, 0:128, :] * (here * inverse)
            both = both + res_recv[r].astype(F32) * (there * inverse)
            block = both.T.astype(BF)

            @pl.when(t < 3)
            def _():
                stage[t] = block
                ax_copy(t).start()

            @pl.when(t == 3)
            def _():
                att[mine] = block
                share(3)

            @pl.when(t > 0)
            def _():
                ax_arrive(t - 1)
                share(t - 1)

            @pl.when(t > 1)
            def _():
                relay(t - 2)

        return state

    lax.fori_loop(0, 8, by_tile, state)

    def branch(dz):
        zs = lax.rem(z + dz, 4)
        heads = jnp.concatenate([att[zs * 4 + h] for h in range(4)], axis=1)
        return dot(heads, ow[zs])

    def ow_arrive(d):
        src = lax.rem(z + d, 4)
        remote(ow.at[src], ow.at[src], ow_send.at[0], ow_recv.at[d - 1], at(dz=1)).wait_recv()

    ow_own.wait()
    for d in (1, 2, 3):
        ow_arrive(d)
    result = emb[:, my_cols] + branch(0)
    relay(2)
    relay(3)
    result = result + branch(1) + branch(3)
    for t in range(4):
        az_arrive(t, 2)
        az_arrive(t, 3)
    out_ref[...] = (result + branch(2)).astype(BF)

    for i in range(4):
        pool_copy(i).wait_send()
    for d in (1, 2, 3):
        q_copy(d).wait_send()
        kvx_copy(d).wait_send()
        ow_copy(d).wait_send()
        ax_copy(d - 1).wait_send()

    def drain(n, _):
        for k in range(2):
            own_copy(n, k).wait_send()
        pair_copy(n).wait_send()
        mate_copy(n).wait_send()
        result_copy(n).wait_send()
        scale_copy(n).wait_send()
        for i in range(4):
            az_copy(n, i).wait_send()
        return 0

    lax.fori_loop(0, 4, drain, 0)


def on_device(tokens, key_query, value_weight, proj_weight, norm_gain, qkv_weight, out_weight):
    dma = pltpu.SemaphoreType.DMA
    vm = pltpu.VMEM
    scratch = [
        vm((2, NV, CH, 1024), BF),
        vm((128, 1024), BF),
        vm((128, 1024), BF),
        vm((1024, 1024), BF),
        vm((1024, 2048), BF),
        vm((2, 1536, 128), BF),
        vm((1536, 128), F32),
        vm((2048, 1536), BF),
        vm((NV * CH, 128), F32),
        vm((4, CH, 1024), BF),
        vm((3, CH, 1024), BF),
        vm((4, CH, 128), F32),
        vm((3, CH, 128), F32),
        vm((ROWS, 1024), BF),
        vm((ROWS, 2048), F32),
        vm((ROWS, 2048), BF),
        vm((4, ROWS, 128), BF),
        vm((4, 2 * ROWS, 128), BF),
        vm((8, ROWS, 128), BF),
        vm((16, 2 * ROWS, 128), BF),
        vm((1024, 512), F32),
        vm((1024, 512), F32),
        vm((1024, 512), BF),
        vm((1024, 512), BF),
        vm((8, 144, 512), F32),
        vm((8, 8, 512), F32),
        vm((4, 128, 512), BF),
        vm((4, 128, 512), BF),
        vm((4, 8, 512), F32),
        vm((4, 8, 512), F32),
        vm((4, 512, 512), BF),
        vm((3, ROWS, 128), BF),
        vm((16, ROWS, 128), BF),
        dma((2,)), dma((2,)), dma((2,)), dma,
        dma((3,)), dma((3,)), dma((3,)), dma((3,)), dma((4,)), dma((4,)),
        dma((3,)), dma((3,)), dma((3,)), dma((8,)), dma((4,)), dma((16,)),
        dma((4,)), dma((4,)), dma((4,)), dma((4,)), dma((4,)), dma((4,)),
        dma((3,)), dma((3,)), dma((3,)), dma((3,)), dma((16,)), dma((16,)),
    ]
    anywhere = pl.BlockSpec(memory_space=pl.ANY)
    vmem = pl.BlockSpec(memory_space=pltpu.VMEM)
    return pl.pallas_call(
        kernel,
        out_shape=jax.ShapeDtypeStruct((ROWS, 512), BF),
        in_specs=[anywhere, vmem, anywhere, anywhere, vmem, anywhere, anywhere],
        out_specs=vmem,
        scratch_shapes=scratch,
        compiler_params=pltpu.CompilerParams(
            collective_id=1, has_side_effects=True, vmem_limit_bytes=62 * 1024 * 1024
        ),
        name="block",
    )(
        tokens,
        key_query.T,
        value_weight,
        proj_weight,
        norm_gain.reshape(1, 2048),
        qkv_weight.reshape(2048 * 12, 128),
        out_weight.reshape(512, 2048),
    )


def solution(mesh):
    return jax.shard_map(
        on_device,
        mesh=mesh,
        in_specs=(
            P("var", "patch", None),
            P(),
            P(),
            P(),
            P(),
            P(None, None, "var", None),
            P("var", None, None),
        ),
        out_specs=P("patch", "var"),
        check_vma=False,
    )
```

```python
import functools

import jax
import jax.numpy as jnp
from jax import lax
from jax.experimental import pallas as pl
from jax.experimental.pallas import tpu as pltpu
from jax.sharding import PartitionSpec as P

MESH = pl.DeviceIdType.MESH
NT = (((1,), (1,)), ((), ()))
BF = jnp.bfloat16
F32 = jnp.float32

ROWS, NV, CH = 512, 12, 128
Q_SCALE = 128 ** (-0.5) * 1.4426950408889634


def order(e):
    if isinstance(e, int):
        return (0, 1, 3, 2)[e]
    return e + lax.div(e, 2) * (5 - 2 * e)


def dot(a, b):
    return jnp.dot(a, b, preferred_element_type=F32)


def kernel(
    tok_hbm, kq_ref, vw_hbm, proj_hbm, gain_ref, w2_hbm, ow_hbm,
    out_ref,
    tok, kqp, expand, vw, proj, wstage, wf, wq,
    wn, part_send, part_recv, stat_send, stat_recv, pooled,
    emb, normed, q4, kv4, q_buf, kv, s0, s1, p0, p1, acc, mref,
    res_send, res_recv, scale_send, scale_recv,
    ow, stage, att,
    sem_tok, sem_w, sem_w2, sem_ow_own,
    ps_send, ps_recv, st_send, st_recv, pool_send, pool_recv,
    q_send, q_recv, kvx_send, own_send, fwd_send, kv_recv,
    mate_send, mate_recv, rs_send, rs_recv, ss_send, ss_recv,
    ow_send, ow_recv, ax_send, ax_recv, az_send, az_recv,
):
    z = lax.axis_index("var")
    place = lax.axis_index("patch")
    x = lax.div(place, 8)
    y = lax.rem(lax.div(place, 2), 4)
    c = lax.rem(place, 2)

    def at(dx=0, dy=0, dz=0, dc=0):
        px = lax.rem(x + dx, 4)
        py = lax.rem(y + dy, 4)
        pc = lax.rem(c + dc, 2)
        return (lax.rem(z + dz, 4), (px * 4 + py) * 2 + pc)

    def remote(src, dst, send, recv, device):
        return pltpu.make_async_remote_copy(
            src_ref=src, dst_ref=dst, send_sem=send, recv_sem=recv,
            device_id=device, device_id_type=MESH,
        )

    def tok_copy(j, slot):
        base = pl.multiple_of(lax.rem(z + order(3 - j), 4) * CH, CH)
        return pltpu.make_async_copy(
            tok_hbm.at[:, pl.ds(base, CH), :], tok.at[slot], sem_tok.at[slot]
        )

    vw_copy = pltpu.make_async_copy(vw_hbm, vw, sem_w.at[0])
    proj_copy = pltpu.make_async_copy(proj_hbm, proj, sem_w.at[1])
    tok_copy(0, 0).start()
    vw_copy.start()
    tok_copy(1, 1).start()
    proj_copy.start()

    def w2_copy(i, slot):
        base = pl.multiple_of(i * 1536, 1536)
        return pltpu.make_async_copy(
            w2_hbm.at[pl.ds(base, 1536), :], wstage.at[slot], sem_w2.at[slot]
        )

    w2_copy(0, 0).start()
    w2_copy(1, 1).start()

    barrier = pltpu.get_barrier_semaphore()
    partners = [at(dx=d) for d in (1, 2, 3)] + [at(dy=d) for d in (1, 2, 3)]
    partners += [at(dz=d) for d in (1, 2, 3)] + [at(dc=1)]
    for device in partners:
        pl.semaphore_signal(barrier, inc=1, device_id=device, device_id_type=MESH)

    kqp[...] = jnp.zeros_like(kqp)
    kqp[0:16, :] = kq_ref[...]
    head_of = lax.broadcasted_iota(jnp.int32, (128, 1024), 0)
    lane = lax.broadcasted_iota(jnp.int32, (128, 1024), 1)
    expand[...] = jnp.where(lax.div(lane, 64) == head_of, 1.0, 0.0).astype(BF)

    vw_copy.wait()

    def part_copy(j):
        dz = order(3 - j)
        return remote(
            part_send.at[j], part_recv.at[3 - dz], ps_send.at[j], ps_recv.at[3 - dz], at(dz=dz)
        )

    def stat_copy(j):
        dz = order(3 - j)
        return remote(
            stat_send.at[j], stat_recv.at[3 - dz], st_send.at[j], st_recv.at[3 - dz], at(dz=dz)
        )

    def pool_chunk(j, _):
        slot = lax.rem(j, 2)
        tok_copy(j, slot).wait()
        scores = lax.dot_general(
            tok[slot].reshape(NV * CH, 1024), kqp[...], NT, preferred_element_type=F32
        ).reshape(NV, CH, 128)
        peak = jnp.max(scores, axis=0)
        weights = jnp.exp(scores - peak[None])
        totals = jnp.sum(weights, axis=0)
        first_lanes = lax.broadcasted_iota(jnp.int32, (CH, 128), 1) < 16
        stat_send[j] = jnp.where(first_lanes, peak, pltpu.roll(totals, 16, 1))
        wn[...] = weights.astype(BF).astype(F32).reshape(NV * CH, 128)

        upper = jnp.where(lax.broadcasted_iota(jnp.int32, (NV * CH, 128), 1) >= 64, 1, 0)
        values = dot(tok[slot].reshape(NV * CH, 1024), vw[...])
        wide = jnp.concatenate(
            [jnp.take_along_axis(wn[...], 2 * q + upper, axis=1) for q in range(8)], axis=1
        )
        part_send[j] = jnp.sum((values * wide).reshape(NV, CH, 1024), axis=0).astype(BF)

        @pl.when(j < 2)
        def _():
            tok_copy(j + 2, slot).start()

        @pl.when(j == 0)
        def _():
            pl.semaphore_wait(barrier, len(partners))

        @pl.when(j < 3)
        def _():
            part_copy(j).start()
            stat_copy(j).start()

        return 0

    lax.fori_loop(0, 4, pool_chunk, 0)

    for i in range(3):
        part_copy(i).wait_send()
        stat_copy(i).wait_send()
        remote(part_send.at[0], part_recv.at[i], ps_send.at[0], ps_recv.at[i], at(dz=1)).wait_recv()
        remote(stat_send.at[0], stat_recv.at[i], st_send.at[0], st_recv.at[i], at(dz=1)).wait_recv()
    peaks = [stat_send[3]] + [stat_recv[i] for i in range(3)]
    top = functools.reduce(jnp.maximum, peaks)
    factors = [jnp.exp(l - top) for l in peaks]
    inverse = 1.0 / sum(f * pltpu.roll(l, 112, 1) for f, l in zip(factors, peaks))
    real = lax.broadcasted_iota(jnp.int32, (CH, 128), 1) < 16
    total = jnp.zeros((CH, 1024), F32)
    for g in range(4):
        share = jnp.where(real, factors[g] * inverse, 0.0)
        high = share.astype(BF)
        low = (share - high.astype(F32)).astype(BF)
        wide = dot(high, expand[...]) + dot(low, expand[...])
        part = part_send[3] if g == 0 else part_recv[g - 1]
        total = total + wide * part.astype(F32)
    own_rows = pl.ds(pl.multiple_of(z * CH, CH), CH)
    pooled[own_rows, :] = total.astype(BF)

    def pool_rows(dz, half=None):
        base = lax.rem(z + dz, 4) * CH
        if half is None:
            return pooled.at[pl.ds(pl.multiple_of(base, CH), CH), :]
        return pooled.at[pl.ds(pl.multiple_of(base + half * (CH // 2), CH // 2), CH // 2), :]

    def pool_copy(i):
        rows = (pool_rows(0), pool_rows(0), pool_rows(3, 0), pool_rows(1, 1))[i]
        return remote(rows, rows, pool_send.at[i], pool_recv.at[i], at(dz=(1, 3, 1, 3)[i]))

    def pool_arrive(i):
        rows = (pool_rows(3), pool_rows(1), pool_rows(2, 0), pool_rows(2, 1))[i]
        remote(rows, rows, pool_send.at[0], pool_recv.at[i], at(dz=1)).wait_recv()

    pool_copy(0).start()
    pool_copy(1).start()

    def relayout(i, _):
        slot = lax.rem(i, 2)
        w2_copy(i, slot).wait()
        wf[...] = wstage[slot].astype(F32)
        rows = pl.ds(pl.multiple_of(i * 128, 128), 128)
        for n in range(12):
            to = n if n < 4 else 4 + 2 * (n % 4) + n // 8
            wq[rows, to * 128 : (to + 1) * 128] = wf[pl.ds(n, 128, stride=12), :].astype(BF)

        @pl.when(i < 14)
        def _():
            w2_copy(i + 2, slot).start()

        return 0

    lax.fori_loop(0, 11, relayout, 0)
    for i in (0, 1):
        pool_arrive(i)
        pool_copy(i + 2).start()
    lax.fori_loop(11, 16, relayout, 0)
    proj_copy.wait()
    for i in (2, 3):
        pool_arrive(i)

    def project(i, _):
        cs = pl.ds(pl.multiple_of(i * 512, 512), 512)
        emb[:, cs] = dot(pooled[...], proj[:, cs])
        return 0

    lax.fori_loop(0, 4, project, 0)

    def norm(i, _):
        rows = pl.ds(pl.multiple_of(i * 128, 128), 128)
        block = emb[rows, :]
        center = block - jnp.mean(block, axis=1, keepdims=True)
        variance = jnp.mean(center * center, axis=1, keepdims=True)
        normed[rows, :] = (center / jnp.sqrt(variance + 1e-05) * gain_ref[...]).astype(BF)
        return 0

    lax.fori_loop(0, 4, norm, 0)

    def q_copy(d):
        dst = order((4 - d) % 4)
        head = lax.rem(x + d, 4)
        return remote(
            q4.at[head], q_buf.at[3 - dst], q_send.at[d - 1], q_recv.at[dst - 1], at(dx=d)
        )

    def kvx_copy(d):
        dst = order((4 - d) % 4)
        head = lax.rem(x + d, 4)
        slot = own_slot(dst)
        return remote(kv4.at[head], kv.at[slot], kvx_send.at[d - 1], kv_recv.at[slot], at(dx=d))

    odd = lax.rem(y, 2)
    partner = at(dy=1 + 2 * odd)
    mate = at(dy=3 - 2 * odd)

    def own_slot(r):
        return (0, 4, 6, 8)[r] if isinstance(r, int) else jnp.where(r == 0, 0, 2 + 2 * r)

    def pair_slot(r):
        return (2, 10, 12, 14)[r] if isinstance(r, int) else jnp.where(r == 0, 2, 8 + 2 * r)

    def own_copy(r, k):
        slot = (own_slot(r) + 1, pair_slot(r))[k]
        return remote(
            kv.at[own_slot(r)], kv.at[slot], own_send.at[r * 2 + k], kv_recv.at[slot],
            (at(dc=1), partner)[k],
        )

    def pair_copy(r):
        slot = pair_slot(r)
        return remote(
            kv.at[slot], kv.at[slot + 1], fwd_send.at[r], kv_recv.at[slot + 1], at(dc=1)
        )

    def mate_copy(r):
        return remote(
            q_buf.at[3 - r], q_buf.at[4 + r], mate_send.at[r], mate_recv.at[r], mate
        )

    def keys_values(head, write):
        cs = pl.ds(pl.multiple_of(512 + head * 256, 256), 256)
        both = dot(normed[...], wq[:, cs])
        write(slice(0, 512), both[:, 0:128].astype(BF))
        for j in range(4):
            tile = both[j * 128 : (j + 1) * 128, 128:256]
            write(slice(512 + j * 128, 640 + j * 128), tile.T.astype(BF))

    def write_own(rows, value):
        kv[0, rows, :] = value

    keys_values(x, write_own)
    own_copy(0, 0).start()
    own_copy(0, 1).start()
    queries = dot(normed[...], wq[:, 0:512]) * Q_SCALE
    for h in range(4):
        q4[h] = queries[:, h * 128 : (h + 1) * 128].astype(BF)
    for d in (1, 3, 2):
        q_copy(d).start()
    q_buf[3] = q4[x]
    mate_copy(0).start()
    for d in (1, 3, 2):
        head = lax.rem(x + d, 4)

        def write_other(rows, value, head=head):
            kv4[head, rows, :] = value

        keys_values(head, write_other)
        if d != 2:
            kvx_copy(d).start()

    my_cols = pl.ds(pl.multiple_of(z * 512, 512), 512)
    ow_own = pltpu.make_async_copy(ow_hbm.at[:, my_cols], ow.at[z], sem_ow_own)
    ow_own.start()

    def ow_copy(d):
        cols = pl.ds(pl.multiple_of(lax.rem(z + d, 4) * 512, 512), 512)
        return remote(
            ow_hbm.at[:, cols], ow.at[z], ow_send.at[d - 1], ow_recv.at[3 - d], at(dz=d)
        )

    for d in (1, 3, 2):
        ow_copy(d).start()

    def landed(slot):
        remote(
            kv.at[slot], kv.at[slot], own_send.at[0], kv_recv.at[slot], at(dc=1)
        ).wait_recv()

    def arrive(step):
        @pl.when(step != 2)
        def _():
            landed(2 * step)

        own = jnp.logical_and(step >= 2, step < 5)

        @pl.when(own)
        def _():
            own_copy(step - 1, 0).start()
            own_copy(step - 1, 1).start()

        @pl.when(jnp.logical_not(own))
        def _():
            pair_copy(jnp.where(step == 1, 0, step - 4)).start()

        landed(2 * step + 1)

    for r in (1, 2, 3):
        remote(
            q_buf.at[3], q_buf.at[3 - r], q_send.at[0], q_recv.at[r - 1], at(dx=1)
        ).wait_recv()
        mate_copy(r).start()

    def mate_arrive(r):
        remote(
            q_buf.at[0], q_buf.at[4 + r], mate_send.at[0], mate_recv.at[r], mate
        ).wait_recv()

    acc[...] = jnp.zeros_like(acc)
    mref[...] = jnp.full_like(mref, -1e30)
    ones = jnp.ones((16, 1024), BF)
    landed(1)

    def logits(step, t, slot):
        keys = jnp.concatenate([kv[2 * step, 0:512, :], kv[2 * step + 1, 0:512, :]], axis=0)
        s = lax.dot_general(keys, q_buf[t], NT, preferred_element_type=F32)
        (s0, s1)[slot][...] = s
        return jnp.max(s, axis=0, keepdims=True)

    def weigh(t, slot, block_max):
        old = mref[t, 0:1, :]
        new = jnp.maximum(old, block_max)
        mref[t, 0:1, :] = new
        (p0, p1)[slot][...] = jnp.exp2((s0, s1)[slot][...] - new).astype(BF)
        return jnp.exp2(old - new)

    def add(step, t, slot, rescale):
        pieces = [
            kv[2 * step + i, 512 + j * 128 : 640 + j * 128, :] for i in range(2) for j in range(4)
        ]
        vt = jnp.concatenate([jnp.concatenate(pieces, axis=1), ones], axis=0)
        acc[t] = acc[t] * rescale + dot(vt, (p0, p1)[slot][...])

    def turns(units, state):
        block_max, rescale = state
        for u in range(4):
            following = logits(*units[u + 2], u % 2)
            next_rescale = weigh(units[u + 1][1], (u + 1) % 2, block_max)
            add(*units[u], u % 2, rescale)
            block_max, rescale = following, next_rescale
        return block_max, rescale

    first = weigh(0, 0, logits(0, 0, 0))
    state = (logits(0, 1, 1), first)

    def place_of(k):
        step = jnp.where(k < 4, lax.rem(k, 2), lax.div(k, 2))
        group = jnp.where(k < 4, lax.div(k, 2), lax.rem(k, 2))
        return step, 4 * group

    def by_step(k, state):
        @pl.when(k == 0)
        def _():
            arrive(1)

        @pl.when(k == 1)
        def _():
            landed(own_slot(1))
            kvx_copy(2).start()

        @pl.when(jnp.logical_or(k == 1, k == 2))
        def _():
            arrive(k + 1)
            mate_arrive(2 * k - 2)
            mate_arrive(2 * k - 1)

        @pl.when(k >= 4)
        def _():
            arrive(k)

        step, tile = place_of(k)
        next_step, next_tile = place_of(k + 1)
        last = k == 7
        units = [(step, tile + u) for u in range(4)]
        units.append((next_step, jnp.where(last, 7, next_tile)))
        units.append((jnp.where(last, 5, next_step), jnp.where(last, 7, next_tile + 1)))
        return turns(units, state)

    state = lax.fori_loop(0, 8, by_step, state)

    mine = z * 4 + x

    def ax_copy(t):
        dx = order(3 - t)
        back = order((4 - dx) % 4) if isinstance(dx, int) else order(lax.rem(4 - dx, 4))
        return remote(
            stage.at[t], att.at[mine], ax_send.at[t], ax_recv.at[3 - back], at(dx=dx)
        )

    def az_rows(t, dz, half=None):
        head = lax.rem(z + dz, 4) * 4 + lax.rem(x + order(3 - t), 4)
        if half is None:
            return att.at[head]
        return att.at[head, pl.ds(half * 256, 256), :]

    def az_copy(t, i):
        rows = (az_rows(t, 0), az_rows(t, 0), az_rows(t, 3, 0), az_rows(t, 1, 1))[i]
        return remote(
            rows, rows, az_send.at[t * 4 + i], az_recv.at[t * 4 + i], at(dz=(1, 3, 1, 3)[i])
        )

    def az_arrive(t, i):
        rows = (az_rows(t, 3), az_rows(t, 1), az_rows(t, 2, 0), az_rows(t, 2, 1))[i]
        remote(rows, rows, az_send.at[0], az_recv.at[t * 4 + i], at(dz=1)).wait_recv()

    def share(t):
        az_copy(t, 0).start()
        az_copy(t, 1).start()

    def relay(t):
        for i in (0, 1):
            az_arrive(t, i)
            az_copy(t, i + 2).start()

    def ax_arrive(t):
        head = z * 4 + lax.rem(x + order(3 - t), 4)
        remote(stage.at[0], att.at[head], ax_send.at[0], ax_recv.at[t], at(dx=1)).wait_recv()

    def result_copy(r):
        return remote(
            res_send.at[r], res_recv.at[r], rs_send.at[r], rs_recv.at[r], mate
        )

    def scale_copy(r):
        return remote(
            scale_send.at[r], scale_recv.at[r], ss_send.at[r], ss_recv.at[r], mate
        )

    def tile_of(i):
        inner = jnp.where(lax.rem(i, 2) == 1, 6 - lax.div(i, 2), lax.div(i, 2) - 1)
        return jnp.where(i == 0, 7, jnp.where(i == 7, 3, inner))

    def by_tile(i, state):
        tile = tile_of(i)
        after = tile_of(jnp.minimum(i + 1, 7))
        units = [(4 + j, tile) for j in range(4)] + [(4, after), (5, after)]
        state = turns(units, state)

        @pl.when(tile >= 4)
        def _():
            r = tile - 4
            total = acc[tile, 128:129, :]
            res_send[r] = (acc[tile, 0:128, :] / total).astype(BF)
            scale_send[r, 0:1, :] = mref[tile, 0:1, :]
            scale_send[r, 1:2, :] = total
            result_copy(r).start()
            scale_copy(r).start()

        @pl.when(tile < 4)
        def _():
            t = tile
            r = 3 - t
            remote(
                res_send.at[0], res_recv.at[r], rs_send.at[0], rs_recv.at[r], mate
            ).wait_recv()
            remote(
                scale_send.at[0], scale_recv.at[r], ss_send.at[0], ss_recv.at[r], mate
            ).wait_recv()
            here, there = mref[tile, 0:1, :], scale_recv[r, 0:1, :]
            high = jnp.maximum(here, there)
            here = jnp.exp2(here - high)
            there = jnp.exp2(there - high) * scale_recv[r, 1:2, :]
            inverse = 1.0 / (here * acc[tile, 128:129, :] + there)
            both = acc[tile, 0:128, :] * (here * inverse)
            both = both + res_recv[r].astype(F32) * (there * inverse)
            block = both.T.astype(BF)

            @pl.when(t < 3)
            def _():
                stage[t] = block
                ax_copy(t).start()

            @pl.when(t == 3)
            def _():
                att[mine] = block
                share(3)

        @pl.when(i == 4)
        def _():
            ax_arrive(0)
            share(0)

        @pl.when(i == 6)
        def _():
            ax_arrive(1)
            share(1)
            relay(0)

        return state

    lax.fori_loop(0, 8, by_tile, state)

    def branch(dz):
        zs = lax.rem(z + dz, 4)
        heads = jnp.concatenate([att[zs * 4 + h] for h in range(4)], axis=1)
        return dot(heads, ow[zs])

    def ow_arrive(d):
        src = lax.rem(z + d, 4)
        remote(ow.at[src], ow.at[src], ow_send.at[0], ow_recv.at[d - 1], at(dz=1)).wait_recv()

    ax_arrive(2)
    share(2)
    relay(1)
    ow_own.wait()
    for d in (1, 2, 3):
        ow_arrive(d)
    result = emb[:, my_cols] + branch(0)
    relay(3)
    relay(2)
    result = result + branch(1) + branch(3)
    for t in range(4):
        az_arrive(t, 2)
        az_arrive(t, 3)
    out_ref[...] = (result + branch(2)).astype(BF)

    for i in range(4):
        pool_copy(i).wait_send()
    for d in (1, 2, 3):
        q_copy(d).wait_send()
        kvx_copy(d).wait_send()
        ow_copy(d).wait_send()
        ax_copy(d - 1).wait_send()

    def drain(n, _):
        for k in range(2):
            own_copy(n, k).wait_send()
        pair_copy(n).wait_send()
        mate_copy(n).wait_send()
        result_copy(n).wait_send()
        scale_copy(n).wait_send()
        for i in range(4):
            az_copy(n, i).wait_send()
        return 0

    lax.fori_loop(0, 4, drain, 0)


def on_device(tokens, key_query, value_weight, proj_weight, norm_gain, qkv_weight, out_weight):
    dma = pltpu.SemaphoreType.DMA
    vm = pltpu.VMEM
    scratch = [
        vm((2, NV, CH, 1024), BF),
        vm((128, 1024), BF),
        vm((128, 1024), BF),
        vm((1024, 1024), BF),
        vm((1024, 2048), BF),
        vm((2, 1536, 128), BF),
        vm((1536, 128), F32),
        vm((2048, 1536), BF),
        vm((NV * CH, 128), F32),
        vm((4, CH, 1024), BF),
        vm((3, CH, 1024), BF),
        vm((4, CH, 128), F32),
        vm((3, CH, 128), F32),
        vm((ROWS, 1024), BF),
        vm((ROWS, 2048), F32),
        vm((ROWS, 2048), BF),
        vm((4, ROWS, 128), BF),
        vm((4, 2 * ROWS, 128), BF),
        vm((8, ROWS, 128), BF),
        vm((16, 2 * ROWS, 128), BF),
        vm((1024, 512), F32),
        vm((1024, 512), F32),
        vm((1024, 512), BF),
        vm((1024, 512), BF),
        vm((8, 144, 512), F32),
        vm((8, 8, 512), F32),
        vm((4, 128, 512), BF),
        vm((4, 128, 512), BF),
        vm((4, 8, 512), F32),
        vm((4, 8, 512), F32),
        vm((4, 512, 512), BF),
        vm((3, ROWS, 128), BF),
        vm((16, ROWS, 128), BF),
        dma((2,)), dma((2,)), dma((2,)), dma,
        dma((3,)), dma((3,)), dma((3,)), dma((3,)), dma((4,)), dma((4,)),
        dma((3,)), dma((3,)), dma((3,)), dma((8,)), dma((4,)), dma((16,)),
        dma((4,)), dma((4,)), dma((4,)), dma((4,)), dma((4,)), dma((4,)),
        dma((3,)), dma((3,)), dma((3,)), dma((3,)), dma((16,)), dma((16,)),
    ]
    anywhere = pl.BlockSpec(memory_space=pl.ANY)
    vmem = pl.BlockSpec(memory_space=pltpu.VMEM)
    return pl.pallas_call(
        kernel,
        out_shape=jax.ShapeDtypeStruct((ROWS, 512), BF),
        in_specs=[anywhere, vmem, anywhere, anywhere, vmem, anywhere, anywhere],
        out_specs=vmem,
        scratch_shapes=scratch,
        compiler_params=pltpu.CompilerParams(
            collective_id=1, has_side_effects=True, vmem_limit_bytes=62 * 1024 * 1024
        ),
        name="block",
    )(
        tokens,
        key_query.T,
        value_weight,
        proj_weight,
        norm_gain.reshape(1, 2048),
        qkv_weight.reshape(2048 * 12, 128),
        out_weight.reshape(512, 2048),
    )


def solution(mesh):
    return jax.shard_map(
        on_device,
        mesh=mesh,
        in_specs=(
            P("var", "patch", None),
            P(),
            P(),
            P(),
            P(),
            P(None, None, "var", None),
            P("var", None, None),
        ),
        out_specs=P("patch", "var"),
        check_vma=False,
    )
```

```python
import functools

import jax
import jax.numpy as jnp
from jax import lax
from jax.experimental import pallas as pl
from jax.experimental.pallas import tpu as pltpu
from jax.sharding import PartitionSpec as P

MESH = pl.DeviceIdType.MESH
NT = (((1,), (1,)), ((), ()))
BF = jnp.bfloat16
F32 = jnp.float32

ROWS, NV, CH = 512, 12, 128
Q_SCALE = 128 ** (-0.5) * 1.4426950408889634


def order(e):
    if isinstance(e, int):
        return (0, 1, 3, 2)[e]
    return e + lax.div(e, 2) * (5 - 2 * e)


def dot(a, b):
    return jnp.dot(a, b, preferred_element_type=F32)


def kernel(
    tok_hbm, kq_ref, vw_hbm, proj_hbm, gain_ref, w2_hbm, ow_hbm,
    out_ref,
    tok, kqp, expand, vw, proj, wstage, wf, wq,
    wn, part_send, part_recv, stat_send, stat_recv, pooled,
    emb, normed, q4, kv4, q_buf, kv, s0, s1, p0, p1, acc, mref,
    res_send, res_recv, scale_send, scale_recv,
    ow, stage, att,
    sem_tok, sem_w, sem_w2, sem_ow_own,
    ps_send, ps_recv, st_send, st_recv, pool_send, pool_recv,
    q_send, q_recv, kvx_send, own_send, fwd_send, kv_recv,
    mate_send, mate_recv, rs_send, rs_recv, ss_send, ss_recv,
    ow_send, ow_recv, ax_send, ax_recv, az_send, az_recv,
):
    z = lax.axis_index("var")
    place = lax.axis_index("patch")
    x = lax.div(place, 8)
    y = lax.rem(lax.div(place, 2), 4)
    c = lax.rem(place, 2)

    def at(dx=0, dy=0, dz=0, dc=0):
        px = lax.rem(x + dx, 4)
        py = lax.rem(y + dy, 4)
        pc = lax.rem(c + dc, 2)
        return (lax.rem(z + dz, 4), (px * 4 + py) * 2 + pc)

    def remote(src, dst, send, recv, device):
        return pltpu.make_async_remote_copy(
            src_ref=src, dst_ref=dst, send_sem=send, recv_sem=recv,
            device_id=device, device_id_type=MESH,
        )

    def tok_copy(j, slot):
        base = pl.multiple_of(lax.rem(z + order(3 - j), 4) * CH, CH)
        return pltpu.make_async_copy(
            tok_hbm.at[:, pl.ds(base, CH), :], tok.at[slot], sem_tok.at[slot]
        )

    vw_copy = pltpu.make_async_copy(vw_hbm, vw, sem_w.at[0])
    proj_copy = pltpu.make_async_copy(proj_hbm, proj, sem_w.at[1])
    tok_copy(0, 0).start()
    vw_copy.start()
    tok_copy(1, 1).start()
    proj_copy.start()

    def w2_copy(i, slot):
        base = pl.multiple_of(i * 1536, 1536)
        return pltpu.make_async_copy(
            w2_hbm.at[pl.ds(base, 1536), :], wstage.at[slot], sem_w2.at[slot]
        )

    w2_copy(0, 0).start()
    w2_copy(1, 1).start()

    barrier = pltpu.get_barrier_semaphore()
    partners = [at(dx=d) for d in (1, 2, 3)] + [at(dy=d) for d in (1, 2, 3)]
    partners += [at(dz=d) for d in (1, 2, 3)] + [at(dc=1)]
    for device in partners:
        pl.semaphore_signal(barrier, inc=1, device_id=device, device_id_type=MESH)

    kqp[...] = jnp.zeros_like(kqp)
    kqp[0:16, :] = kq_ref[...]
    head_of = lax.broadcasted_iota(jnp.int32, (128, 1024), 0)
    lane = lax.broadcasted_iota(jnp.int32, (128, 1024), 1)
    expand[...] = jnp.where(lax.div(lane, 64) == head_of, 1.0, 0.0).astype(BF)

    vw_copy.wait()

    def part_copy(j):
        dz = order(3 - j)
        return remote(
            part_send.at[j], part_recv.at[3 - dz], ps_send.at[j], ps_recv.at[3 - dz], at(dz=dz)
        )

    def stat_copy(j):
        dz = order(3 - j)
        return remote(
            stat_send.at[j], stat_recv.at[3 - dz], st_send.at[j], st_recv.at[3 - dz], at(dz=dz)
        )

    def pool_chunk(j, _):
        slot = lax.rem(j, 2)
        tok_copy(j, slot).wait()
        scores = lax.dot_general(
            tok[slot].reshape(NV * CH, 1024), kqp[...], NT, preferred_element_type=F32
        ).reshape(NV, CH, 128)
        peak = jnp.max(scores, axis=0)
        weights = jnp.exp(scores - peak[None])
        totals = jnp.sum(weights, axis=0)
        first_lanes = lax.broadcasted_iota(jnp.int32, (CH, 128), 1) < 16
        stat_send[j] = jnp.where(first_lanes, peak, pltpu.roll(totals, 16, 1))
        wn[...] = weights.astype(BF).astype(F32).reshape(NV * CH, 128)

        upper = jnp.where(lax.broadcasted_iota(jnp.int32, (NV * CH, 128), 1) >= 64, 1, 0)
        values = dot(tok[slot].reshape(NV * CH, 1024), vw[...])
        wide = jnp.concatenate(
            [jnp.take_along_axis(wn[...], 2 * q + upper, axis=1) for q in range(8)], axis=1
        )
        part_send[j] = jnp.sum((values * wide).reshape(NV, CH, 1024), axis=0).astype(BF)

        @pl.when(j < 2)
        def _():
            tok_copy(j + 2, slot).start()

        @pl.when(j == 0)
        def _():
            pl.semaphore_wait(barrier, len(partners))

        @pl.when(j < 3)
        def _():
            part_copy(j).start()
            stat_copy(j).start()

        return 0

    lax.fori_loop(0, 4, pool_chunk, 0)

    for i in range(3):
        part_copy(i).wait_send()
        stat_copy(i).wait_send()
        remote(part_send.at[0], part_recv.at[i], ps_send.at[0], ps_recv.at[i], at(dz=1)).wait_recv()
        remote(stat_send.at[0], stat_recv.at[i], st_send.at[0], st_recv.at[i], at(dz=1)).wait_recv()
    peaks = [stat_send[3]] + [stat_recv[i] for i in range(3)]
    top = functools.reduce(jnp.maximum, peaks)
    factors = [jnp.exp(l - top) for l in peaks]
    inverse = 1.0 / sum(f * pltpu.roll(l, 112, 1) for f, l in zip(factors, peaks))
    real = lax.broadcasted_iota(jnp.int32, (CH, 128), 1) < 16
    total = jnp.zeros((CH, 1024), F32)
    for g in range(4):
        share = jnp.where(real, factors[g] * inverse, 0.0)
        high = share.astype(BF)
        low = (share - high.astype(F32)).astype(BF)
        wide = dot(high, expand[...]) + dot(low, expand[...])
        part = part_send[3] if g == 0 else part_recv[g - 1]
        total = total + wide * part.astype(F32)
    own_rows = pl.ds(pl.multiple_of(z * CH, CH), CH)
    pooled[own_rows, :] = total.astype(BF)

    def pool_rows(dz, half=None):
        base = lax.rem(z + dz, 4) * CH
        if half is None:
            return pooled.at[pl.ds(pl.multiple_of(base, CH), CH), :]
        return pooled.at[pl.ds(pl.multiple_of(base + half * (CH // 2), CH // 2), CH // 2), :]

    def pool_copy(i):
        rows = (pool_rows(0), pool_rows(0), pool_rows(3, 0), pool_rows(1, 1))[i]
        return remote(rows, rows, pool_send.at[i], pool_recv.at[i], at(dz=(1, 3, 1, 3)[i]))

    def pool_arrive(i):
        rows = (pool_rows(3), pool_rows(1), pool_rows(2, 0), pool_rows(2, 1))[i]
        remote(rows, rows, pool_send.at[0], pool_recv.at[i], at(dz=1)).wait_recv()

    pool_copy(0).start()
    pool_copy(1).start()

    def relayout(i, _):
        slot = lax.rem(i, 2)
        w2_copy(i, slot).wait()
        wf[...] = wstage[slot].astype(F32)
        rows = pl.ds(pl.multiple_of(i * 128, 128), 128)
        for n in range(12):
            to = n if n < 4 else 4 + 2 * (n % 4) + n // 8
            wq[rows, to * 128 : (to + 1) * 128] = wf[pl.ds(n, 128, stride=12), :].astype(BF)

        @pl.when(i < 14)
        def _():
            w2_copy(i + 2, slot).start()

        return 0

    lax.fori_loop(0, 11, relayout, 0)
    for i in (0, 1):
        pool_arrive(i)
        pool_copy(i + 2).start()
    lax.fori_loop(11, 16, relayout, 0)
    proj_copy.wait()
    for i in (2, 3):
        pool_arrive(i)

    def project(i, _):
        cs = pl.ds(pl.multiple_of(i * 512, 512), 512)
        emb[:, cs] = dot(pooled[...], proj[:, cs])
        return 0

    lax.fori_loop(0, 4, project, 0)

    def norm(i, _):
        rows = pl.ds(pl.multiple_of(i * 128, 128), 128)
        block = emb[rows, :]
        center = block - jnp.mean(block, axis=1, keepdims=True)
        variance = jnp.mean(center * center, axis=1, keepdims=True)
        normed[rows, :] = (center / jnp.sqrt(variance + 1e-05) * gain_ref[...]).astype(BF)
        return 0

    lax.fori_loop(0, 4, norm, 0)

    def q_copy(d):
        dst = order((4 - d) % 4)
        head = lax.rem(x + d, 4)
        return remote(
            q4.at[head], q_buf.at[3 - dst], q_send.at[d - 1], q_recv.at[dst - 1], at(dx=d)
        )

    def kvx_copy(d):
        dst = order((4 - d) % 4)
        head = lax.rem(x + d, 4)
        slot = own_slot(dst)
        return remote(kv4.at[head], kv.at[slot], kvx_send.at[d - 1], kv_recv.at[slot], at(dx=d))

    odd = lax.rem(y, 2)
    partner = at(dy=1 + 2 * odd)
    mate = at(dy=3 - 2 * odd)

    def own_slot(r):
        return (0, 4, 6, 8)[r] if isinstance(r, int) else jnp.where(r == 0, 0, 2 + 2 * r)

    def pair_slot(r):
        return (2, 10, 12, 14)[r] if isinstance(r, int) else jnp.where(r == 0, 2, 8 + 2 * r)

    def own_copy(r, k):
        slot = (own_slot(r) + 1, pair_slot(r))[k]
        return remote(
            kv.at[own_slot(r)], kv.at[slot], own_send.at[r * 2 + k], kv_recv.at[slot],
            (at(dc=1), partner)[k],
        )

    def pair_copy(r):
        slot = pair_slot(r)
        return remote(
            kv.at[slot], kv.at[slot + 1], fwd_send.at[r], kv_recv.at[slot + 1], at(dc=1)
        )

    def mate_copy(r):
        return remote(
            q_buf.at[3 - r], q_buf.at[4 + r], mate_send.at[r], mate_recv.at[r], mate
        )

    def keys_values(head, write):
        cs = pl.ds(pl.multiple_of(512 + head * 256, 256), 256)
        both = dot(normed[...], wq[:, cs])
        write(slice(0, 512), both[:, 0:128].astype(BF))
        for j in range(4):
            tile = both[j * 128 : (j + 1) * 128, 128:256]
            write(slice(512 + j * 128, 640 + j * 128), tile.T.astype(BF))

    def write_own(rows, value):
        kv[0, rows, :] = value

    keys_values(x, write_own)
    own_copy(0, 0).start()
    own_copy(0, 1).start()
    queries = dot(normed[...], wq[:, 0:512]) * Q_SCALE
    for h in range(4):
        q4[h] = queries[:, h * 128 : (h + 1) * 128].astype(BF)
    for d in (1, 3, 2):
        q_copy(d).start()
    q_buf[3] = q4[x]
    mate_copy(0).start()
    for d in (1, 3, 2):
        head = lax.rem(x + d, 4)

        def write_other(rows, value, head=head):
            kv4[head, rows, :] = value

        keys_values(head, write_other)
        if d != 2:
            kvx_copy(d).start()

    my_cols = pl.ds(pl.multiple_of(z * 512, 512), 512)
    ow_own = pltpu.make_async_copy(ow_hbm.at[:, my_cols], ow.at[z], sem_ow_own)
    ow_own.start()

    def ow_copy(d):
        cols = pl.ds(pl.multiple_of(lax.rem(z + d, 4) * 512, 512), 512)
        return remote(
            ow_hbm.at[:, cols], ow.at[z], ow_send.at[d - 1], ow_recv.at[3 - d], at(dz=d)
        )

    for d in (1, 3, 2):
        ow_copy(d).start()

    def landed(slot):
        remote(
            kv.at[slot], kv.at[slot], own_send.at[0], kv_recv.at[slot], at(dc=1)
        ).wait_recv()

    def bring(step):
        landed(2 * step)
        if step in (2, 3, 4):
            own_copy(step - 1, 0).start()
            own_copy(step - 1, 1).start()
        else:
            pair_copy(0 if step == 1 else step - 4).start()

    def ready(step):
        landed(2 * step + 1)

    for r in (1, 2, 3):
        remote(
            q_buf.at[3], q_buf.at[3 - r], q_send.at[0], q_recv.at[r - 1], at(dx=1)
        ).wait_recv()
        mate_copy(r).start()

    def mate_arrive(r):
        remote(
            q_buf.at[0], q_buf.at[4 + r], mate_send.at[0], mate_recv.at[r], mate
        ).wait_recv()

    acc[...] = jnp.zeros_like(acc)
    mref[...] = jnp.full_like(mref, -1e30)
    ones = jnp.ones((16, 1024), BF)
    landed(1)

    def logits(step, t, slot):
        keys = jnp.concatenate([kv[2 * step, 0:512, :], kv[2 * step + 1, 0:512, :]], axis=0)
        s = lax.dot_general(keys, q_buf[t], NT, preferred_element_type=F32)
        (s0, s1)[slot][...] = s
        return jnp.max(s, axis=0, keepdims=True)

    def weigh(t, slot, block_max):
        old = mref[t, 0:1, :]
        new = jnp.maximum(old, block_max)
        mref[t, 0:1, :] = new
        (p0, p1)[slot][...] = jnp.exp2((s0, s1)[slot][...] - new).astype(BF)
        return jnp.exp2(old - new)

    def add(step, t, slot, rescale):
        pieces = [
            kv[2 * step + i, 512 + j * 128 : 640 + j * 128, :] for i in range(2) for j in range(4)
        ]
        vt = jnp.concatenate([jnp.concatenate(pieces, axis=1), ones], axis=0)
        acc[t] = acc[t] * rescale + dot(vt, (p0, p1)[slot][...])

    def turns(units, state):
        block_max, rescale = state
        for u in range(4):
            following = logits(*units[u + 2], u % 2)
            next_rescale = weigh(units[u + 1][1], (u + 1) % 2, block_max)
            add(*units[u], u % 2, rescale)
            block_max, rescale = following, next_rescale
        return block_max, rescale

    first = weigh(0, 0, logits(0, 0, 0))
    state = (logits(0, 1, 1), first)

    def place_of(k):
        step = jnp.where(k < 4, lax.rem(k, 2), lax.div(k, 2))
        group = jnp.where(k < 4, lax.div(k, 2), lax.rem(k, 2))
        return step, 4 * group

    def by_step(k, state):
        @pl.when(k == 0)
        def _():
            ready(1)

        @pl.when(k == 1)
        def _():
            bring(2)
            kvx_copy(2).start()
            bring(3)
            mate_arrive(0)
            mate_arrive(1)

        @pl.when(k == 2)
        def _():
            mate_arrive(2)
            mate_arrive(3)

        @pl.when(k == 3)
        def _():
            ready(2)

        @pl.when(k == 4)
        def _():
            bring(4)

        @pl.when(k == 5)
        def _():
            ready(3)
            bring(5)

        @pl.when(k == 6)
        def _():
            ready(4)
            bring(6)

        @pl.when(k == 7)
        def _():
            ready(5)
            bring(7)

        step, tile = place_of(k)
        next_step, next_tile = place_of(k + 1)
        last = k == 7
        units = [(step, tile + u) for u in range(4)]
        units.append((next_step, jnp.where(last, 7, next_tile)))
        units.append((jnp.where(last, 5, next_step), jnp.where(last, 7, next_tile + 1)))
        return turns(units, state)

    bring(1)
    state = lax.fori_loop(0, 8, by_step, state)
    ready(6)
    ready(7)

    mine = z * 4 + x

    def ax_copy(t):
        dx = order(3 - t)
        back = order((4 - dx) % 4) if isinstance(dx, int) else order(lax.rem(4 - dx, 4))
        return remote(
            stage.at[t], att.at[mine], ax_send.at[t], ax_recv.at[3 - back], at(dx=dx)
        )

    def az_rows(t, dz, half=None):
        head = lax.rem(z + dz, 4) * 4 + lax.rem(x + order(3 - t), 4)
        if half is None:
            return att.at[head]
        return att.at[head, pl.ds(half * 256, 256), :]

    def az_copy(t, i):
        rows = (az_rows(t, 0), az_rows(t, 0), az_rows(t, 3, 0), az_rows(t, 1, 1))[i]
        return remote(
            rows, rows, az_send.at[t * 4 + i], az_recv.at[t * 4 + i], at(dz=(1, 3, 1, 3)[i])
        )

    def az_arrive(t, i):
        rows = (az_rows(t, 3), az_rows(t, 1), az_rows(t, 2, 0), az_rows(t, 2, 1))[i]
        remote(rows, rows, az_send.at[0], az_recv.at[t * 4 + i], at(dz=1)).wait_recv()

    def share(t):
        az_copy(t, 0).start()
        az_copy(t, 1).start()

    def relay(t):
        for i in (0, 1):
            az_arrive(t, i)
            az_copy(t, i + 2).start()

    def ax_arrive(t):
        head = z * 4 + lax.rem(x + order(3 - t), 4)
        remote(stage.at[0], att.at[head], ax_send.at[0], ax_recv.at[t], at(dx=1)).wait_recv()

    def result_copy(r):
        return remote(
            res_send.at[r], res_recv.at[r], rs_send.at[r], rs_recv.at[r], mate
        )

    def scale_copy(r):
        return remote(
            scale_send.at[r], scale_recv.at[r], ss_send.at[r], ss_recv.at[r], mate
        )

    def tile_of(i):
        inner = jnp.where(lax.rem(i, 2) == 1, 6 - lax.div(i, 2), lax.div(i, 2) - 1)
        return jnp.where(i == 0, 7, jnp.where(i == 7, 3, inner))

    def by_tile(i, state):
        tile = tile_of(i)
        after = tile_of(jnp.minimum(i + 1, 7))
        units = [(4 + j, tile) for j in range(4)] + [(4, after), (5, after)]
        state = turns(units, state)

        @pl.when(tile >= 4)
        def _():
            r = tile - 4
            total = acc[tile, 128:129, :]
            res_send[r] = (acc[tile, 0:128, :] / total).astype(BF)
            scale_send[r, 0:1, :] = mref[tile, 0:1, :]
            scale_send[r, 1:2, :] = total
            result_copy(r).start()
            scale_copy(r).start()

        @pl.when(tile < 4)
        def _():
            t = tile
            r = 3 - t
            remote(
                res_send.at[0], res_recv.at[r], rs_send.at[0], rs_recv.at[r], mate
            ).wait_recv()
            remote(
                scale_send.at[0], scale_recv.at[r], ss_send.at[0], ss_recv.at[r], mate
            ).wait_recv()
            here, there = mref[tile, 0:1, :], scale_recv[r, 0:1, :]
            high = jnp.maximum(here, there)
            here = jnp.exp2(here - high)
            there = jnp.exp2(there - high) * scale_recv[r, 1:2, :]
            inverse = 1.0 / (here * acc[tile, 128:129, :] + there)
            both = acc[tile, 0:128, :] * (here * inverse)
            both = both + res_recv[r].astype(F32) * (there * inverse)
            block = both.T.astype(BF)

            @pl.when(t < 3)
            def _():
                stage[t] = block
                ax_copy(t).start()

            @pl.when(t == 3)
            def _():
                att[mine] = block
                share(3)

        @pl.when(i == 4)
        def _():
            ax_arrive(0)
            share(0)

        @pl.when(i == 6)
        def _():
            ax_arrive(1)
            share(1)
            relay(0)

        return state

    lax.fori_loop(0, 8, by_tile, state)

    def branch(dz):
        zs = lax.rem(z + dz, 4)
        heads = jnp.concatenate([att[zs * 4 + h] for h in range(4)], axis=1)
        return dot(heads, ow[zs])

    def ow_arrive(d):
        src = lax.rem(z + d, 4)
        remote(ow.at[src], ow.at[src], ow_send.at[0], ow_recv.at[d - 1], at(dz=1)).wait_recv()

    ax_arrive(2)
    share(2)
    relay(1)
    ow_own.wait()
    for d in (1, 2, 3):
        ow_arrive(d)
    result = emb[:, my_cols] + branch(0)
    relay(3)
    relay(2)
    result = result + branch(1) + branch(3)
    for t in range(4):
        az_arrive(t, 2)
        az_arrive(t, 3)
    out_ref[...] = (result + branch(2)).astype(BF)

    for i in range(4):
        pool_copy(i).wait_send()
    for d in (1, 2, 3):
        q_copy(d).wait_send()
        kvx_copy(d).wait_send()
        ow_copy(d).wait_send()
        ax_copy(d - 1).wait_send()

    def drain(n, _):
        for k in range(2):
            own_copy(n, k).wait_send()
        pair_copy(n).wait_send()
        mate_copy(n).wait_send()
        result_copy(n).wait_send()
        scale_copy(n).wait_send()
        for i in range(4):
            az_copy(n, i).wait_send()
        return 0

    lax.fori_loop(0, 4, drain, 0)


def on_device(tokens, key_query, value_weight, proj_weight, norm_gain, qkv_weight, out_weight):
    dma = pltpu.SemaphoreType.DMA
    vm = pltpu.VMEM
    scratch = [
        vm((2, NV, CH, 1024), BF),
        vm((128, 1024), BF),
        vm((128, 1024), BF),
        vm((1024, 1024), BF),
        vm((1024, 2048), BF),
        vm((2, 1536, 128), BF),
        vm((1536, 128), F32),
        vm((2048, 1536), BF),
        vm((NV * CH, 128), F32),
        vm((4, CH, 1024), BF),
        vm((3, CH, 1024), BF),
        vm((4, CH, 128), F32),
        vm((3, CH, 128), F32),
        vm((ROWS, 1024), BF),
        vm((ROWS, 2048), F32),
        vm((ROWS, 2048), BF),
        vm((4, ROWS, 128), BF),
        vm((4, 2 * ROWS, 128), BF),
        vm((8, ROWS, 128), BF),
        vm((16, 2 * ROWS, 128), BF),
        vm((1024, 512), F32),
        vm((1024, 512), F32),
        vm((1024, 512), BF),
        vm((1024, 512), BF),
        vm((8, 144, 512), F32),
        vm((8, 8, 512), F32),
        vm((4, 128, 512), BF),
        vm((4, 128, 512), BF),
        vm((4, 8, 512), F32),
        vm((4, 8, 512), F32),
        vm((4, 512, 512), BF),
        vm((3, ROWS, 128), BF),
        vm((16, ROWS, 128), BF),
        dma((2,)), dma((2,)), dma((2,)), dma,
        dma((3,)), dma((3,)), dma((3,)), dma((3,)), dma((4,)), dma((4,)),
        dma((3,)), dma((3,)), dma((3,)), dma((8,)), dma((4,)), dma((16,)),
        dma((4,)), dma((4,)), dma((4,)), dma((4,)), dma((4,)), dma((4,)),
        dma((3,)), dma((3,)), dma((3,)), dma((3,)), dma((16,)), dma((16,)),
    ]
    anywhere = pl.BlockSpec(memory_space=pl.ANY)
    vmem = pl.BlockSpec(memory_space=pltpu.VMEM)
    return pl.pallas_call(
        kernel,
        out_shape=jax.ShapeDtypeStruct((ROWS, 512), BF),
        in_specs=[anywhere, vmem, anywhere, anywhere, vmem, anywhere, anywhere],
        out_specs=vmem,
        scratch_shapes=scratch,
        compiler_params=pltpu.CompilerParams(
            collective_id=1, has_side_effects=True, vmem_limit_bytes=62 * 1024 * 1024
        ),
        name="block",
    )(
        tokens,
        key_query.T,
        value_weight,
        proj_weight,
        norm_gain.reshape(1, 2048),
        qkv_weight.reshape(2048 * 12, 128),
        out_weight.reshape(512, 2048),
    )


def solution(mesh):
    return jax.shard_map(
        on_device,
        mesh=mesh,
        in_specs=(
            P("var", "patch", None),
            P(),
            P(),
            P(),
            P(),
            P(None, None, "var", None),
            P("var", None, None),
        ),
        out_specs=P("patch", "var"),
        check_vma=False,
    )
```

```python
import functools

import jax
import jax.numpy as jnp
from jax import lax
from jax.experimental import pallas as pl
from jax.experimental.pallas import tpu as pltpu
from jax.sharding import PartitionSpec as P

MESH = pl.DeviceIdType.MESH
NT = (((1,), (1,)), ((), ()))
BF = jnp.bfloat16
F32 = jnp.float32

ROWS, NV, CH = 512, 12, 128
Q_SCALE = 128 ** (-0.5) * 1.4426950408889634


def order(e):
    if isinstance(e, int):
        return (0, 1, 3, 2)[e]
    return e + lax.div(e, 2) * (5 - 2 * e)


def dot(a, b):
    return jnp.dot(a, b, preferred_element_type=F32)


def kernel(
    tok_hbm, kq_ref, vw_hbm, proj_hbm, gain_ref, w2_hbm, ow_hbm,
    out_ref,
    tok, kqp, expand, vw, proj, wstage, wf, wq,
    wn, part_send, part_recv, stat_send, stat_recv, pooled,
    emb, normed, q4, kv4, q_buf, kv, s0, s1, p0, p1, acc, mref,
    res_send, res_recv, scale_send, scale_recv,
    ow, stage, att,
    sem_tok, sem_w, sem_w2, sem_ow_own,
    ps_send, ps_recv, st_send, st_recv, pool_send, pool_recv,
    q_send, q_recv, kvx_send, own_send, fwd_send, kv_recv,
    mate_send, mate_recv, rs_send, rs_recv, ss_send, ss_recv,
    ow_send, ow_recv, ax_send, ax_recv, az_send, az_recv,
):
    z = lax.axis_index("var")
    place = lax.axis_index("patch")
    x = lax.div(place, 8)
    y = lax.rem(lax.div(place, 2), 4)
    c = lax.rem(place, 2)

    def at(dx=0, dy=0, dz=0, dc=0):
        px = lax.rem(x + dx, 4)
        py = lax.rem(y + dy, 4)
        pc = lax.rem(c + dc, 2)
        return (lax.rem(z + dz, 4), (px * 4 + py) * 2 + pc)

    def remote(src, dst, send, recv, device):
        return pltpu.make_async_remote_copy(
            src_ref=src, dst_ref=dst, send_sem=send, recv_sem=recv,
            device_id=device, device_id_type=MESH,
        )

    def tok_copy(j, slot):
        base = pl.multiple_of(lax.rem(z + order(3 - j), 4) * CH, CH)
        return pltpu.make_async_copy(
            tok_hbm.at[:, pl.ds(base, CH), :], tok.at[slot], sem_tok.at[slot]
        )

    vw_copy = pltpu.make_async_copy(vw_hbm, vw, sem_w.at[0])
    proj_copy = pltpu.make_async_copy(proj_hbm, proj, sem_w.at[1])
    tok_copy(0, 0).start()
    vw_copy.start()
    tok_copy(1, 1).start()
    proj_copy.start()

    def w2_copy(i, slot):
        base = pl.multiple_of(i * 1536, 1536)
        return pltpu.make_async_copy(
            w2_hbm.at[pl.ds(base, 1536), :], wstage.at[slot], sem_w2.at[slot]
        )

    w2_copy(0, 0).start()
    w2_copy(1, 1).start()

    barrier = pltpu.get_barrier_semaphore()
    partners = [at(dx=d) for d in (1, 2, 3)] + [at(dy=d) for d in (1, 2, 3)]
    partners += [at(dz=d) for d in (1, 2, 3)] + [at(dc=1)]
    for device in partners:
        pl.semaphore_signal(barrier, inc=1, device_id=device, device_id_type=MESH)

    kqp[...] = jnp.zeros_like(kqp)
    kqp[0:16, :] = kq_ref[...]
    head_of = lax.broadcasted_iota(jnp.int32, (128, 1024), 0)
    lane = lax.broadcasted_iota(jnp.int32, (128, 1024), 1)
    expand[...] = jnp.where(lax.div(lane, 64) == head_of, 1.0, 0.0).astype(BF)

    vw_copy.wait()

    def part_copy(j):
        dz = order(3 - j)
        return remote(
            part_send.at[j], part_recv.at[3 - dz], ps_send.at[j], ps_recv.at[3 - dz], at(dz=dz)
        )

    def stat_copy(j):
        dz = order(3 - j)
        return remote(
            stat_send.at[j], stat_recv.at[3 - dz], st_send.at[j], st_recv.at[3 - dz], at(dz=dz)
        )

    def pool_chunk(j, _):
        slot = lax.rem(j, 2)
        tok_copy(j, slot).wait()
        scores = lax.dot_general(
            tok[slot].reshape(NV * CH, 1024), kqp[...], NT, preferred_element_type=F32
        ).reshape(NV, CH, 128)
        peak = jnp.max(scores, axis=0)
        weights = jnp.exp(scores - peak[None])
        totals = jnp.sum(weights, axis=0)
        first_lanes = lax.broadcasted_iota(jnp.int32, (CH, 128), 1) < 16
        stat_send[j] = jnp.where(first_lanes, peak, pltpu.roll(totals, 16, 1)).T[0:32, :]
        wn[...] = weights.astype(BF).astype(F32).reshape(NV * CH, 128)

        upper = jnp.where(lax.broadcasted_iota(jnp.int32, (NV * CH, 128), 1) >= 64, 1, 0)
        values = dot(tok[slot].reshape(NV * CH, 1024), vw[...])
        wide = jnp.concatenate(
            [jnp.take_along_axis(wn[...], 2 * q + upper, axis=1) for q in range(8)], axis=1
        )
        part_send[j] = jnp.sum((values * wide).reshape(NV, CH, 1024), axis=0).astype(BF)

        @pl.when(j < 2)
        def _():
            tok_copy(j + 2, slot).start()

        @pl.when(j == 0)
        def _():
            pl.semaphore_wait(barrier, len(partners))

        @pl.when(j < 3)
        def _():
            part_copy(j).start()
            stat_copy(j).start()

        return 0

    lax.fori_loop(0, 4, pool_chunk, 0)

    for i in range(3):
        part_copy(i).wait_send()
        stat_copy(i).wait_send()
        remote(part_send.at[0], part_recv.at[i], ps_send.at[0], ps_recv.at[i], at(dz=1)).wait_recv()
        remote(stat_send.at[0], stat_recv.at[i], st_send.at[0], st_recv.at[i], at(dz=1)).wait_recv()
    empty = jnp.zeros((96, 128), F32)
    peaks = [stat_send[3]] + [stat_recv[i] for i in range(3)]
    peaks = [jnp.concatenate([p, empty], axis=0).T for p in peaks]
    top = functools.reduce(jnp.maximum, peaks)
    factors = [jnp.exp(l - top) for l in peaks]
    inverse = 1.0 / sum(f * pltpu.roll(l, 112, 1) for f, l in zip(factors, peaks))
    real = lax.broadcasted_iota(jnp.int32, (CH, 128), 1) < 16
    total = jnp.zeros((CH, 1024), F32)
    for g in range(4):
        share = jnp.where(real, factors[g] * inverse, 0.0)
        high = share.astype(BF)
        low = (share - high.astype(F32)).astype(BF)
        wide = dot(high, expand[...]) + dot(low, expand[...])
        part = part_send[3] if g == 0 else part_recv[g - 1]
        total = total + wide * part.astype(F32)
    own_rows = pl.ds(pl.multiple_of(z * CH, CH), CH)
    pooled[own_rows, :] = total.astype(BF)

    def pool_rows(dz, half=None):
        base = lax.rem(z + dz, 4) * CH
        if half is None:
            return pooled.at[pl.ds(pl.multiple_of(base, CH), CH), :]
        return pooled.at[pl.ds(pl.multiple_of(base + half * (CH // 2), CH // 2), CH // 2), :]

    def pool_copy(i):
        rows = (pool_rows(0), pool_rows(0), pool_rows(3, 0), pool_rows(1, 1))[i]
        return remote(rows, rows, pool_send.at[i], pool_recv.at[i], at(dz=(1, 3, 1, 3)[i]))

    def pool_arrive(i):
        rows = (pool_rows(3), pool_rows(1), pool_rows(2, 0), pool_rows(2, 1))[i]
        remote(rows, rows, pool_send.at[0], pool_recv.at[i], at(dz=1)).wait_recv()

    pool_copy(0).start()
    pool_copy(1).start()

    def relayout(i, _):
        slot = lax.rem(i, 2)
        w2_copy(i, slot).wait()
        wf[...] = wstage[slot].astype(F32)
        rows = pl.ds(pl.multiple_of(i * 128, 128), 128)
        for n in range(12):
            to = n if n < 4 else 4 + 2 * (n % 4) + n // 8
            wq[rows, to * 128 : (to + 1) * 128] = wf[pl.ds(n, 128, stride=12), :].astype(BF)

        @pl.when(i < 14)
        def _():
            w2_copy(i + 2, slot).start()

        return 0

    lax.fori_loop(0, 11, relayout, 0)
    for i in (0, 1):
        pool_arrive(i)
        pool_copy(i + 2).start()
    lax.fori_loop(11, 16, relayout, 0)
    proj_copy.wait()
    for i in (2, 3):
        pool_arrive(i)

    def project(i, _):
        cs = pl.ds(pl.multiple_of(i * 512, 512), 512)
        emb[:, cs] = dot(pooled[...], proj[:, cs])
        return 0

    lax.fori_loop(0, 4, project, 0)

    def norm(i, _):
        rows = pl.ds(pl.multiple_of(i * 128, 128), 128)
        block = emb[rows, :]
        center = block - jnp.mean(block, axis=1, keepdims=True)
        variance = jnp.mean(center * center, axis=1, keepdims=True)
        normed[rows, :] = (center / jnp.sqrt(variance + 1e-05) * gain_ref[...]).astype(BF)
        return 0

    lax.fori_loop(0, 4, norm, 0)

    def q_copy(d):
        dst = order((4 - d) % 4)
        head = lax.rem(x + d, 4)
        return remote(
            q4.at[head], q_buf.at[3 - dst], q_send.at[d - 1], q_recv.at[dst - 1], at(dx=d)
        )

    def kvx_copy(d):
        dst = order((4 - d) % 4)
        head = lax.rem(x + d, 4)
        slot = own_slot(dst)
        return remote(kv4.at[head], kv.at[slot], kvx_send.at[d - 1], kv_recv.at[slot], at(dx=d))

    odd = lax.rem(y, 2)
    partner = at(dy=1 + 2 * odd)
    mate = at(dy=3 - 2 * odd)

    def own_slot(r):
        return (0, 4, 6, 8)[r] if isinstance(r, int) else jnp.where(r == 0, 0, 2 + 2 * r)

    def pair_slot(r):
        return (2, 10, 12, 14)[r] if isinstance(r, int) else jnp.where(r == 0, 2, 8 + 2 * r)

    def own_copy(r, k):
        slot = (own_slot(r) + 1, pair_slot(r))[k]
        return remote(
            kv.at[own_slot(r)], kv.at[slot], own_send.at[r * 2 + k], kv_recv.at[slot],
            (at(dc=1), partner)[k],
        )

    def pair_copy(r):
        slot = pair_slot(r)
        return remote(
            kv.at[slot], kv.at[slot + 1], fwd_send.at[r], kv_recv.at[slot + 1], at(dc=1)
        )

    def mate_copy(r):
        return remote(
            q_buf.at[3 - r], q_buf.at[4 + r], mate_send.at[r], mate_recv.at[r], mate
        )

    def keys_values(head, write):
        cs = pl.ds(pl.multiple_of(512 + head * 256, 256), 256)
        both = dot(normed[...], wq[:, cs])
        write(slice(0, 512), both[:, 0:128].astype(BF))
        for j in range(4):
            tile = both[j * 128 : (j + 1) * 128, 128:256]
            write(slice(512 + j * 128, 640 + j * 128), tile.T.astype(BF))

    def write_own(rows, value):
        kv[0, rows, :] = value

    queries = dot(normed[...], wq[:, 0:512]) * Q_SCALE
    for h in range(4):
        q4[h] = queries[:, h * 128 : (h + 1) * 128].astype(BF)
    for d in (2, 1, 3):
        q_copy(d).start()
    q_buf[3] = q4[x]
    mate_copy(0).start()
    keys_values(x, write_own)
    own_copy(0, 0).start()
    own_copy(0, 1).start()
    for d in (1, 3, 2):
        head = lax.rem(x + d, 4)

        def write_other(rows, value, head=head):
            kv4[head, rows, :] = value

        keys_values(head, write_other)
        if d != 2:
            kvx_copy(d).start()

    my_cols = pl.ds(pl.multiple_of(z * 512, 512), 512)
    ow_own = pltpu.make_async_copy(ow_hbm.at[:, my_cols], ow.at[z], sem_ow_own)
    ow_own.start()

    def ow_copy(d):
        cols = pl.ds(pl.multiple_of(lax.rem(z + d, 4) * 512, 512), 512)
        return remote(
            ow_hbm.at[:, cols], ow.at[z], ow_send.at[d - 1], ow_recv.at[3 - d], at(dz=d)
        )

    for d in (1, 3, 2):
        ow_copy(d).start()

    def landed(slot):
        remote(
            kv.at[slot], kv.at[slot], own_send.at[0], kv_recv.at[slot], at(dc=1)
        ).wait_recv()

    def bring(step):
        landed(2 * step)
        if step in (2, 3, 4):
            own_copy(step - 1, 0).start()
            own_copy(step - 1, 1).start()
        else:
            pair_copy(0 if step == 1 else step - 4).start()

    def ready(step):
        landed(2 * step + 1)

    for r in (1, 2, 3):
        remote(
            q_buf.at[3], q_buf.at[3 - r], q_send.at[0], q_recv.at[r - 1], at(dx=1)
        ).wait_recv()
        mate_copy(r).start()
        if r == 2:
            bring(1)

    def mate_arrive(r):
        remote(
            q_buf.at[0], q_buf.at[4 + r], mate_send.at[0], mate_recv.at[r], mate
        ).wait_recv()

    acc[...] = jnp.zeros_like(acc)
    mref[...] = jnp.full_like(mref, -1e30)
    ones = jnp.ones((16, 1024), BF)
    landed(1)

    def logits(step, t, slot):
        keys = jnp.concatenate([kv[2 * step, 0:512, :], kv[2 * step + 1, 0:512, :]], axis=0)
        s = lax.dot_general(keys, q_buf[t], NT, preferred_element_type=F32)
        (s0, s1)[slot][...] = s
        return jnp.max(s, axis=0, keepdims=True)

    def weigh(t, slot, block_max):
        old = mref[t, 0:1, :]
        new = jnp.maximum(old, block_max)
        mref[t, 0:1, :] = new
        (p0, p1)[slot][...] = jnp.exp2((s0, s1)[slot][...] - new).astype(BF)
        return jnp.exp2(old - new)

    def add(step, t, slot, rescale):
        pieces = [
            kv[2 * step + i, 512 + j * 128 : 640 + j * 128, :] for i in range(2) for j in range(4)
        ]
        vt = jnp.concatenate([jnp.concatenate(pieces, axis=1), ones], axis=0)
        acc[t] = acc[t] * rescale + dot(vt, (p0, p1)[slot][...])

    def turns(units, state):
        block_max, rescale = state
        for u in range(4):
            following = logits(*units[u + 2], u % 2)
            next_rescale = weigh(units[u + 1][1], (u + 1) % 2, block_max)
            add(*units[u], u % 2, rescale)
            block_max, rescale = following, next_rescale
        return block_max, rescale

    first = weigh(0, 0, logits(0, 0, 0))
    state = (logits(0, 1, 1), first)

    def place_of(k):
        step = jnp.where(k < 4, lax.rem(k, 2), lax.div(k, 2))
        group = jnp.where(k < 4, lax.div(k, 2), lax.rem(k, 2))
        return step, 4 * group

    def by_step(k, state):
        @pl.when(k == 0)
        def _():
            ready(1)

        @pl.when(k == 1)
        def _():
            bring(2)
            kvx_copy(2).start()
            mate_arrive(0)
            mate_arrive(1)

        @pl.when(k == 2)
        def _():
            bring(3)
            mate_arrive(2)
            mate_arrive(3)

        @pl.when(k == 3)
        def _():
            ready(2)

        @pl.when(k == 4)
        def _():
            bring(4)

        @pl.when(k == 5)
        def _():
            ready(3)
            bring(5)

        @pl.when(k == 6)
        def _():
            ready(4)
            bring(6)

        @pl.when(k == 7)
        def _():
            ready(5)
            bring(7)

        step, tile = place_of(k)
        next_step, next_tile = place_of(k + 1)
        last = k == 7
        units = [(step, tile + u) for u in range(4)]
        units.append((next_step, jnp.where(last, 7, next_tile)))
        units.append((jnp.where(last, 5, next_step), jnp.where(last, 7, next_tile + 1)))
        return turns(units, state)

    state = lax.fori_loop(0, 8, by_step, state)
    ready(6)
    ready(7)

    mine = z * 4 + x

    def ax_copy(t):
        dx = order(3 - t)
        back = order((4 - dx) % 4) if isinstance(dx, int) else order(lax.rem(4 - dx, 4))
        return remote(
            stage.at[t], att.at[mine], ax_send.at[t], ax_recv.at[3 - back], at(dx=dx)
        )

    def az_rows(t, dz, half=None):
        head = lax.rem(z + dz, 4) * 4 + lax.rem(x + order(3 - t), 4)
        if half is None:
            return att.at[head]
        return att.at[head, pl.ds(half * 256, 256), :]

    def az_copy(t, i):
        rows = (az_rows(t, 0), az_rows(t, 0), az_rows(t, 3, 0), az_rows(t, 1, 1))[i]
        return remote(
            rows, rows, az_send.at[t * 4 + i], az_recv.at[t * 4 + i], at(dz=(1, 3, 1, 3)[i])
        )

    def az_arrive(t, i):
        rows = (az_rows(t, 3), az_rows(t, 1), az_rows(t, 2, 0), az_rows(t, 2, 1))[i]
        remote(rows, rows, az_send.at[0], az_recv.at[t * 4 + i], at(dz=1)).wait_recv()

    def share(t):
        az_copy(t, 0).start()
        az_copy(t, 1).start()

    def relay(t):
        for i in (0, 1):
            az_arrive(t, i)
            az_copy(t, i + 2).start()

    def ax_arrive(t):
        head = z * 4 + lax.rem(x + order(3 - t), 4)
        remote(stage.at[0], att.at[head], ax_send.at[0], ax_recv.at[t], at(dx=1)).wait_recv()

    def result_copy(r):
        return remote(
            res_send.at[r], res_recv.at[r], rs_send.at[r], rs_recv.at[r], mate
        )

    def scale_copy(r):
        return remote(
            scale_send.at[r], scale_recv.at[r], ss_send.at[r], ss_recv.at[r], mate
        )

    def tile_of(i):
        inner = jnp.where(lax.rem(i, 2) == 1, 6 - lax.div(i, 2), lax.div(i, 2) - 1)
        return jnp.where(i == 0, 7, jnp.where(i == 7, 3, inner))

    def by_tile(i, state):
        tile = tile_of(i)
        after = tile_of(jnp.minimum(i + 1, 7))
        units = [(4 + j, tile) for j in range(4)] + [(4, after), (5, after)]
        state = turns(units, state)

        @pl.when(tile >= 4)
        def _():
            r = tile - 4
            total = acc[tile, 128:129, :]
            res_send[r] = (acc[tile, 0:128, :] / total).astype(BF)
            scale_send[r, 0:1, :] = mref[tile, 0:1, :]
            scale_send[r, 1:2, :] = total
            result_copy(r).start()
            scale_copy(r).start()

        @pl.when(tile < 4)
        def _():
            t = tile
            r = 3 - t
            remote(
                res_send.at[0], res_recv.at[r], rs_send.at[0], rs_recv.at[r], mate
            ).wait_recv()
            remote(
                scale_send.at[0], scale_recv.at[r], ss_send.at[0], ss_recv.at[r], mate
            ).wait_recv()
            here, there = mref[tile, 0:1, :], scale_recv[r, 0:1, :]
            high = jnp.maximum(here, there)
            here = jnp.exp2(here - high)
            there = jnp.exp2(there - high) * scale_recv[r, 1:2, :]
            inverse = 1.0 / (here * acc[tile, 128:129, :] + there)
            both = acc[tile, 0:128, :] * (here * inverse)
            both = both + res_recv[r].astype(F32) * (there * inverse)
            block = both.T.astype(BF)

            @pl.when(t < 3)
            def _():
                stage[t] = block
                ax_copy(t).start()

            @pl.when(t == 3)
            def _():
                att[mine] = block
                share(3)

        @pl.when(i == 4)
        def _():
            ax_arrive(0)
            share(0)

        @pl.when(i == 6)
        def _():
            ax_arrive(1)
            share(1)
            relay(0)

        return state

    lax.fori_loop(0, 8, by_tile, state)

    def branch(dz):
        zs = lax.rem(z + dz, 4)
        heads = jnp.concatenate([att[zs * 4 + h] for h in range(4)], axis=1)
        return dot(heads, ow[zs])

    def ow_arrive(d):
        src = lax.rem(z + d, 4)
        remote(ow.at[src], ow.at[src], ow_send.at[0], ow_recv.at[d - 1], at(dz=1)).wait_recv()

    ax_arrive(2)
    share(2)
    relay(1)
    ow_own.wait()
    for d in (1, 2, 3):
        ow_arrive(d)
    result = emb[:, my_cols] + branch(0)
    relay(3)
    relay(2)
    result = result + branch(1) + branch(3)
    for t in range(4):
        az_arrive(t, 2)
        az_arrive(t, 3)
    out_ref[...] = (result + branch(2)).astype(BF)

    for i in range(4):
        pool_copy(i).wait_send()
    for d in (1, 2, 3):
        q_copy(d).wait_send()
        kvx_copy(d).wait_send()
        ow_copy(d).wait_send()
        ax_copy(d - 1).wait_send()

    def drain(n, _):
        for k in range(2):
            own_copy(n, k).wait_send()
        pair_copy(n).wait_send()
        mate_copy(n).wait_send()
        result_copy(n).wait_send()
        scale_copy(n).wait_send()
        for i in range(4):
            az_copy(n, i).wait_send()
        return 0

    lax.fori_loop(0, 4, drain, 0)


def on_device(tokens, key_query, value_weight, proj_weight, norm_gain, qkv_weight, out_weight):
    dma = pltpu.SemaphoreType.DMA
    vm = pltpu.VMEM
    scratch = [
        vm((2, NV, CH, 1024), BF),
        vm((128, 1024), BF),
        vm((128, 1024), BF),
        vm((1024, 1024), BF),
        vm((1024, 2048), BF),
        vm((2, 1536, 128), BF),
        vm((1536, 128), F32),
        vm((2048, 1536), BF),
        vm((NV * CH, 128), F32),
        vm((4, CH, 1024), BF),
        vm((3, CH, 1024), BF),
        vm((4, 32, CH), F32),
        vm((3, 32, CH), F32),
        vm((ROWS, 1024), BF),
        vm((ROWS, 2048), F32),
        vm((ROWS, 2048), BF),
        vm((4, ROWS, 128), BF),
        vm((4, 2 * ROWS, 128), BF),
        vm((8, ROWS, 128), BF),
        vm((16, 2 * ROWS, 128), BF),
        vm((1024, 512), F32),
        vm((1024, 512), F32),
        vm((1024, 512), BF),
        vm((1024, 512), BF),
        vm((8, 144, 512), F32),
        vm((8, 8, 512), F32),
        vm((4, 128, 512), BF),
        vm((4, 128, 512), BF),
        vm((4, 8, 512), F32),
        vm((4, 8, 512), F32),
        vm((4, 512, 512), BF),
        vm((3, ROWS, 128), BF),
        vm((16, ROWS, 128), BF),
        dma((2,)), dma((2,)), dma((2,)), dma,
        dma((3,)), dma((3,)), dma((3,)), dma((3,)), dma((4,)), dma((4,)),
        dma((3,)), dma((3,)), dma((3,)), dma((8,)), dma((4,)), dma((16,)),
        dma((4,)), dma((4,)), dma((4,)), dma((4,)), dma((4,)), dma((4,)),
        dma((3,)), dma((3,)), dma((3,)), dma((3,)), dma((16,)), dma((16,)),
    ]
    anywhere = pl.BlockSpec(memory_space=pl.ANY)
    vmem = pl.BlockSpec(memory_space=pltpu.VMEM)
    return pl.pallas_call(
        kernel,
        out_shape=jax.ShapeDtypeStruct((ROWS, 512), BF),
        in_specs=[anywhere, vmem, anywhere, anywhere, vmem, anywhere, anywhere],
        out_specs=vmem,
        scratch_shapes=scratch,
        compiler_params=pltpu.CompilerParams(
            collective_id=1, has_side_effects=True, vmem_limit_bytes=62 * 1024 * 1024
        ),
        name="block",
    )(
        tokens,
        key_query.T,
        value_weight,
        proj_weight,
        norm_gain.reshape(1, 2048),
        qkv_weight.reshape(2048 * 12, 128),
        out_weight.reshape(512, 2048),
    )


def solution(mesh):
    return jax.shard_map(
        on_device,
        mesh=mesh,
        in_specs=(
            P("var", "patch", None),
            P(),
            P(),
            P(),
            P(),
            P(None, None, "var", None),
            P("var", None, None),
        ),
        out_specs=P("patch", "var"),
        check_vma=False,
    )
```

```python
import functools

import jax
import jax.numpy as jnp
from jax import lax
from jax.experimental import pallas as pl
from jax.experimental.pallas import tpu as pltpu
from jax.sharding import PartitionSpec as P

MESH = pl.DeviceIdType.MESH
NT = (((1,), (1,)), ((), ()))
BF = jnp.bfloat16
F32 = jnp.float32

ROWS, NV, CH = 512, 12, 128
Q_SCALE = 128 ** (-0.5) * 1.4426950408889634


def order(e):
    if isinstance(e, int):
        return (0, 1, 3, 2)[e]
    return e + lax.div(e, 2) * (5 - 2 * e)


def dot(a, b):
    return jnp.dot(a, b, preferred_element_type=F32)


def kernel(
    tok_hbm, kq_ref, vw_hbm, proj_hbm, gain_ref, w2_hbm, ow_hbm,
    out_ref,
    tok, kqp, expand, vw, proj, wstage, wf, wq,
    wn, part_send, part_recv, stat_send, stat_recv, pooled,
    emb, normed, q4, kv4, q_buf, kv, s0, s1, p0, p1, acc, mref,
    res_send, res_recv, scale_send, scale_recv,
    ow, stage, att,
    sem_tok, sem_w, sem_w2, sem_ow_own,
    ps_send, ps_recv, st_send, st_recv, pool_send, pool_recv,
    q_send, q_recv, kvx_send, own_send, fwd_send, kv_recv,
    mate_send, mate_recv, rs_send, rs_recv, ss_send, ss_recv,
    ow_send, ow_recv, ax_send, ax_recv, az_send, az_recv,
):
    z = lax.axis_index("var")
    place = lax.axis_index("patch")
    x = lax.div(place, 8)
    y = lax.rem(lax.div(place, 2), 4)
    c = lax.rem(place, 2)

    def at(dx=0, dy=0, dz=0, dc=0):
        px = lax.rem(x + dx, 4)
        py = lax.rem(y + dy, 4)
        pc = lax.rem(c + dc, 2)
        return (lax.rem(z + dz, 4), (px * 4 + py) * 2 + pc)

    def remote(src, dst, send, recv, device):
        return pltpu.make_async_remote_copy(
            src_ref=src, dst_ref=dst, send_sem=send, recv_sem=recv,
            device_id=device, device_id_type=MESH,
        )

    def tok_copy(j, slot):
        base = pl.multiple_of(lax.rem(z + order(3 - j), 4) * CH, CH)
        return pltpu.make_async_copy(
            tok_hbm.at[:, pl.ds(base, CH), :], tok.at[slot], sem_tok.at[slot]
        )

    vw_copy = pltpu.make_async_copy(vw_hbm, vw, sem_w.at[0])
    proj_copy = pltpu.make_async_copy(proj_hbm, proj, sem_w.at[1])
    tok_copy(0, 0).start()
    vw_copy.start()

    def w2_copy(i, slot):
        base = pl.multiple_of(i * 1536, 1536)
        return pltpu.make_async_copy(
            w2_hbm.at[pl.ds(base, 1536), :], wstage.at[slot], sem_w2.at[slot]
        )

    barrier = pltpu.get_barrier_semaphore()
    partners = [at(dx=d) for d in (1, 2, 3)] + [at(dy=d) for d in (1, 2, 3)]
    partners += [at(dz=d) for d in (1, 2, 3)] + [at(dc=1)]
    for device in partners:
        pl.semaphore_signal(barrier, inc=1, device_id=device, device_id_type=MESH)

    kqp[...] = jnp.zeros_like(kqp)
    kqp[0:16, :] = kq_ref[...]
    head_of = lax.broadcasted_iota(jnp.int32, (128, 1024), 0)
    lane = lax.broadcasted_iota(jnp.int32, (128, 1024), 1)
    expand[...] = jnp.where(lax.div(lane, 64) == head_of, 1.0, 0.0).astype(BF)

    vw_copy.wait()

    def part_copy(j):
        dz = order(3 - j)
        return remote(
            part_send.at[j], part_recv.at[3 - dz], ps_send.at[j], ps_recv.at[3 - dz], at(dz=dz)
        )

    def stat_copy(j):
        dz = order(3 - j)
        return remote(
            stat_send.at[j], stat_recv.at[3 - dz], st_send.at[j], st_recv.at[3 - dz], at(dz=dz)
        )

    def pool_chunk(j, _):
        slot = lax.rem(j, 2)
        tok_copy(j, slot).wait()

        @pl.when(j == 0)
        def _():
            tok_copy(1, 1).start()
            proj_copy.start()
            w2_copy(0, 0).start()
            w2_copy(1, 1).start()

        scores = lax.dot_general(
            tok[slot].reshape(NV * CH, 1024), kqp[...], NT, preferred_element_type=F32
        ).reshape(NV, CH, 128)
        peak = jnp.max(scores, axis=0)
        weights = jnp.exp(scores - peak[None])
        totals = jnp.sum(weights, axis=0)
        first_lanes = lax.broadcasted_iota(jnp.int32, (CH, 128), 1) < 16
        stat_send[j] = jnp.where(first_lanes, peak, pltpu.roll(totals, 16, 1)).T[0:32, :]
        wn[...] = weights.astype(BF).astype(F32).reshape(NV * CH, 128)

        upper = jnp.where(lax.broadcasted_iota(jnp.int32, (NV * CH, 128), 1) >= 64, 1, 0)
        values = dot(tok[slot].reshape(NV * CH, 1024), vw[...])
        wide = jnp.concatenate(
            [jnp.take_along_axis(wn[...], 2 * q + upper, axis=1) for q in range(8)], axis=1
        )
        part_send[j] = jnp.sum((values * wide).reshape(NV, CH, 1024), axis=0).astype(BF)

        @pl.when(j < 2)
        def _():
            tok_copy(j + 2, slot).start()

        @pl.when(j == 0)
        def _():
            pl.semaphore_wait(barrier, len(partners))

        @pl.when(j < 3)
        def _():
            part_copy(j).start()
            stat_copy(j).start()

        return 0

    lax.fori_loop(0, 4, pool_chunk, 0)

    for i in range(3):
        part_copy(i).wait_send()
        stat_copy(i).wait_send()
        remote(part_send.at[0], part_recv.at[i], ps_send.at[0], ps_recv.at[i], at(dz=1)).wait_recv()
        remote(stat_send.at[0], stat_recv.at[i], st_send.at[0], st_recv.at[i], at(dz=1)).wait_recv()
    empty = jnp.zeros((96, 128), F32)
    peaks = [stat_send[3]] + [stat_recv[i] for i in range(3)]
    peaks = [jnp.concatenate([p, empty], axis=0).T for p in peaks]
    top = functools.reduce(jnp.maximum, peaks)
    factors = [jnp.exp(l - top) for l in peaks]
    inverse = 1.0 / sum(f * pltpu.roll(l, 112, 1) for f, l in zip(factors, peaks))
    real = lax.broadcasted_iota(jnp.int32, (CH, 128), 1) < 16
    total = jnp.zeros((CH, 1024), F32)
    for g in range(4):
        share = jnp.where(real, factors[g] * inverse, 0.0)
        high = share.astype(BF)
        low = (share - high.astype(F32)).astype(BF)
        wide = dot(high, expand[...]) + dot(low, expand[...])
        part = part_send[3] if g == 0 else part_recv[g - 1]
        total = total + wide * part.astype(F32)
    own_rows = pl.ds(pl.multiple_of(z * CH, CH), CH)
    pooled[own_rows, :] = total.astype(BF)

    def pool_rows(dz, half=None):
        base = lax.rem(z + dz, 4) * CH
        if half is None:
            return pooled.at[pl.ds(pl.multiple_of(base, CH), CH), :]
        return pooled.at[pl.ds(pl.multiple_of(base + half * (CH // 2), CH // 2), CH // 2), :]

    def pool_copy(i):
        rows = (pool_rows(0), pool_rows(0), pool_rows(3, 0), pool_rows(1, 1))[i]
        return remote(rows, rows, pool_send.at[i], pool_recv.at[i], at(dz=(1, 3, 1, 3)[i]))

    def pool_arrive(i):
        rows = (pool_rows(3), pool_rows(1), pool_rows(2, 0), pool_rows(2, 1))[i]
        remote(rows, rows, pool_send.at[0], pool_recv.at[i], at(dz=1)).wait_recv()

    pool_copy(0).start()
    pool_copy(1).start()

    def relayout(i, _):
        slot = lax.rem(i, 2)
        w2_copy(i, slot).wait()
        wf[...] = wstage[slot].astype(F32)
        rows = pl.ds(pl.multiple_of(i * 128, 128), 128)
        for n in range(12):
            to = n if n < 4 else 4 + 2 * (n % 4) + n // 8
            wq[rows, to * 128 : (to + 1) * 128] = wf[pl.ds(n, 128, stride=12), :].astype(BF)

        @pl.when(i < 14)
        def _():
            w2_copy(i + 2, slot).start()

        return 0

    lax.fori_loop(0, 11, relayout, 0)
    for i in (0, 1):
        pool_arrive(i)
        pool_copy(i + 2).start()
    lax.fori_loop(11, 16, relayout, 0)
    proj_copy.wait()
    for i in (2, 3):
        pool_arrive(i)

    def project(i, _):
        cs = pl.ds(pl.multiple_of(i * 1024, 1024), 1024)
        emb[:, cs] = dot(pooled[...], proj[:, cs])
        return 0

    lax.fori_loop(0, 2, project, 0)

    def norm(i, _):
        rows = pl.ds(pl.multiple_of(i * 128, 128), 128)
        block = emb[rows, :]
        center = block - jnp.mean(block, axis=1, keepdims=True)
        variance = jnp.mean(center * center, axis=1, keepdims=True)
        normed[rows, :] = (center / jnp.sqrt(variance + 1e-05) * gain_ref[...]).astype(BF)
        return 0

    lax.fori_loop(0, 4, norm, 0)

    def q_copy(d):
        dst = order((4 - d) % 4)
        head = lax.rem(x + d, 4)
        return remote(
            q4.at[head], q_buf.at[3 - dst], q_send.at[d - 1], q_recv.at[dst - 1], at(dx=d)
        )

    def kvx_copy(d):
        dst = order((4 - d) % 4)
        head = lax.rem(x + d, 4)
        slot = own_slot(dst)
        return remote(kv4.at[head], kv.at[slot], kvx_send.at[d - 1], kv_recv.at[slot], at(dx=d))

    odd = lax.rem(y, 2)
    partner = at(dy=1 + 2 * odd)
    mate = at(dy=3 - 2 * odd)

    def own_slot(r):
        return (0, 4, 6, 8)[r] if isinstance(r, int) else jnp.where(r == 0, 0, 2 + 2 * r)

    def pair_slot(r):
        return (2, 10, 12, 14)[r] if isinstance(r, int) else jnp.where(r == 0, 2, 8 + 2 * r)

    def own_copy(r, k):
        slot = (own_slot(r) + 1, pair_slot(r))[k]
        return remote(
            kv.at[own_slot(r)], kv.at[slot], own_send.at[r * 2 + k], kv_recv.at[slot],
            (at(dc=1), partner)[k],
        )

    def pair_copy(r):
        slot = pair_slot(r)
        return remote(
            kv.at[slot], kv.at[slot + 1], fwd_send.at[r], kv_recv.at[slot + 1], at(dc=1)
        )

    def mate_copy(r):
        return remote(
            q_buf.at[3 - r], q_buf.at[4 + r], mate_send.at[r], mate_recv.at[r], mate
        )

    def keys_values(head, write):
        cs = pl.ds(pl.multiple_of(512 + head * 256, 256), 256)
        both = dot(normed[...], wq[:, cs])
        write(slice(0, 512), both[:, 0:128].astype(BF))
        for j in range(4):
            tile = both[j * 128 : (j + 1) * 128, 128:256]
            write(slice(512 + j * 128, 640 + j * 128), tile.T.astype(BF))

    def write_own(rows, value):
        kv[0, rows, :] = value

    queries = dot(normed[...], wq[:, 0:512]) * Q_SCALE
    for h in range(4):
        q4[h] = queries[:, h * 128 : (h + 1) * 128].astype(BF)
    for d in (2, 1, 3):
        q_copy(d).start()
    q_buf[3] = q4[x]
    mate_copy(0).start()
    keys_values(x, write_own)
    own_copy(0, 0).start()
    own_copy(0, 1).start()
    for d in (1, 3, 2):
        head = lax.rem(x + d, 4)

        def write_other(rows, value, head=head):
            kv4[head, rows, :] = value

        keys_values(head, write_other)
        if d != 2:
            kvx_copy(d).start()

    my_cols = pl.ds(pl.multiple_of(z * 512, 512), 512)
    ow_own = pltpu.make_async_copy(ow_hbm.at[:, my_cols], ow.at[z], sem_ow_own)
    ow_own.start()

    def ow_copy(d):
        cols = pl.ds(pl.multiple_of(lax.rem(z + d, 4) * 512, 512), 512)
        return remote(
            ow_hbm.at[:, cols], ow.at[z], ow_send.at[d - 1], ow_recv.at[3 - d], at(dz=d)
        )

    for d in (1, 3, 2):
        ow_copy(d).start()

    def landed(slot):
        remote(
            kv.at[slot], kv.at[slot], own_send.at[0], kv_recv.at[slot], at(dc=1)
        ).wait_recv()

    def bring(step):
        landed(2 * step)
        if step in (2, 3, 4):
            own_copy(step - 1, 0).start()
            own_copy(step - 1, 1).start()
        else:
            pair_copy(0 if step == 1 else step - 4).start()

    def ready(step):
        landed(2 * step + 1)

    def mate_arrive(r):
        remote(
            q_buf.at[0], q_buf.at[4 + r], mate_send.at[0], mate_recv.at[r], mate
        ).wait_recv()

    acc[...] = jnp.zeros_like(acc)
    mref[...] = jnp.full_like(mref, -1e30)
    ones = jnp.ones((16, 1024), BF)
    def logits(step, t, slot):
        keys = jnp.concatenate([kv[2 * step, 0:512, :], kv[2 * step + 1, 0:512, :]], axis=0)
        s = lax.dot_general(keys, q_buf[t], NT, preferred_element_type=F32)
        (s0, s1)[slot][...] = s
        return jnp.max(s, axis=0, keepdims=True)

    def weigh(t, slot, block_max):
        old = mref[t, 0:1, :]
        new = jnp.maximum(old, block_max)
        mref[t, 0:1, :] = new
        (p0, p1)[slot][...] = jnp.exp2((s0, s1)[slot][...] - new).astype(BF)
        return jnp.exp2(old - new)

    def add(step, t, slot, rescale):
        pieces = [
            kv[2 * step + i, 512 + j * 128 : 640 + j * 128, :] for i in range(2) for j in range(4)
        ]
        vt = jnp.concatenate([jnp.concatenate(pieces, axis=1), ones], axis=0)
        acc[t] = acc[t] * rescale + dot(vt, (p0, p1)[slot][...])

    def turns(units, state):
        block_max, rescale = state
        for u in range(4):
            following = logits(*units[u + 2], u % 2)
            next_rescale = weigh(units[u + 1][1], (u + 1) % 2, block_max)
            add(*units[u], u % 2, rescale)
            block_max, rescale = following, next_rescale
        return block_max, rescale

    def q_arrive(r):
        remote(
            q_buf.at[3], q_buf.at[3 - r], q_send.at[0], q_recv.at[r - 1], at(dx=1)
        ).wait_recv()
        mate_copy(r).start()

    q_arrive(1)
    q_arrive(2)
    landed(1)
    bring(1)
    first = weigh(3, 0, logits(0, 3, 0))
    state = (logits(0, 2, 1), first)
    q_arrive(3)

    def place_of(k):
        step = jnp.where(k < 4, lax.rem(k, 2), lax.div(k, 2))
        return step, jnp.where(k < 4, lax.div(k, 2), lax.rem(k, 2))

    def tile_at(group, u):
        return jnp.where(group == 0, 3 - u, 4 + u)

    def by_step(k, state):
        @pl.when(k == 0)
        def _():
            ready(1)

        @pl.when(k == 1)
        def _():
            bring(2)
            kvx_copy(2).start()
            mate_arrive(0)
            mate_arrive(1)

        @pl.when(k == 2)
        def _():
            bring(3)
            mate_arrive(2)
            mate_arrive(3)

        @pl.when(k == 3)
        def _():
            ready(2)

        @pl.when(k == 4)
        def _():
            bring(4)

        @pl.when(k == 5)
        def _():
            ready(3)
            bring(5)

        @pl.when(k == 6)
        def _():
            ready(4)
            bring(6)

        @pl.when(k == 7)
        def _():
            ready(5)
            bring(7)

        step, group = place_of(k)
        next_step, next_group = place_of(k + 1)
        last = k == 7
        units = [(step, tile_at(group, u)) for u in range(4)]
        units.append((next_step, jnp.where(last, 7, tile_at(next_group, 0))))
        units.append(
            (jnp.where(last, 5, next_step), jnp.where(last, 7, tile_at(next_group, 1)))
        )
        return turns(units, state)

    state = lax.fori_loop(0, 8, by_step, state)
    ready(6)
    ready(7)

    mine = z * 4 + x

    def ax_copy(t):
        dx = order(3 - t)
        back = order((4 - dx) % 4) if isinstance(dx, int) else order(lax.rem(4 - dx, 4))
        return remote(
            stage.at[t], att.at[mine], ax_send.at[t], ax_recv.at[3 - back], at(dx=dx)
        )

    def az_rows(t, dz, half=None):
        head = lax.rem(z + dz, 4) * 4 + lax.rem(x + order(3 - t), 4)
        if half is None:
            return att.at[head]
        return att.at[head, pl.ds(half * 256, 256), :]

    def az_copy(t, i):
        rows = (az_rows(t, 0), az_rows(t, 0), az_rows(t, 3, 0), az_rows(t, 1, 1))[i]
        return remote(
            rows, rows, az_send.at[t * 4 + i], az_recv.at[t * 4 + i], at(dz=(1, 3, 1, 3)[i])
        )

    def az_arrive(t, i):
        rows = (az_rows(t, 3), az_rows(t, 1), az_rows(t, 2, 0), az_rows(t, 2, 1))[i]
        remote(rows, rows, az_send.at[0], az_recv.at[t * 4 + i], at(dz=1)).wait_recv()

    def share(t):
        az_copy(t, 0).start()
        az_copy(t, 1).start()

    def relay(t):
        for i in (0, 1):
            az_arrive(t, i)
            az_copy(t, i + 2).start()

    def ax_arrive(t):
        head = z * 4 + lax.rem(x + order(3 - t), 4)
        remote(stage.at[0], att.at[head], ax_send.at[0], ax_recv.at[t], at(dx=1)).wait_recv()

    def result_copy(r):
        return remote(
            res_send.at[r], res_recv.at[r], rs_send.at[r], rs_recv.at[r], mate
        )

    def scale_copy(r):
        return remote(
            scale_send.at[r], scale_recv.at[r], ss_send.at[r], ss_recv.at[r], mate
        )

    def tile_of(i):
        inner = jnp.where(lax.rem(i, 2) == 1, 6 - lax.div(i, 2), lax.div(i, 2) - 1)
        return jnp.where(i == 0, 7, jnp.where(i == 7, 3, inner))

    def by_tile(i, state):
        tile = tile_of(i)
        after = tile_of(jnp.minimum(i + 1, 7))
        units = [(4 + j, tile) for j in range(4)] + [(4, after), (5, after)]
        state = turns(units, state)

        @pl.when(tile >= 4)
        def _():
            r = tile - 4
            total = acc[tile, 128:129, :]
            res_send[r] = (acc[tile, 0:128, :] / total).astype(BF)
            scale_send[r, 0:1, :] = mref[tile, 0:1, :]
            scale_send[r, 1:2, :] = total
            result_copy(r).start()
            scale_copy(r).start()

        @pl.when(tile < 4)
        def _():
            t = tile
            r = 3 - t
            remote(
                res_send.at[0], res_recv.at[r], rs_send.at[0], rs_recv.at[r], mate
            ).wait_recv()
            remote(
                scale_send.at[0], scale_recv.at[r], ss_send.at[0], ss_recv.at[r], mate
            ).wait_recv()
            here, there = mref[tile, 0:1, :], scale_recv[r, 0:1, :]
            high = jnp.maximum(here, there)
            here = jnp.exp2(here - high)
            there = jnp.exp2(there - high) * scale_recv[r, 1:2, :]
            inverse = 1.0 / (here * acc[tile, 128:129, :] + there)
            both = acc[tile, 0:128, :] * (here * inverse)
            both = both + res_recv[r].astype(F32) * (there * inverse)
            block = both.T.astype(BF)

            @pl.when(t < 3)
            def _():
                stage[t] = block
                ax_copy(t).start()

            @pl.when(t == 3)
            def _():
                att[mine] = block
                share(3)

        @pl.when(i == 4)
        def _():
            ax_arrive(0)
            share(0)

        @pl.when(i == 6)
        def _():
            ax_arrive(1)
            share(1)
            relay(0)

        return state

    lax.fori_loop(0, 8, by_tile, state)

    def branch(dz):
        zs = lax.rem(z + dz, 4)
        heads = jnp.concatenate([att[zs * 4 + h] for h in range(4)], axis=1)
        return dot(heads, ow[zs])

    def ow_arrive(d):
        src = lax.rem(z + d, 4)
        remote(ow.at[src], ow.at[src], ow_send.at[0], ow_recv.at[d - 1], at(dz=1)).wait_recv()

    ax_arrive(2)
    share(2)
    relay(1)
    ow_own.wait()
    for d in (1, 2, 3):
        ow_arrive(d)
    result = emb[:, my_cols] + branch(0)
    relay(3)
    relay(2)
    result = result + branch(1) + branch(3)
    for t in range(4):
        az_arrive(t, 2)
        az_arrive(t, 3)
    out_ref[...] = (result + branch(2)).astype(BF)

    for i in range(4):
        pool_copy(i).wait_send()
    for d in (1, 2, 3):
        q_copy(d).wait_send()
        kvx_copy(d).wait_send()
        ow_copy(d).wait_send()
        ax_copy(d - 1).wait_send()

    def drain(n, _):
        for k in range(2):
            own_copy(n, k).wait_send()
        pair_copy(n).wait_send()
        mate_copy(n).wait_send()
        result_copy(n).wait_send()
        scale_copy(n).wait_send()
        for i in range(4):
            az_copy(n, i).wait_send()
        return 0

    lax.fori_loop(0, 4, drain, 0)


def on_device(tokens, key_query, value_weight, proj_weight, norm_gain, qkv_weight, out_weight):
    dma = pltpu.SemaphoreType.DMA
    vm = pltpu.VMEM
    scratch = [
        vm((2, NV, CH, 1024), BF),
        vm((128, 1024), BF),
        vm((128, 1024), BF),
        vm((1024, 1024), BF),
        vm((1024, 2048), BF),
        vm((2, 1536, 128), BF),
        vm((1536, 128), F32),
        vm((2048, 1536), BF),
        vm((NV * CH, 128), F32),
        vm((4, CH, 1024), BF),
        vm((3, CH, 1024), BF),
        vm((4, 32, CH), F32),
        vm((3, 32, CH), F32),
        vm((ROWS, 1024), BF),
        vm((ROWS, 2048), F32),
        vm((ROWS, 2048), BF),
        vm((4, ROWS, 128), BF),
        vm((4, 2 * ROWS, 128), BF),
        vm((8, ROWS, 128), BF),
        vm((16, 2 * ROWS, 128), BF),
        vm((1024, 512), F32),
        vm((1024, 512), F32),
        vm((1024, 512), BF),
        vm((1024, 512), BF),
        vm((8, 144, 512), F32),
        vm((8, 8, 512), F32),
        vm((4, 128, 512), BF),
        vm((4, 128, 512), BF),
        vm((4, 8, 512), F32),
        vm((4, 8, 512), F32),
        vm((4, 512, 512), BF),
        vm((3, ROWS, 128), BF),
        vm((16, ROWS, 128), BF),
        dma((2,)), dma((2,)), dma((2,)), dma,
        dma((3,)), dma((3,)), dma((3,)), dma((3,)), dma((4,)), dma((4,)),
        dma((3,)), dma((3,)), dma((3,)), dma((8,)), dma((4,)), dma((16,)),
        dma((4,)), dma((4,)), dma((4,)), dma((4,)), dma((4,)), dma((4,)),
        dma((3,)), dma((3,)), dma((3,)), dma((3,)), dma((16,)), dma((16,)),
    ]
    anywhere = pl.BlockSpec(memory_space=pl.ANY)
    vmem = pl.BlockSpec(memory_space=pltpu.VMEM)
    return pl.pallas_call(
        kernel,
        out_shape=jax.ShapeDtypeStruct((ROWS, 512), BF),
        in_specs=[anywhere, vmem, anywhere, anywhere, vmem, anywhere, anywhere],
        out_specs=vmem,
        scratch_shapes=scratch,
        compiler_params=pltpu.CompilerParams(
            collective_id=1, has_side_effects=True, vmem_limit_bytes=62 * 1024 * 1024
        ),
        name="block",
    )(
        tokens,
        key_query.T,
        value_weight,
        proj_weight,
        norm_gain.reshape(1, 2048),
        qkv_weight.reshape(2048 * 12, 128),
        out_weight.reshape(512, 2048),
    )


def solution(mesh):
    return jax.shard_map(
        on_device,
        mesh=mesh,
        in_specs=(
            P("var", "patch", None),
            P(),
            P(),
            P(),
            P(),
            P(None, None, "var", None),
            P("var", None, None),
        ),
        out_specs=P("patch", "var"),
        check_vma=False,
    )
```

```python
import functools

import jax
import jax.numpy as jnp
from jax import lax
from jax.experimental import pallas as pl
from jax.experimental.pallas import tpu as pltpu
from jax.sharding import PartitionSpec as P

MESH = pl.DeviceIdType.MESH
NT = (((1,), (1,)), ((), ()))
BF = jnp.bfloat16
F32 = jnp.float32

ROWS, NV, CH = 512, 12, 128
Q_SCALE = 128 ** (-0.5) * 1.4426950408889634


def order(e):
    if isinstance(e, int):
        return (0, 1, 3, 2)[e]
    return e + lax.div(e, 2) * (5 - 2 * e)


def dot(a, b):
    return jnp.dot(a, b, preferred_element_type=F32)


def kernel(
    tok_hbm, kq_ref, vw_hbm, proj_hbm, gain_ref, w2_hbm, ow_hbm,
    out_ref,
    tok, kqp, expand, vw, proj, wstage, wf, wq,
    wn, part_send, part_recv, stat_send, stat_recv, pooled,
    emb, normed, q4, kv4, q_buf, kv, s0, s1, p0, p1, acc, mref,
    res_send, res_recv, scale_send, scale_recv,
    ow, stage, att,
    sem_tok, sem_w, sem_w2, sem_ow_own,
    ps_send, ps_recv, st_send, st_recv, pool_send, pool_recv,
    q_send, q_recv, kvx_send, own_send, fwd_send, kv_recv,
    mate_send, mate_recv, rs_send, rs_recv, ss_send, ss_recv,
    ow_send, ow_recv, ax_send, ax_recv, az_send, az_recv,
):
    z = lax.axis_index("var")
    place = lax.axis_index("patch")
    x = lax.div(place, 8)
    y = lax.rem(lax.div(place, 2), 4)
    c = lax.rem(place, 2)

    def at(dx=0, dy=0, dz=0, dc=0):
        px = lax.rem(x + dx, 4)
        py = lax.rem(y + dy, 4)
        pc = lax.rem(c + dc, 2)
        return (lax.rem(z + dz, 4), (px * 4 + py) * 2 + pc)

    def remote(src, dst, send, recv, device):
        return pltpu.make_async_remote_copy(
            src_ref=src, dst_ref=dst, send_sem=send, recv_sem=recv,
            device_id=device, device_id_type=MESH,
        )

    def tok_copy(j, slot):
        base = pl.multiple_of(lax.rem(z + order(3 - j), 4) * CH, CH)
        return pltpu.make_async_copy(
            tok_hbm.at[:, pl.ds(base, CH), :], tok.at[slot], sem_tok.at[slot]
        )

    vw_copy = pltpu.make_async_copy(vw_hbm, vw, sem_w.at[0])
    proj_copy = pltpu.make_async_copy(proj_hbm, proj, sem_w.at[1])
    tok_copy(0, 0).start()
    vw_copy.start()

    def w2_copy(i, slot):
        base = pl.multiple_of(i * 1536, 1536)
        return pltpu.make_async_copy(
            w2_hbm.at[pl.ds(base, 1536), :], wstage.at[slot], sem_w2.at[slot]
        )

    barrier = pltpu.get_barrier_semaphore()
    partners = [at(dx=d) for d in (1, 2, 3)] + [at(dy=d) for d in (1, 2, 3)]
    partners += [at(dz=d) for d in (1, 2, 3)] + [at(dc=1)]
    for device in partners:
        pl.semaphore_signal(barrier, inc=1, device_id=device, device_id_type=MESH)

    kqp[...] = jnp.zeros_like(kqp)
    kqp[0:16, :] = kq_ref[...]
    head_of = lax.broadcasted_iota(jnp.int32, (128, 1024), 0)
    lane = lax.broadcasted_iota(jnp.int32, (128, 1024), 1)
    expand[...] = jnp.where(lax.div(lane, 64) == head_of, 1.0, 0.0).astype(BF)

    vw_copy.wait()

    def part_copy(j):
        dz = order(3 - j)
        return remote(
            part_send.at[j], part_recv.at[3 - dz], ps_send.at[j], ps_recv.at[3 - dz], at(dz=dz)
        )

    def stat_copy(j):
        dz = order(3 - j)
        return remote(
            stat_send.at[j], stat_recv.at[3 - dz], st_send.at[j], st_recv.at[3 - dz], at(dz=dz)
        )

    def pool_chunk(j, _):
        slot = lax.rem(j, 2)
        tok_copy(j, slot).wait()

        @pl.when(j == 0)
        def _():
            tok_copy(1, 1).start()
            proj_copy.start()
            w2_copy(0, 0).start()
            w2_copy(1, 1).start()

        scores = lax.dot_general(
            tok[slot].reshape(NV * CH, 1024), kqp[...], NT, preferred_element_type=F32
        ).reshape(NV, CH, 128)
        peak = jnp.max(scores, axis=0)
        weights = jnp.exp(scores - peak[None])
        totals = jnp.sum(weights, axis=0)
        first_lanes = lax.broadcasted_iota(jnp.int32, (CH, 128), 1) < 16
        stat_send[j] = jnp.where(first_lanes, peak, pltpu.roll(totals, 16, 1)).T[0:32, :]
        wn[...] = weights.astype(BF).astype(F32).reshape(NV * CH, 128)

        upper = jnp.where(lax.broadcasted_iota(jnp.int32, (NV * CH, 128), 1) >= 64, 1, 0)
        values = dot(tok[slot].reshape(NV * CH, 1024), vw[...])
        wide = jnp.concatenate(
            [jnp.take_along_axis(wn[...], 2 * q + upper, axis=1) for q in range(8)], axis=1
        )
        part_send[j] = jnp.sum((values * wide).reshape(NV, CH, 1024), axis=0).astype(BF)

        @pl.when(j < 2)
        def _():
            tok_copy(j + 2, slot).start()

        @pl.when(j == 0)
        def _():
            pl.semaphore_wait(barrier, len(partners))

        @pl.when(j < 3)
        def _():
            part_copy(j).start()
            stat_copy(j).start()

        return 0

    lax.fori_loop(0, 4, pool_chunk, 0)

    for i in range(3):
        part_copy(i).wait_send()
        stat_copy(i).wait_send()
        remote(part_send.at[0], part_recv.at[i], ps_send.at[0], ps_recv.at[i], at(dz=1)).wait_recv()
        remote(stat_send.at[0], stat_recv.at[i], st_send.at[0], st_recv.at[i], at(dz=1)).wait_recv()
    empty = jnp.zeros((96, 128), F32)
    peaks = [stat_send[3]] + [stat_recv[i] for i in range(3)]
    peaks = [jnp.concatenate([p, empty], axis=0).T for p in peaks]
    top = functools.reduce(jnp.maximum, peaks)
    factors = [jnp.exp(l - top) for l in peaks]
    inverse = 1.0 / sum(f * pltpu.roll(l, 112, 1) for f, l in zip(factors, peaks))
    real = lax.broadcasted_iota(jnp.int32, (CH, 128), 1) < 16
    total = jnp.zeros((CH, 1024), F32)
    for g in range(4):
        share = jnp.where(real, factors[g] * inverse, 0.0)
        high = share.astype(BF)
        low = (share - high.astype(F32)).astype(BF)
        wide = dot(high, expand[...]) + dot(low, expand[...])
        part = part_send[3] if g == 0 else part_recv[g - 1]
        total = total + wide * part.astype(F32)
    own_rows = pl.ds(pl.multiple_of(z * CH, CH), CH)
    pooled[own_rows, :] = total.astype(BF)

    def pool_rows(dz, half=None):
        base = lax.rem(z + dz, 4) * CH
        if half is None:
            return pooled.at[pl.ds(pl.multiple_of(base, CH), CH), :]
        return pooled.at[pl.ds(pl.multiple_of(base + half * (CH // 2), CH // 2), CH // 2), :]

    def pool_copy(i):
        rows = (pool_rows(0), pool_rows(0), pool_rows(3, 0), pool_rows(1, 1))[i]
        return remote(rows, rows, pool_send.at[i], pool_recv.at[i], at(dz=(1, 3, 1, 3)[i]))

    def pool_arrive(i):
        rows = (pool_rows(3), pool_rows(1), pool_rows(2, 0), pool_rows(2, 1))[i]
        remote(rows, rows, pool_send.at[0], pool_recv.at[i], at(dz=1)).wait_recv()

    pool_copy(0).start()
    pool_copy(1).start()

    def relayout(i, _):
        slot = lax.rem(i, 2)
        w2_copy(i, slot).wait()
        wf[...] = wstage[slot].astype(F32)
        rows = pl.ds(pl.multiple_of(i * 128, 128), 128)
        for n in range(12):
            to = n if n < 4 else 4 + 2 * (n % 4) + n // 8
            wq[rows, to * 128 : (to + 1) * 128] = wf[pl.ds(n, 128, stride=12), :].astype(BF)

        @pl.when(i < 14)
        def _():
            w2_copy(i + 2, slot).start()

        return 0

    lax.fori_loop(0, 11, relayout, 0)
    for i in (0, 1):
        pool_arrive(i)
        pool_copy(i + 2).start()
    lax.fori_loop(11, 16, relayout, 0)
    proj_copy.wait()
    for i in (2, 3):
        pool_arrive(i)

    def project(i, _):
        cs = pl.ds(pl.multiple_of(i * 1024, 1024), 1024)
        emb[:, cs] = dot(pooled[...], proj[:, cs])
        return 0

    lax.fori_loop(0, 2, project, 0)

    def norm(i, _):
        rows = pl.ds(pl.multiple_of(i * 128, 128), 128)
        block = emb[rows, :]
        center = block - jnp.mean(block, axis=1, keepdims=True)
        variance = jnp.mean(center * center, axis=1, keepdims=True)
        scale = 1.0 / jnp.sqrt(variance + 1e-05)
        normed[rows, :] = (center * scale * gain_ref[...]).astype(BF)
        return 0

    lax.fori_loop(0, 4, norm, 0)

    def q_copy(d):
        dst = order((4 - d) % 4)
        head = lax.rem(x + d, 4)
        return remote(
            q4.at[head], q_buf.at[3 - dst], q_send.at[d - 1], q_recv.at[dst - 1], at(dx=d)
        )

    def kvx_copy(d):
        dst = order((4 - d) % 4)
        head = lax.rem(x + d, 4)
        slot = own_slot(dst)
        return remote(kv4.at[head], kv.at[slot], kvx_send.at[d - 1], kv_recv.at[slot], at(dx=d))

    odd = lax.rem(y, 2)
    partner = at(dy=1 + 2 * odd)
    mate = at(dy=3 - 2 * odd)

    def own_slot(r):
        return (0, 4, 6, 8)[r] if isinstance(r, int) else jnp.where(r == 0, 0, 2 + 2 * r)

    def pair_slot(r):
        return (2, 10, 12, 14)[r] if isinstance(r, int) else jnp.where(r == 0, 2, 8 + 2 * r)

    def own_copy(r, k):
        slot = (own_slot(r) + 1, pair_slot(r))[k]
        return remote(
            kv.at[own_slot(r)], kv.at[slot], own_send.at[r * 2 + k], kv_recv.at[slot],
            (at(dc=1), partner)[k],
        )

    def pair_copy(r):
        slot = pair_slot(r)
        return remote(
            kv.at[slot], kv.at[slot + 1], fwd_send.at[r], kv_recv.at[slot + 1], at(dc=1)
        )

    def mate_copy(r):
        return remote(
            q_buf.at[3 - r], q_buf.at[4 + r], mate_send.at[r], mate_recv.at[r], mate
        )

    def keys_values(head, write):
        cs = pl.ds(pl.multiple_of(512 + head * 256, 256), 256)
        both = dot(normed[...], wq[:, cs])
        write(slice(0, 512), both[:, 0:128].astype(BF))
        for j in range(4):
            tile = both[j * 128 : (j + 1) * 128, 128:256]
            write(slice(512 + j * 128, 640 + j * 128), tile.T.astype(BF))

    def write_own(rows, value):
        kv[0, rows, :] = value

    queries = dot(normed[...], wq[:, 0:512]) * Q_SCALE
    for h in range(4):
        q4[h] = queries[:, h * 128 : (h + 1) * 128].astype(BF)
    for d in (2, 1, 3):
        q_copy(d).start()
    q_buf[3] = q4[x]
    mate_copy(0).start()
    keys_values(x, write_own)
    own_copy(0, 0).start()
    own_copy(0, 1).start()
    for d in (1, 3, 2):
        head = lax.rem(x + d, 4)

        def write_other(rows, value, head=head):
            kv4[head, rows, :] = value

        keys_values(head, write_other)
        if d != 2:
            kvx_copy(d).start()

    my_cols = pl.ds(pl.multiple_of(z * 512, 512), 512)
    ow_own = pltpu.make_async_copy(ow_hbm.at[:, my_cols], ow.at[z], sem_ow_own)
    ow_own.start()

    def ow_copy(d):
        cols = pl.ds(pl.multiple_of(lax.rem(z + d, 4) * 512, 512), 512)
        return remote(
            ow_hbm.at[:, cols], ow.at[z], ow_send.at[d - 1], ow_recv.at[3 - d], at(dz=d)
        )

    for d in (1, 3, 2):
        ow_copy(d).start()

    def landed(slot):
        remote(
            kv.at[slot], kv.at[slot], own_send.at[0], kv_recv.at[slot], at(dc=1)
        ).wait_recv()

    def bring(step):
        landed(2 * step)
        if step in (2, 3, 4):
            own_copy(step - 1, 0).start()
            own_copy(step - 1, 1).start()
        else:
            pair_copy(0 if step == 1 else step - 4).start()

    def ready(step):
        landed(2 * step + 1)

    def mate_arrive(r):
        remote(
            q_buf.at[0], q_buf.at[4 + r], mate_send.at[0], mate_recv.at[r], mate
        ).wait_recv()

    acc[...] = jnp.zeros_like(acc)
    mref[...] = jnp.full_like(mref, -1e30)
    ones = jnp.ones((16, 1024), BF)
    def logits(step, t, slot):
        keys = jnp.concatenate([kv[2 * step, 0:512, :], kv[2 * step + 1, 0:512, :]], axis=0)
        s = lax.dot_general(keys, q_buf[t], NT, preferred_element_type=F32)
        (s0, s1)[slot][...] = s
        return jnp.max(s, axis=0, keepdims=True)

    def weigh(t, slot, block_max):
        old = mref[t, 0:1, :]
        new = jnp.maximum(old, block_max)
        mref[t, 0:1, :] = new
        (p0, p1)[slot][...] = jnp.exp2((s0, s1)[slot][...] - new).astype(BF)
        return jnp.exp2(old - new)

    def add(step, t, slot, rescale):
        pieces = [
            kv[2 * step + i, 512 + j * 128 : 640 + j * 128, :] for i in range(2) for j in range(4)
        ]
        vt = jnp.concatenate([jnp.concatenate(pieces, axis=1), ones], axis=0)
        acc[t] = acc[t] * rescale + dot(vt, (p0, p1)[slot][...])

    def turns(units, state):
        block_max, rescale = state
        for u in range(4):
            following, next_rescale = block_max, rescale
            if u + 2 < len(units):
                following = logits(*units[u + 2], u % 2)
            if u + 1 < len(units):
                next_rescale = weigh(units[u + 1][1], (u + 1) % 2, block_max)
            add(*units[u], u % 2, rescale)
            block_max, rescale = following, next_rescale
        return block_max, rescale

    def q_arrive(r):
        remote(
            q_buf.at[3], q_buf.at[3 - r], q_send.at[0], q_recv.at[r - 1], at(dx=1)
        ).wait_recv()
        mate_copy(r).start()

    q_arrive(1)
    q_arrive(2)
    landed(1)
    bring(1)
    first = weigh(3, 0, logits(0, 3, 0))
    state = (logits(0, 2, 1), first)
    q_arrive(3)

    def place_of(k):
        step = jnp.where(k < 4, lax.rem(k, 2), lax.div(k, 2))
        return step, jnp.where(k < 4, lax.div(k, 2), lax.rem(k, 2))

    def tile_at(group, u):
        return jnp.where(group == 0, 3 - u, 4 + u)

    def by_step(k, state):
        @pl.when(k == 0)
        def _():
            ready(1)

        @pl.when(k == 1)
        def _():
            bring(2)
            kvx_copy(2).start()
            mate_arrive(0)
            mate_arrive(1)

        @pl.when(k == 2)
        def _():
            bring(3)
            mate_arrive(2)
            mate_arrive(3)

        @pl.when(k == 3)
        def _():
            ready(2)

        @pl.when(k == 4)
        def _():
            bring(4)

        @pl.when(k == 5)
        def _():
            ready(3)
            bring(5)

        @pl.when(k == 6)
        def _():
            ready(4)
            bring(6)

        @pl.when(k == 7)
        def _():
            ready(5)
            bring(7)

        step, group = place_of(k)
        next_step, next_group = place_of(k + 1)
        last = k == 7
        units = [(step, tile_at(group, u)) for u in range(4)]
        units.append((next_step, jnp.where(last, 7, tile_at(next_group, 0))))
        units.append(
            (jnp.where(last, 5, next_step), jnp.where(last, 7, tile_at(next_group, 1)))
        )
        return turns(units, state)

    state = lax.fori_loop(0, 8, by_step, state)
    ready(6)
    ready(7)

    mine = z * 4 + x

    def ax_copy(t):
        dx = order(3 - t)
        back = order((4 - dx) % 4) if isinstance(dx, int) else order(lax.rem(4 - dx, 4))
        return remote(
            stage.at[t], att.at[mine], ax_send.at[t], ax_recv.at[3 - back], at(dx=dx)
        )

    def az_rows(t, dz, half=None):
        head = lax.rem(z + dz, 4) * 4 + lax.rem(x + order(3 - t), 4)
        if half is None:
            return att.at[head]
        return att.at[head, pl.ds(half * 256, 256), :]

    def az_copy(t, i):
        rows = (az_rows(t, 0), az_rows(t, 0), az_rows(t, 3, 0), az_rows(t, 1, 1))[i]
        return remote(
            rows, rows, az_send.at[t * 4 + i], az_recv.at[t * 4 + i], at(dz=(1, 3, 1, 3)[i])
        )

    def az_arrive(t, i):
        rows = (az_rows(t, 3), az_rows(t, 1), az_rows(t, 2, 0), az_rows(t, 2, 1))[i]
        remote(rows, rows, az_send.at[0], az_recv.at[t * 4 + i], at(dz=1)).wait_recv()

    def share(t):
        az_copy(t, 0).start()
        az_copy(t, 1).start()

    def relay(t):
        for i in (0, 1):
            az_arrive(t, i)
            az_copy(t, i + 2).start()

    def ax_arrive(t):
        head = z * 4 + lax.rem(x + order(3 - t), 4)
        remote(stage.at[0], att.at[head], ax_send.at[0], ax_recv.at[t], at(dx=1)).wait_recv()

    def result_copy(r):
        return remote(
            res_send.at[r], res_recv.at[r], rs_send.at[r], rs_recv.at[r], mate
        )

    def scale_copy(r):
        return remote(
            scale_send.at[r], scale_recv.at[r], ss_send.at[r], ss_recv.at[r], mate
        )

    def tile_of(i):
        inner = jnp.where(lax.rem(i, 2) == 1, 6 - lax.div(i, 2), lax.div(i, 2) - 1)
        return jnp.where(i == 0, 7, jnp.where(i == 7, 3, inner))

    def finish(t):
        r = 3 - t
        remote(
            res_send.at[0], res_recv.at[r], rs_send.at[0], rs_recv.at[r], mate
        ).wait_recv()
        remote(
            scale_send.at[0], scale_recv.at[r], ss_send.at[0], ss_recv.at[r], mate
        ).wait_recv()
        here, there = mref[t, 0:1, :], scale_recv[r, 0:1, :]
        high = jnp.maximum(here, there)
        here = jnp.exp2(here - high)
        there = jnp.exp2(there - high) * scale_recv[r, 1:2, :]
        inverse = 1.0 / (here * acc[t, 128:129, :] + there)
        both = acc[t, 0:128, :] * (here * inverse)
        both = both + res_recv[r].astype(F32) * (there * inverse)
        block = both.T.astype(BF)
        return block

    def by_tile(i, state):
        tile = tile_of(i)
        after = tile_of(i + 1)
        state = turns([(4 + j, tile) for j in range(4)] + [(4, after), (5, after)], state)

        @pl.when(tile >= 4)
        def _():
            r = tile - 4
            total = acc[tile, 128:129, :]
            res_send[r] = (acc[tile, 0:128, :] / total).astype(BF)
            scale_send[r, 0:1, :] = mref[tile, 0:1, :]
            scale_send[r, 1:2, :] = total
            result_copy(r).start()
            scale_copy(r).start()

        @pl.when(tile < 4)
        def _():
            stage[tile] = finish(tile)
            ax_copy(tile).start()

        @pl.when(i == 4)
        def _():
            ax_arrive(0)
            share(0)

        @pl.when(i == 6)
        def _():
            ax_arrive(1)
            share(1)
            relay(0)

        return state

    state = lax.fori_loop(0, 7, by_tile, state)
    turns([(4 + j, 3) for j in range(4)], state)
    att[mine] = finish(3)
    share(3)

    def branch(dz):
        zs = lax.rem(z + dz, 4)
        heads = jnp.concatenate([att[zs * 4 + h] for h in range(4)], axis=1)
        return dot(heads, ow[zs])

    def ow_arrive(d):
        src = lax.rem(z + d, 4)
        remote(ow.at[src], ow.at[src], ow_send.at[0], ow_recv.at[d - 1], at(dz=1)).wait_recv()

    ax_arrive(2)
    share(2)
    relay(1)
    ow_own.wait()
    for d in (1, 2, 3):
        ow_arrive(d)
    result = emb[:, my_cols] + branch(0)
    relay(3)
    relay(2)
    result = result + branch(1) + branch(3)
    for t in range(4):
        az_arrive(t, 2)
        az_arrive(t, 3)
    out_ref[...] = (result + branch(2)).astype(BF)

    for i in range(4):
        pool_copy(i).wait_send()
    for d in (1, 2, 3):
        q_copy(d).wait_send()
        kvx_copy(d).wait_send()
        ow_copy(d).wait_send()
        ax_copy(d - 1).wait_send()

    def drain(n, _):
        for k in range(2):
            own_copy(n, k).wait_send()
        pair_copy(n).wait_send()
        mate_copy(n).wait_send()
        result_copy(n).wait_send()
        scale_copy(n).wait_send()
        for i in range(4):
            az_copy(n, i).wait_send()
        return 0

    lax.fori_loop(0, 4, drain, 0)


def on_device(tokens, key_query, value_weight, proj_weight, norm_gain, qkv_weight, out_weight):
    dma = pltpu.SemaphoreType.DMA
    vm = pltpu.VMEM
    scratch = [
        vm((2, NV, CH, 1024), BF),
        vm((128, 1024), BF),
        vm((128, 1024), BF),
        vm((1024, 1024), BF),
        vm((1024, 2048), BF),
        vm((2, 1536, 128), BF),
        vm((1536, 128), F32),
        vm((2048, 1536), BF),
        vm((NV * CH, 128), F32),
        vm((4, CH, 1024), BF),
        vm((3, CH, 1024), BF),
        vm((4, 32, CH), F32),
        vm((3, 32, CH), F32),
        vm((ROWS, 1024), BF),
        vm((ROWS, 2048), F32),
        vm((ROWS, 2048), BF),
        vm((4, ROWS, 128), BF),
        vm((4, 2 * ROWS, 128), BF),
        vm((8, ROWS, 128), BF),
        vm((16, 2 * ROWS, 128), BF),
        vm((1024, 512), F32),
        vm((1024, 512), F32),
        vm((1024, 512), BF),
        vm((1024, 512), BF),
        vm((8, 144, 512), F32),
        vm((8, 8, 512), F32),
        vm((4, 128, 512), BF),
        vm((4, 128, 512), BF),
        vm((4, 8, 512), F32),
        vm((4, 8, 512), F32),
        vm((4, 512, 512), BF),
        vm((3, ROWS, 128), BF),
        vm((16, ROWS, 128), BF),
        dma((2,)), dma((2,)), dma((2,)), dma,
        dma((3,)), dma((3,)), dma((3,)), dma((3,)), dma((4,)), dma((4,)),
        dma((3,)), dma((3,)), dma((3,)), dma((8,)), dma((4,)), dma((16,)),
        dma((4,)), dma((4,)), dma((4,)), dma((4,)), dma((4,)), dma((4,)),
        dma((3,)), dma((3,)), dma((3,)), dma((3,)), dma((16,)), dma((16,)),
    ]
    anywhere = pl.BlockSpec(memory_space=pl.ANY)
    vmem = pl.BlockSpec(memory_space=pltpu.VMEM)
    return pl.pallas_call(
        kernel,
        out_shape=jax.ShapeDtypeStruct((ROWS, 512), BF),
        in_specs=[anywhere, vmem, anywhere, anywhere, vmem, anywhere, anywhere],
        out_specs=vmem,
        scratch_shapes=scratch,
        compiler_params=pltpu.CompilerParams(
            collective_id=1, has_side_effects=True, vmem_limit_bytes=62 * 1024 * 1024
        ),
        name="block",
    )(
        tokens,
        key_query.T,
        value_weight,
        proj_weight,
        norm_gain.reshape(1, 2048),
        qkv_weight.reshape(2048 * 12, 128),
        out_weight.reshape(512, 2048),
    )


def solution(mesh):
    return jax.shard_map(
        on_device,
        mesh=mesh,
        in_specs=(
            P("var", "patch", None),
            P(),
            P(),
            P(),
            P(),
            P(None, None, "var", None),
            P("var", None, None),
        ),
        out_specs=P("patch", "var"),
        check_vma=False,
    )
```
